128 devices in a mesh: dp: 128 (over z, y, x, core).
Axes of the slice: x: 4, y: 4, z: 4, core: 2. Of those that a mesh axis runs over, the one named last changes fastest.
Arguments:
- encoder_states: bfloat16 [4096, 128, 256], P(None, 'dp'), may hold values from -6 to 6
- position_permutation: int32 [4096, 128], replicated, may hold values from 0 to 127, as said below
- observed_tokens: int32 [4096], replicated, may hold values from 16 to 112, as said below
- decoder_slot: int32 [4096], replicated, may hold values from 0 to 4095, each once
- hidden_token_vector: bfloat16 [256], replicated, may hold values from -5 to 5
- temporal_embedding: bfloat16 [64, 256], replicated, may hold values from -3 to 3
- entry_scale_factor: bfloat16 [256], replicated, may hold values from 0.099609375 to 1.8984375
- entry_offset_vector: bfloat16 [256], replicated, may hold values from -2 to 2
- query_key_value_matrices: bfloat16 [256, 768], replicated, may hold values from -0.375 to 0.375
- query_value_biases: bfloat16 [2, 256], replicated, may hold values from -3 to 3
- attention_outmatrix: bfloat16 [256, 256], replicated, may hold values from -3 to 3
- attention_outbias: bfloat16 [256], replicated, may hold values from -2 to 2
- center_scale_factor: bfloat16 [256], replicated, may hold values from 0.099609375 to 1.8984375
- center_offset_vector: bfloat16 [256], replicated, may hold values from -2 to 2
- widening_matrix: bfloat16 [256, 1024], replicated, may hold values from -0.375 to 0.375
- widening_bias: bfloat16 [1024], replicated, may hold values from -3 to 3
- narrowing_matrix: bfloat16 [1024, 256], replicated, may hold values from -0.1875 to 0.1875
- narrowing_bias: bfloat16 [256], replicated, may hold values from -2 to 2
- output_sensitivity: bfloat16 [4096, 128, 256], P('dp'), may hold values from -6 to 6
Outputs:
- decoded: bfloat16 [4096, 128, 256], P('dp')
- grad_encoded: bfloat16 [4096, 128, 256], P(None, 'dp')
- grad_placeholder: float32 [256], replicated
- grad_timesteps: float32 [64, 256], replicated
- entry_scale_derivative: float32 [256], replicated
- entry_offset_derivative: float32 [256], replicated
- grad_projection: float32 [256, 768], replicated
- grad_offsets: float32 [2, 256], replicated
- grad_mixing: float32 [256, 256], replicated
- grad_recenter: float32 [256], replicated
- grad_midnorm: float32 [256], replicated
- grad_midshift: float32 [256], replicated
- grad_expansion: float32 [256, 1024], replicated
- grad_lifting: float32 [1024], replicated
- grad_reduction: float32 [1024, 256], replicated
- grad_trailing: float32 [256], replicated
The draws below stay inside these ranges and needn't reach their ends.
Inputs may be any that keep to these rules, and one draw needn't show every extreme that they name: `position_permutation`: each row holds every position of 0 to 127 once; its first observed_tokens[b] entries are trajectory b's visible positions. In about half of the trajectories, drawn from the seed, exactly the even positions (the states) are visible. `observed_tokens`: either 128 // 2 (only actions masked) or a count drawn evenly. A permutation: trajectory b is decoded in slot decoder_slot[b], held by device decoder_slot[b] // 32.
All inputs are finite; a program needn't handle non-finite values.
Results may differ from the reference program's by a relative error of at most 0.011.
Values may be sent and summed in bfloat16 or wider, within the bound.
A program may use at most 192 MiB of HBM per device.

```python
import math
import jax
import jax.numpy as jnp
from jax import lax

EMBED_DIMENSION = 256
HEADS = 4
HEAD = 64
FF = 1024
L = 128
TRAJ = 4096


def shared_kind(key):
    kinds = jax.random.randint(key, (TRAJ,), 0, 2)
    return kinds.at[0].set(0).at[1].set(0)


def draw_position_permutation(key, part):
    kinds = shared_kind(key)
    key = jax.random.fold_in(key, 11)
    keys_all = jax.random.split(key, TRAJ)
    ranking = jax.vmap(lambda single: jax.random.permutation(single, L))(keys_all).astype(jnp.int32)
    parity = jnp.arange(L, dtype=jnp.int32) % 2
    scores = jnp.where(kinds[:, None] == 1, parity[None, :] * L + ranking, ranking)
    return jnp.argsort(scores, axis=1).astype(jnp.int32)


def draw_observed_tokens(key, part):
    kinds = shared_kind(key)
    key = jax.random.fold_in(key, 12)
    lowest = L // 8
    highest = L - L // 8
    counts = jax.random.randint(key, (TRAJ,), lowest, highest + 1)
    counts = counts.at[0].set(highest).at[1].set(lowest)
    return jnp.where(kinds == 1, L // 2, counts).astype(jnp.int32)


def steps_of(stream_key, dims, cuts, low, largest):
    level = 1.0
    for axis_at, parts in cuts:
        steps = jax.random.uniform(jax.random.fold_in(jax.random.fold_in(stream_key, 6), axis_at), (parts,), jnp.float32, low / len(cuts), largest / len(cuts))
        level = level * jnp.repeat(jnp.exp(steps), dims[axis_at] // parts).reshape((-1,) + (1,) * (len(dims) - 1 - axis_at))
    return level


def noise(own_key, dims, width, bound, cuts=(), held_as=jnp.bfloat16):
    factor_of = steps_of(own_key, dims, cuts, -0.22, 0.18) if cuts else 1.0
    values = jax.random.normal(own_key, dims, jnp.float32) * width * factor_of
    return jnp.minimum(jnp.maximum(values, -bound), bound).astype(held_as)


def setup_inputs(seed: int = 0) -> dict:
    arg_keys = jax.random.split(jax.random.key(seed), 20)
    return {
        "encoder_states": noise(arg_keys[0], (TRAJ, L, EMBED_DIMENSION), 1.0, 6.0, ((1, 128),)),
        "position_permutation": draw_position_permutation(jax.random.fold_in(arg_keys[19], 71), 0),
        "observed_tokens": draw_observed_tokens(jax.random.fold_in(arg_keys[19], 71), 0),
        "decoder_slot": jax.random.permutation(arg_keys[3], TRAJ).astype(jnp.int32),
        "hidden_token_vector": noise(arg_keys[4], (EMBED_DIMENSION,), 1.0, 5.0),
        "temporal_embedding": noise(arg_keys[5], (L // 2, EMBED_DIMENSION), 0.5, 3.0),
        "entry_scale_factor": jnp.clip(1.0 + 0.18 * jax.random.normal(arg_keys[6], (EMBED_DIMENSION,), jnp.float32), 0.099609375, 1.8984375).astype(jnp.bfloat16),
        "entry_offset_vector": noise(arg_keys[7], (EMBED_DIMENSION,), 0.3, 2.0),
        "query_key_value_matrices": noise(arg_keys[8], (EMBED_DIMENSION, 3 * EMBED_DIMENSION), EMBED_DIMENSION ** -0.5, 0.375),
        "query_value_biases": noise(arg_keys[9], (2, EMBED_DIMENSION), 0.5, 3.0),
        "attention_outmatrix": noise(arg_keys[10], (EMBED_DIMENSION, EMBED_DIMENSION), (EMBED_DIMENSION // 64) ** -0.5, 3.0),
        "attention_outbias": noise(arg_keys[11], (EMBED_DIMENSION,), 0.3, 2.0),
        "center_scale_factor": jnp.clip(1.0 + 0.18 * jax.random.normal(arg_keys[12], (EMBED_DIMENSION,), jnp.float32), 0.099609375, 1.8984375).astype(jnp.bfloat16),
        "center_offset_vector": noise(arg_keys[13], (EMBED_DIMENSION,), 0.3, 2.0),
        "widening_matrix": noise(arg_keys[14], (EMBED_DIMENSION, FF), EMBED_DIMENSION ** -0.5, 0.375),
        "widening_bias": noise(arg_keys[15], (FF,), 0.5, 3.0),
        "narrowing_matrix": noise(arg_keys[16], (FF, EMBED_DIMENSION), FF ** -0.5, 0.1875),
        "narrowing_bias": noise(arg_keys[17], (EMBED_DIMENSION,), 0.3, 2.0),
        "output_sensitivity": noise(arg_keys[18], (TRAJ, L, EMBED_DIMENSION), 1.0, 6.0, ((0, 128),)),
    }


@jax.custom_vjp
def bottom_portion(v):
    return lax.optimization_barrier(v.astype(jnp.bfloat16)).astype(jnp.float32)

@jax.custom_vjp
def low_back(v):
    return v

def low_keep(v):
    return (bottom_portion(v), None)

def low_pass(kept, grad):
    return (grad,)

def back_keep(v):
    return (v, None)

def back_low(kept, grad):
    return (bottom_portion(grad),)
bottom_portion.defvjp(low_keep, low_pass)
low_back.defvjp(back_keep, back_low)
EPSILON = 1e-05

def matmul(operand, against):
    return jnp.einsum('...d,de->...e', operand, against, precision=lax.Precision.HIGHEST)

def standardize_rows(values, gain_vec, shift_vec):
    centred = values - lax.optimization_barrier(jnp.mean(values, axis=-1, keepdims=True))
    spread = lax.optimization_barrier(jnp.mean(centred * centred, axis=-1, keepdims=True))
    return centred * lax.rsqrt(spread + EPSILON) * gain_vec + shift_vec

def evaluate_decoder(decoder_arguments, observed_indicator, hidden_token_vector, temporal_embedding, entry_scale_factor, entry_offset_vector, query_key_value_matrices, query_value_biases, attention_outmatrix, attention_outbias, center_scale_factor, center_offset_vector, widening_matrix, widening_bias, narrowing_matrix, narrowing_bias):
    batch_size, length, features = decoder_arguments.shape
    stamped = jnp.repeat(temporal_embedding, 2, axis=0)
    argument_bundle = jnp.where(observed_indicator[:, :, None], decoder_arguments, hidden_token_vector) + stamped
    leading_segment = bottom_portion(standardize_rows(argument_bundle, entry_scale_factor, entry_offset_vector))
    joined = jnp.concatenate([query_value_biases[0], jnp.zeros_like(query_value_biases[0]), query_value_biases[1]])
    triple = bottom_portion(low_back(matmul(leading_segment, query_key_value_matrices) + joined))
    shaped = triple.reshape(batch_size, length, 3, HEADS, HEAD)
    queries = shaped[:, :, 0]
    key_part = shaped[:, :, 1]
    value_part = shaped[:, :, 2]
    scores = low_back(jnp.einsum('sqhd,skhd->shqk', queries, key_part, precision=lax.Precision.HIGHEST) / math.sqrt(HEAD))
    attention = bottom_portion(jax.nn.softmax(scores, axis=-1))
    attended = bottom_portion(low_back(jnp.einsum('shqk,skhd->sqhd', attention, value_part, precision=lax.Precision.HIGHEST)))
    attended = attended.reshape(batch_size, length, features)
    middle = argument_bundle + low_back(matmul(attended, attention_outmatrix) + attention_outbias)
    second = bottom_portion(standardize_rows(middle, center_scale_factor, center_offset_vector))
    hidden = low_back(matmul(second, widening_matrix) + widening_bias)
    active = bottom_portion(jax.nn.gelu(hidden, approximate=False))
    return middle + low_back(matmul(active, narrowing_matrix) + narrowing_bias)

def reference(encoder_states, position_permutation, observed_tokens, decoder_slot, hidden_token_vector, temporal_embedding, entry_scale_factor, entry_offset_vector, query_key_value_matrices, query_value_biases, attention_outmatrix, attention_outbias, center_scale_factor, center_offset_vector, widening_matrix, widening_bias, narrowing_matrix, narrowing_bias, output_sensitivity):
    overall, length, features = encoder_states.shape
    weight_collection = tuple((cohort_element.astype(jnp.float32) for cohort_element in (hidden_token_vector, temporal_embedding, entry_scale_factor, entry_offset_vector, query_key_value_matrices, query_value_biases, attention_outmatrix, attention_outbias, center_scale_factor, center_offset_vector, widening_matrix, widening_bias, narrowing_matrix, narrowing_bias)))
    group_size = math.gcd(overall, 32)
    blocks = overall // group_size
    positions = jnp.arange(length, dtype=jnp.int32)
    targets = output_sensitivity[decoder_slot]
    pieces = (encoder_states.reshape(blocks, group_size, length, features), position_permutation.reshape(blocks, group_size, length), observed_tokens.reshape(blocks, group_size), targets.reshape(blocks, group_size, length, features))

    def one_block(totals, cohort_element):
        decoder_arguments, block_order, block_visible, block_target = cohort_element
        matches = (block_order[:, :, None] == positions[None, None, :]).astype(jnp.int32)
        rank_of = lax.optimization_barrier(jnp.sum(matches * positions[None, :, None], axis=1))
        observed_indicator = rank_of < block_visible[:, None]

        def apply_block(values, *weights):
            return evaluate_decoder(values, observed_indicator, *weights)
        result, pullback = jax.vjp(apply_block, decoder_arguments.astype(jnp.float32), *weight_collection)
        gradients = pullback(block_target.astype(jnp.float32))
        totals = tuple((earlier + update for earlier, update in zip(totals, gradients[1:])))
        return (totals, (result.astype(jnp.bfloat16), gradients[0].astype(jnp.bfloat16)))
    initial = tuple((jnp.zeros_like(cohort_element) for cohort_element in weight_collection))
    totals, (results, input_grads) = lax.scan(one_block, initial, pieces)
    decoded = jnp.zeros((overall, length, features), jnp.bfloat16).at[decoder_slot].set(results.reshape(overall, length, features))
    grad_encoded = input_grads.reshape(overall, length, features)
    return (decoded, grad_encoded, totals[0], totals[1], totals[2], totals[3], totals[4], totals[5], totals[6], totals[7], totals[8], totals[9], totals[10], totals[11], totals[12], totals[13])
```

```python
import functools
import math

import jax
import jax.numpy as jnp
from jax import lax
from jax.experimental import pallas as pl
from jax.experimental.pallas import tpu as pltpu
from jax.sharding import PartitionSpec as P

MESH = pl.DeviceIdType.MESH

F32 = jnp.float32
BF = jnp.bfloat16
EPSILON = 1e-05
G = 4
L = 128
D = 256
H = 4
R = G * L


def nn(a, b):
    return lax.dot_general(a, b, (((1,), (0,)), ((), ())), preferred_element_type=F32)


def nt(a, b):
    return lax.dot_general(a, b, (((1,), (1,)), ((), ())), preferred_element_type=F32)


def tn(a, b):
    return lax.dot_general(a, b, (((0,), (0,)), ((), ())), preferred_element_type=F32)


def fold(x):
    return jnp.sum(x.reshape(x.shape[0] // 8, 8, x.shape[1]), axis=0)


def norm(x):
    c = x - jnp.mean(x, axis=-1, keepdims=True)
    inv = lax.rsqrt(jnp.mean(c * c, axis=-1, keepdims=True) + EPSILON)
    return c * inv, inv


def norm_back(up, n, inv, gain):
    e = up * gain
    return inv * (e - jnp.mean(e, axis=-1, keepdims=True) - n * jnp.mean(e * n, axis=-1, keepdims=True))


A1, A2, A3, A4, A5 = 0.254829592, -0.284496736, 1.421413741, -1.453152027, 1.061405429
PP = 0.3275911 * math.sqrt(0.5)
CP = 1.0 / math.sqrt(2.0 * math.pi)


def gelu_parts(h):
    t = pl.reciprocal(1.0 + PP * jnp.abs(h), approx=True)
    e = jnp.exp(h * h * -0.5)
    q = t * (0.5 * A1 + t * (0.5 * A2 + t * (0.5 * A3 + t * (0.5 * A4 + t * (0.5 * A5))))) * e
    phi = jnp.where(h >= 0.0, 1.0 - q, q)
    return h * phi, phi + (CP * h) * e


def head_masks():
    lane = lax.broadcasted_iota(jnp.int32, (1, D), 1) // 64
    return [(lane == h).astype(F32).astype(BF) for h in range(H)]


def group(w, s, acc, load_x, load_mask, load_up, store_out, store_ret):
    rows = lambda t: slice(t * L, (t + 1) * L)
    masks = head_masks()
    stamped = w.stamped[...]
    hid = w.hidden[...]
    inv1, inv2, mask = [None] * G, [None] * G, [None] * G
    for t in range(G):
        x = load_x(t)
        m = load_mask(t)
        m2 = jnp.concatenate([m, m], axis=1) > 0.5
        x = jnp.where(m2, x, hid) + stamped
        s.mid[rows(t), :] = x
        n, inv1[t] = norm(x)
        s.n1[rows(t), :] = n
        s.first[rows(t), :] = (n * w.gain1[...] + w.shift1[...]).astype(BF)
    for c, ref in enumerate((s.q, s.k, s.v)):
        y = nn(s.first[...], w.qkv[:, c * D:(c + 1) * D]) + w.bqkv[:, c * D:(c + 1) * D]
        y = y.astype(BF)
        if c == 0:
            y = y * BF(0.125)
        ref[...] = y
    for t in range(G):
        q = s.q[rows(t), :]
        for h in range(H):
            s.qm[t, h * L:(h + 1) * L, :] = q * masks[h]
        st = nt(s.k[rows(t), :], s.qm[t])
        e = jnp.exp(st - jnp.max(st, axis=0, keepdims=True))
        p = e * (1.0 / jnp.sum(e, axis=0, keepdims=True))
        s.p[t] = p
        s.pb[t] = p.astype(BF)
    for t in range(G):
        vt = s.v[rows(t), :].T
        for h in range(H):
            o = nn(vt[h * 64:(h + 1) * 64, :], s.pb[t, :, h * L:(h + 1) * L])
            s.ot[h * 64:(h + 1) * 64, rows(t)] = o.astype(BF)
        s.o[rows(t), :] = s.ot[:, rows(t)].T
    proj = nn(s.o[...], w.out[...])
    for t in range(G):
        mid = s.mid[rows(t), :] + proj[rows(t), :] + w.bout[...]
        s.mid[rows(t), :] = mid
        n, inv2[t] = norm(mid)
        s.n2[rows(t), :] = n
        s.second[rows(t), :] = (n * w.gain2[...] + w.shift2[...]).astype(BF)
    for c in range(4):
        cols = slice(c * D, (c + 1) * D)
        for t in range(G):
            up = load_up(t)
            h = nn(s.second[rows(t), :], w.wide[:, cols]) + w.bwide[:, cols]
            ba = nt(up, w.narrow[cols, :])
            a, da = gelu_parts(h)
            s.act[rows(t), cols] = a.astype(BF)
            bh = ba * da
            s.bh[rows(t), cols] = bh.astype(BF)
            acc.lift[:, cols] += fold(bh)
    dec = nn(s.act[...], w.narrow[...])
    bsec = nt(s.bh[...], w.wide[...])
    for t in range(G):
        up = load_up(t).astype(F32)
        store_out(t, (s.mid[rows(t), :] + dec[rows(t), :] + w.bnarrow[...]).astype(BF))
        n, b = s.n2[rows(t), :], bsec[rows(t), :]
        acc.trail[...] += fold(up)
        acc.midnorm[...] += fold(b * n)
        acc.midshift[...] += fold(b)
        bm = up + norm_back(b, n, inv2[t], w.gain2[...])
        s.mid[rows(t), :] = bm
        acc.recenter[...] += fold(bm)
        s.branch[rows(t), :] = bm.astype(BF)
    s.do[...] = nt(s.branch[...], w.out[...]).astype(BF)
    for t in range(G):
        do = s.do[rows(t), :]
        for h in range(H):
            s.dom[t, h * L:(h + 1) * L, :] = do * masks[h]
        dp = nt(s.v[rows(t), :], s.dom[t])
        p = s.p[t]
        pd = p * dp
        ds = pd - p * jnp.sum(pd, axis=0, keepdims=True)
        s.ds[t] = ds.astype(BF)
    for t in range(G):
        dv = nn(s.pb[t], s.dom[t])
        dk = nn(s.ds[t], s.qm[t])
        s.bt[rows(t), 2 * D:] = dv.astype(BF)
        s.bt[rows(t), D:2 * D] = dk.astype(BF)
        acc.offsets[:, D:] += fold(dv)
        kt = s.k[rows(t), :].T
        for h in range(H):
            dq = nn(kt[h * 64:(h + 1) * 64, :], s.ds[t, :, h * L:(h + 1) * L]) * 0.125
            s.dqt[t, h * 64:(h + 1) * 64, :] = dq.astype(BF)
        dq = s.dqt[t].T
        s.bt[rows(t), :D] = dq
        acc.offsets[:, :D] += fold(dq.astype(F32))
    bfirst = nt(s.bt[...], w.qkv[...])
    for t in range(G):
        n, b = s.n1[rows(t), :], bfirst[rows(t), :]
        acc.scale[...] += fold(b * n)
        acc.shift[...] += fold(b)
        bi = s.mid[rows(t), :] + norm_back(b, n, inv1[t], w.gain1[...])
        m = load_mask(t)
        m2 = jnp.concatenate([m, m], axis=1) > 0.5
        acc.time[...] += bi
        ret = jnp.where(m2, bi, 0.0)
        acc.hidden[...] += fold(bi - ret)
        store_ret(t, ret)
    up = s.up_all()
    acc.proj[...] += tn(s.first[...], s.bt[...])
    acc.mix[...] += nn(s.ot[...], s.branch[...])
    acc.exp[...] += tn(s.second[...], s.bh[...])
    acc.red[...] += tn(up, s.act[...])


class Bag:
    def __init__(self, **kw):
        self.__dict__.update(kw)


SCRATCH = dict(
    mid=((R, D), F32), n1=((R, D), F32), n2=((R, D), F32), first=((R, D), BF), second=((R, D), BF),
    q=((R, D), BF), k=((R, D), BF), v=((R, D), BF), qm=((G, H * L, D), BF), dom=((G, H * L, D), BF),
    p=((G, L, H * L), F32), pb=((G, L, H * L), BF), ds=((G, L, H * L), BF),
    ot=((D, R), BF), o=((R, D), BF), dqt=((G, D, L), BF),
    act=((R, 4 * D), BF), bh=((R, 4 * D), BF), branch=((R, D), BF), do=((R, D), BF), bt=((R, 3 * D), BF),
)
ACC = dict(
    lift=(8, 4 * D), trail=(8, D), midnorm=(8, D), midshift=(8, D), recenter=(8, D), offsets=(8, 2 * D),
    scale=(8, D), shift=(8, D), hidden=(8, D), time=(L, D),
)
COLUMNS = dict(proj=(0, 3 * D), mix=(3 * D, D), exp=(4 * D, 4 * D), red=(8 * D, 4 * D))
WIDE = 12 * D
WEIGHTS = dict(
    hidden=((1, D), F32), stamped=((L, D), F32), gain1=((1, D), F32), shift1=((1, D), F32), qkv=((D, 3 * D), BF),
    bqkv=((1, 3 * D), F32), out=((D, D), BF), bout=((1, D), F32), gain2=((1, D), F32), shift2=((1, D), F32),
    wide=((D, 4 * D), BF), bwide=((1, 4 * D), F32), narrow=((4 * D, D), BF), bnarrow=((1, D), F32),
)


def weights_of(hidden_token_vector, temporal_embedding, entry_scale_factor, entry_offset_vector, query_key_value_matrices,
               query_value_biases, attention_outmatrix, attention_outbias, center_scale_factor, center_offset_vector,
               widening_matrix, widening_bias, narrowing_matrix, narrowing_bias):
    row = lambda v: v.astype(F32).reshape(1, -1)
    b = query_value_biases
    return dict(
        hidden=row(hidden_token_vector), stamped=jnp.repeat(temporal_embedding.astype(F32), 2, axis=0),
        gain1=row(entry_scale_factor), shift1=row(entry_offset_vector), qkv=query_key_value_matrices,
        bqkv=row(jnp.concatenate([b[0], jnp.zeros_like(b[0]), b[1]])), out=attention_outmatrix, bout=row(attention_outbias),
        gain2=row(center_scale_factor), shift2=row(center_offset_vector), wide=widening_matrix, bwide=row(widening_bias),
        narrow=narrowing_matrix, bnarrow=row(narrowing_bias))


N = 128
PHASES = 4
EACH = 8
TRAJ = 4096
CHIPS = 64
CW = 384
VECTORS = dict(lift=4, trail=1, midnorm=1, midshift=1, recenter=1, offsets=2, scale=1, shift=1, hidden=1)
SMALL = 80
HALF = SMALL // 2


def place_of(slot):
    return (slot // EACH) % PHASES * (N * EACH) + slot // 32 * EACH + slot % EACH


def prep_kernel(unroll, place, obs, enc, perm, out, pown, oown, src, dst, owner, sem):
    me = lax.axis_index("dp")
    x = enc[...].astype(F32)
    src[:TRAJ] = x[:, :L]
    src[TRAJ:] = x[:, L:]

    def block(i, _):
        js = [place[i * unroll + u] for u in range(unroll)]
        vs = [(src[pl.ds(i * unroll + u, 1), :], src[pl.ds(TRAJ + i * unroll + u, 1), :]) for u in range(unroll)]
        for u in range(unroll):
            dst[pl.ds(js[u], 1), :] = vs[u][0]
            dst[pl.ds(TRAJ + js[u], 1), :] = vs[u][1]
            owner[js[u]] = i * unroll + u
        return 0

    lax.fori_loop(0, TRAJ // unroll, block, 0)
    copies = []
    for j in range(32):
        b = owner[(j // EACH) * (N * EACH) + me * EACH + j % EACH]
        copy = pltpu.make_async_copy(perm.at[pl.ds(b, 1)], pown.at[pl.ds(j, 1)], sem.at[j])
        copy.start()
        copies.append(copy)
        oown[j] = obs[b]
    for g in range(PHASES):
        at = g * N * EACH
        y = jnp.concatenate([dst[pl.ds(at, N * EACH), :], dst[pl.ds(TRAJ + at, N * EACH), :]], axis=1)
        out[g] = y.astype(BF).reshape(N, EACH, D)
    for copy in copies:
        copy.wait()


def prep(place, obs, enc, perm):
    vm, sm, an = (pl.BlockSpec(memory_space=m) for m in (pltpu.VMEM, pltpu.SMEM, pl.ANY))
    return pl.pallas_call(
        functools.partial(prep_kernel, 16),
        out_shape=[
            jax.ShapeDtypeStruct((PHASES, N, EACH, D), BF),
            jax.ShapeDtypeStruct((32, L), jnp.int32),
            jax.ShapeDtypeStruct((32,), jnp.int32),
        ],
        in_specs=[sm, sm, vm, an],
        out_specs=[vm, vm, sm],
        scratch_shapes=[
            pltpu.VMEM((2 * TRAJ, L), F32),
            pltpu.VMEM((2 * TRAJ, L), F32),
            pltpu.SMEM((TRAJ,), jnp.int32),
            pltpu.SemaphoreType.DMA((32,)),
        ],
        compiler_params=pltpu.CompilerParams(vmem_limit_bytes=56 << 20),
    )(place, obs, enc, perm)


def shifted(me, k):
    c = (me + k) % 2
    x = (me // 2 + k // 2) % 4
    y = (me // 8 + k // 8) % 4
    z = (me // 32 + k // 32) % 4
    return ((z * 4 + y) * 4 + x) * 2 + c


def remote(src, dst, send, recv, to):
    return pltpu.make_async_remote_copy(src, dst, send, recv, device_id=(to,), device_id_type=MESH)


def landed_all(ref, sem):
    pltpu.make_async_copy(ref, ref, sem).wait()


MAIN_SCRATCH = dict(
    recv=((PHASES, N, EACH, D), BF), ret=((PHASES, N, EACH, D), BF), land=((PHASES, N, EACH, D), BF),
    mask=((32, L, L), F32), x32=((2, N * EACH, L), F32), ret32=((2, N * EACH, L), F32),
    land32=((2 * TRAJ, L), F32), out32=((2 * TRAJ, L), F32), ga=((D, WIDE), F32),
    sib_send=((CHIPS, 16, CW), BF), sib_recv=((CHIPS, 16, CW), BF),
    rs_send=((CHIPS, 16, CW), BF), rs_recv=((CHIPS, 16, CW), BF), ag_send=((16, CW), BF),
    small=((SMALL, D), F32), small_sib=((HALF, D), F32), hop_send=((3, HALF, D), F32), hop=((3, 4, HALF, D), F32),
)


def main_kernel(*refs):
    nw = len(WEIGHTS)
    outgoing, pown, oown, place, upr = refs[:5]
    w = Bag(**dict(zip(WEIGHTS, refs[5:5 + nw])))
    refs = refs[5 + nw:]
    dec, genc, ag, small_out = refs[:4]
    refs = refs[4:]
    m = Bag(**dict(zip(MAIN_SCRATCH, refs)))
    refs = refs[len(MAIN_SCRATCH):]
    s = Bag(**dict(zip(SCRATCH, refs)))
    refs = refs[len(SCRATCH):]
    acc = Bag(**dict(zip(ACC, refs)))
    in_send, in_recv, out_send, out_recv, one_send, one_recv, rs_sem, ag_sem = refs[len(ACC):]
    for k, (at, width) in COLUMNS.items():
        setattr(acc, k, m.ga.at[:, pl.ds(at, width)])
    me = lax.axis_index("dp")
    core, chip = me % 2, me // 2
    sibling = me + 1 - 2 * core

    for g in range(PHASES):
        pltpu.make_async_copy(outgoing.at[g, me], m.recv.at[g, me], in_recv.at[g]).start()

        def send_in(k, _):
            to = shifted(me, k)
            remote(outgoing.at[g, to], m.recv.at[g, me], in_send.at[g], in_recv.at[g], to).start()
            return 0

        lax.fori_loop(1, N, send_in, 0)

    m.ga[...] = jnp.zeros_like(m.ga)
    for k in ACC:
        r = getattr(acc, k)
        r[...] = jnp.zeros_like(r)

    def one_mask(j, _):
        order = pown[pl.ds(j, 1), :]
        hot = (order == lax.broadcasted_iota(jnp.int32, (L, L), 0)).astype(F32).astype(BF)
        early = (lax.broadcasted_iota(jnp.int32, (L, L), 0) < oown[j]).astype(F32).astype(BF)
        m.mask[j] = nn(hot, early)
        return 0

    lax.fori_loop(0, 32, one_mask, 0)

    def phase(g, _):
        landed_all(m.recv.at[g], in_recv.at[g])
        a = m.recv[g].reshape(N * EACH, D).astype(F32)
        m.x32[0] = a[:, :L]
        m.x32[1] = a[:, L:]

        def half(hf, _):
            base = g * EACH + hf * G
            own = lambda t: pl.ds(hf * G + t, L, stride=EACH)
            s.up_all = lambda: upr[pl.ds(base, G)].reshape(R, D)

            def store_out(t, v):
                dec[base + t] = v

            def store_ret(t, v):
                for i in range(2):
                    m.ret32[i, own(t), :] = v[:, i * L:(i + 1) * L]

            group(
                w, s, acc,
                load_x=lambda t: jnp.concatenate([m.x32[i, own(t), :] for i in range(2)], axis=1),
                load_mask=lambda t: m.mask[base + t],
                load_up=lambda t: upr[base + t],
                store_out=store_out,
                store_ret=store_ret,
            )
            return 0

        lax.fori_loop(0, EACH // G, half, 0)
        m.ret[g] = jnp.concatenate([m.ret32[0], m.ret32[1]], axis=1).astype(BF).reshape(N, EACH, D)
        pltpu.make_async_copy(m.ret.at[g, me], m.land.at[g, me], out_recv.at[g]).start()

        def send_out(k, _):
            to = shifted(me, k)
            remote(m.ret.at[g, to], m.land.at[g, me], out_send.at[g], out_recv.at[g], to).start()
            return 0

        lax.fori_loop(1, N, send_out, 0)
        return 0

    lax.fori_loop(0, PHASES, phase, 0)

    for r in range(16):
        for j in range(4):
            at = pl.multiple_of((2 * j + 1 - core) * CW, L)
            m.sib_send[r * 4 + j] = m.ga[r * 16:(r + 1) * 16, pl.ds(at, CW)].astype(BF)
    big_sib = remote(m.sib_send, m.sib_recv, one_send.at[0], one_recv.at[0], sibling)
    big_sib.start()
    t3 = acc.time[...].reshape(64, 2, D)
    m.small[:64] = t3[:, 0] + t3[:, 1]
    m.small[64:] = jnp.zeros((16, D), F32)
    at = 64
    for k, rows in VECTORS.items():
        v = jnp.sum(getattr(acc, k)[...], axis=0, keepdims=True)
        for i in range(rows):
            m.small[at:at + 1, :] = v[:, i * D:(i + 1) * D]
            at += 1
    mine = pl.ds(pl.multiple_of(core * HALF, 8), HALF)
    other = pl.ds(pl.multiple_of((1 - core) * HALF, 8), HALF)
    small_sib = remote(m.small.at[other], m.small_sib, one_send.at[1], one_recv.at[1], sibling)
    small_sib.start()
    small_sib.wait()
    value = m.small[mine, :] + m.small_sib[...]

    def hop_start(axis, value):
        unit = (2, 8, 32)[axis]
        here = (me // unit) % 4
        m.hop_send[axis] = value
        m.hop[axis, here] = value
        copies = []
        for d in (1, 3, 2):
            to = me + ((here + d) % 4 - here) * unit
            c = remote(m.hop_send.at[axis], m.hop.at[axis, here], one_send.at[2 + 3 * axis + d - 1], one_recv.at[2 + 3 * axis + d - 1], to)
            c.start()
            copies.append(c)
        return copies

    def hop_end(axis, copies):
        for c in copies:
            c.wait()
        return (m.hop[axis, 0] + m.hop[axis, 1]) + (m.hop[axis, 2] + m.hop[axis, 3])

    copies = hop_start(0, value)
    big_sib.wait()
    for r in range(16):
        for j in range(4):
            at = pl.multiple_of((2 * j + core) * CW, L)
            v = m.ga[r * 16:(r + 1) * 16, pl.ds(at, CW)] + m.sib_recv[r * 4 + j].astype(F32)
            m.rs_send[r * 4 + j] = v.astype(BF)
    pltpu.make_async_copy(m.rs_send.at[chip], m.rs_recv.at[chip], rs_sem.at[1]).start()

    def send_rs(k, _):
        to = shifted(me, 2 * k)
        remote(m.rs_send.at[to // 2], m.rs_recv.at[chip], rs_sem.at[0], rs_sem.at[1], to).start()
        return 0

    lax.fori_loop(1, CHIPS, send_rs, 0)
    value = hop_end(0, copies)
    copies = hop_start(1, value)

    for g in range(PHASES):
        landed_all(m.land.at[g], out_recv.at[g])
        a = m.land[g].reshape(N * EACH, D).astype(F32)
        m.land32[g * N * EACH:(g + 1) * N * EACH] = a[:, :L]
        m.land32[TRAJ + g * N * EACH:TRAJ + (g + 1) * N * EACH] = a[:, L:]
    value = hop_end(1, copies)
    copies = hop_start(2, value)
    landed_all(m.rs_recv, rs_sem.at[1])
    m.ag_send[...] = jnp.sum(m.rs_recv[...].astype(F32), axis=0).astype(BF)
    pltpu.make_async_copy(m.ag_send, ag.at[core, chip], ag_sem.at[1]).start()

    def send_ag(k, _):
        to = shifted(me, 2 * k)
        remote(m.ag_send, ag.at[core, chip], ag_sem.at[0], ag_sem.at[1], to).start()
        return 0

    lax.fori_loop(1, CHIPS, send_ag, 0)
    value = hop_end(2, copies)
    small_out[mine, :] = value
    small_last = remote(small_out.at[mine], small_out.at[mine], one_send.at[11], one_recv.at[11], sibling)
    small_last.start()

    def gather(i, _):
        js = [place[i * 16 + u] for u in range(16)]
        vs = [(m.land32[pl.ds(j, 1), :], m.land32[pl.ds(TRAJ + j, 1), :]) for j in js]
        for u in range(16):
            m.out32[pl.ds(i * 16 + u, 1), :] = vs[u][0]
            m.out32[pl.ds(TRAJ + i * 16 + u, 1), :] = vs[u][1]
        return 0

    lax.fori_loop(0, TRAJ // 16, gather, 0)
    genc[...] = jnp.concatenate([m.out32[:TRAJ], m.out32[TRAJ:]], axis=1).astype(BF)
    landed_all(ag.at[core], ag_sem.at[1])
    big_last = remote(ag.at[core], ag.at[core], one_send.at[12], one_recv.at[12], sibling)
    big_last.start()
    small_last.wait()
    for g in range(PHASES):
        landed_all(m.recv.at[g, pl.ds(0, N - 1)], in_send.at[g])
        landed_all(m.ret.at[g, pl.ds(0, N - 1)], out_send.at[g])
    landed_all(m.rs_send.at[pl.ds(0, CHIPS - 1)], rs_sem.at[0])
    landed_all(m.rs_send.at[pl.ds(0, CHIPS - 1)], ag_sem.at[0])
    big_last.wait()


def main(outgoing, pown, oown, place, up, weights):
    vm, sm, an = (pl.BlockSpec(memory_space=m) for m in (pltpu.VMEM, pltpu.SMEM, pl.ANY))
    scratch = [pltpu.VMEM(shape, kind) for shape, kind in MAIN_SCRATCH.values()]
    scratch += [pltpu.VMEM(shape, kind) for shape, kind in SCRATCH.values()]
    scratch += [pltpu.VMEM(shape, F32) for shape in ACC.values()]
    scratch += [pltpu.SemaphoreType.DMA((n,)) for n in (PHASES, PHASES, PHASES, PHASES, 13, 13, 2, 2)]
    return pl.pallas_call(
        main_kernel,
        out_shape=[
            jax.ShapeDtypeStruct((32, L, D), BF),
            jax.ShapeDtypeStruct((TRAJ, D), BF),
            jax.ShapeDtypeStruct((2, CHIPS, 16, CW), BF),
            jax.ShapeDtypeStruct((SMALL, D), F32),
        ],
        in_specs=[an, vm, sm, sm, vm] + [vm] * len(WEIGHTS),
        out_specs=[vm] * 4,
        scratch_shapes=scratch,
        compiler_params=pltpu.CompilerParams(vmem_limit_bytes=62 << 20, has_side_effects=True),
    )(outgoing, pown, oown, place, up, *[weights[k] for k in WEIGHTS])


LAST = dict(time=64, **VECTORS)


def last_kernel(dec, genc, ag, small, dec_out, genc_out, proj, mix, exp, red, *rest):
    outs, (ga, sem) = rest[:len(LAST)], rest[len(LAST):]
    copies = [pltpu.make_async_copy(dec, dec_out, sem.at[0]), pltpu.make_async_copy(genc, genc_out, sem.at[1])]
    for copy in copies:
        copy.start()
    for r in range(16):
        for c in range(8):
            ga[r * 16:(r + 1) * 16, c * CW:(c + 1) * CW] = ag[c % 2, r * 4 + c // 2].astype(F32)
    proj[...] = ga[:, :3 * D]
    mix[...] = ga[:, 3 * D:4 * D]
    exp[...] = ga[:, 4 * D:8 * D]
    red[...] = ga[:, 8 * D:].T
    at = 0
    for out, rows in zip(outs, LAST.values()):
        out[...] = small[at:at + rows, :]
        at += rows
    for copy in copies:
        copy.wait()


def last(dec, genc, ag, small):
    vm, an = (pl.BlockSpec(memory_space=m) for m in (pltpu.VMEM, pl.ANY))
    shapes = [((32, L, D), BF), ((TRAJ, D), BF), ((D, 3 * D), F32), ((D, D), F32), ((D, 4 * D), F32), ((4 * D, D), F32)]
    shapes += [((rows, D), F32) for rows in LAST.values()]
    return pl.pallas_call(
        last_kernel,
        out_shape=[jax.ShapeDtypeStruct(*s) for s in shapes],
        in_specs=[an, an, vm, vm],
        out_specs=[an, an] + [vm] * (len(shapes) - 2),
        scratch_shapes=[pltpu.VMEM((D, WIDE), F32), pltpu.SemaphoreType.DMA((2,))],
        compiler_params=pltpu.CompilerParams(vmem_limit_bytes=40 << 20),
    )(dec, genc, ag, small)


def on_device(encoder_states, position_permutation, observed_tokens, decoder_slot, *rest):
    weights, sensitivity = weights_of(*rest[:-1]), rest[-1]
    place = place_of(decoder_slot)
    outgoing, pown, oown = prep(place, observed_tokens, encoder_states.reshape(TRAJ, D), position_permutation)
    dec, genc, ag, small = main(outgoing, pown, oown, place, sensitivity, weights)
    dec, genc, proj, mix, exp, red, *vectors = last(dec, genc, ag, small)
    v = dict(zip(LAST, vectors))
    flat = lambda k: v[k].reshape(-1)
    return (
        dec, genc.reshape(TRAJ, 1, D), flat("hidden"), v["time"], flat("scale"), flat("shift"), proj, v["offsets"], mix,
        flat("recenter"), flat("midnorm"), flat("midshift"), exp, flat("lift"), red, flat("trail"),
    )


def solution(mesh):
    in_specs = (P(None, "dp", None),) + (P(),) * 17 + (P("dp", None, None),)
    out_specs = (P("dp", None, None), P(None, "dp", None)) + (P(),) * 14
    return jax.shard_map(on_device, mesh=mesh, in_specs=in_specs, out_specs=out_specs, check_vma=False)
```

```python
import functools
import math

import jax
import jax.numpy as jnp
from jax import lax
from jax.experimental import pallas as pl
from jax.experimental.pallas import tpu as pltpu
from jax.sharding import PartitionSpec as P

MESH = pl.DeviceIdType.MESH

F32 = jnp.float32
BF = jnp.bfloat16
EPSILON = 1e-05
G = 4
L = 128
D = 256
H = 4
R = G * L


def nn(a, b):
    return lax.dot_general(a, b, (((1,), (0,)), ((), ())), preferred_element_type=F32)


def nt(a, b):
    return lax.dot_general(a, b, (((1,), (1,)), ((), ())), preferred_element_type=F32)


def tn(a, b):
    return lax.dot_general(a, b, (((0,), (0,)), ((), ())), preferred_element_type=F32)


def fold(x):
    return jnp.sum(x.reshape(x.shape[0] // 8, 8, x.shape[1]), axis=0)


def norm(x):
    c = x - jnp.mean(x, axis=-1, keepdims=True)
    inv = lax.rsqrt(jnp.mean(c * c, axis=-1, keepdims=True) + EPSILON)
    return c * inv, inv


def norm_back(up, n, inv, gain):
    e = up * gain
    return inv * (e - jnp.mean(e, axis=-1, keepdims=True) - n * jnp.mean(e * n, axis=-1, keepdims=True))


A1, A2, A3, A4, A5 = 0.254829592, -0.284496736, 1.421413741, -1.453152027, 1.061405429
PP = 0.3275911 * math.sqrt(0.5)
CP = 1.0 / math.sqrt(2.0 * math.pi)


def gelu_parts(h):
    t = pl.reciprocal(1.0 + PP * jnp.abs(h), approx=True)
    e = jnp.exp(h * h * -0.5)
    q = t * (0.5 * A1 + t * (0.5 * A2 + t * (0.5 * A3 + t * (0.5 * A4 + t * (0.5 * A5))))) * e
    phi = jnp.where(h >= 0.0, 1.0 - q, q)
    return h * phi, phi + (CP * h) * e


def head_masks():
    lane = lax.broadcasted_iota(jnp.int32, (1, D), 1) // 64
    return [(lane == h).astype(F32).astype(BF) for h in range(H)]


def group(w, s, acc, load_x, load_mask, load_up, store_out, store_ret):
    rows = lambda t: slice(t * L, (t + 1) * L)
    masks = head_masks()
    stamped = w.stamped[...]
    hid = w.hidden[...]
    inv1, inv2, mask = [None] * G, [None] * G, [None] * G
    for t in range(G):
        x = load_x(t)
        m = load_mask(t)
        m2 = jnp.concatenate([m, m], axis=1) > 0.5
        x = jnp.where(m2, x, hid) + stamped
        s.mid[rows(t), :] = x
        n, inv1[t] = norm(x)
        s.n1[rows(t), :] = n
        s.first[rows(t), :] = (n * w.gain1[...] + w.shift1[...]).astype(BF)
    for c, ref in enumerate((s.q, s.k, s.v)):
        y = nn(s.first[...], w.qkv[:, c * D:(c + 1) * D]) + w.bqkv[:, c * D:(c + 1) * D]
        y = y.astype(BF)
        if c == 0:
            y = y * BF(0.125)
        ref[...] = y
    for t in range(G):
        q = s.q[rows(t), :]
        for h in range(H):
            s.qm[t, h * L:(h + 1) * L, :] = q * masks[h]
        st = nt(s.k[rows(t), :], s.qm[t])
        e = jnp.exp(st - jnp.max(st, axis=0, keepdims=True))
        p = e * (1.0 / jnp.sum(e, axis=0, keepdims=True))
        s.p[t] = p
        s.pb[t] = p.astype(BF)
    for t in range(G):
        vt = s.v[rows(t), :].T
        for h in range(H):
            o = nn(vt[h * 64:(h + 1) * 64, :], s.pb[t, :, h * L:(h + 1) * L])
            s.ot[h * 64:(h + 1) * 64, rows(t)] = o.astype(BF)
        s.o[rows(t), :] = s.ot[:, rows(t)].T
    proj = nn(s.o[...], w.out[...])
    for t in range(G):
        mid = s.mid[rows(t), :] + proj[rows(t), :] + w.bout[...]
        s.mid[rows(t), :] = mid
        n, inv2[t] = norm(mid)
        s.n2[rows(t), :] = n
        s.second[rows(t), :] = (n * w.gain2[...] + w.shift2[...]).astype(BF)
    for c in range(4):
        cols = slice(c * D, (c + 1) * D)
        for t in range(G):
            up = load_up(t)
            h = nn(s.second[rows(t), :], w.wide[:, cols]) + w.bwide[:, cols]
            ba = nt(up, w.narrow[cols, :])
            a, da = gelu_parts(h)
            s.act[rows(t), cols] = a.astype(BF)
            bh = ba * da
            s.bh[rows(t), cols] = bh.astype(BF)
            acc.lift[:, cols] += fold(bh)
    dec = nn(s.act[...], w.narrow[...])
    bsec = nt(s.bh[...], w.wide[...])
    for t in range(G):
        up = load_up(t).astype(F32)
        store_out(t, (s.mid[rows(t), :] + dec[rows(t), :] + w.bnarrow[...]).astype(BF))
        n, b = s.n2[rows(t), :], bsec[rows(t), :]
        acc.trail[...] += fold(up)
        acc.midnorm[...] += fold(b * n)
        acc.midshift[...] += fold(b)
        bm = up + norm_back(b, n, inv2[t], w.gain2[...])
        s.mid[rows(t), :] = bm
        acc.recenter[...] += fold(bm)
        s.branch[rows(t), :] = bm.astype(BF)
    s.do[...] = nt(s.branch[...], w.out[...]).astype(BF)
    for t in range(G):
        do = s.do[rows(t), :]
        for h in range(H):
            s.dom[t, h * L:(h + 1) * L, :] = do * masks[h]
        dp = nt(s.v[rows(t), :], s.dom[t])
        p = s.p[t]
        pd = p * dp
        ds = pd - p * jnp.sum(pd, axis=0, keepdims=True)
        s.ds[t] = ds.astype(BF)
    for t in range(G):
        dv = nn(s.pb[t], s.dom[t])
        dk = nn(s.ds[t], s.qm[t])
        s.bt[rows(t), 2 * D:] = dv.astype(BF)
        s.bt[rows(t), D:2 * D] = dk.astype(BF)
        acc.offsets[:, D:] += fold(dv)
        kt = s.k[rows(t), :].T
        for h in range(H):
            dq = nn(kt[h * 64:(h + 1) * 64, :], s.ds[t, :, h * L:(h + 1) * L]) * 0.125
            s.dqt[t, h * 64:(h + 1) * 64, :] = dq.astype(BF)
        dq = s.dqt[t].T
        s.bt[rows(t), :D] = dq
        acc.offsets[:, :D] += fold(dq.astype(F32))
    bfirst = nt(s.bt[...], w.qkv[...])
    for t in range(G):
        n, b = s.n1[rows(t), :], bfirst[rows(t), :]
        acc.scale[...] += fold(b * n)
        acc.shift[...] += fold(b)
        bi = s.mid[rows(t), :] + norm_back(b, n, inv1[t], w.gain1[...])
        m = load_mask(t)
        m2 = jnp.concatenate([m, m], axis=1) > 0.5
        acc.time[...] += bi
        ret = jnp.where(m2, bi, 0.0)
        acc.hidden[...] += fold(bi - ret)
        store_ret(t, ret)
    up = s.up_all()
    acc.proj[...] += tn(s.first[...], s.bt[...])
    acc.mix[...] += nn(s.ot[...], s.branch[...])
    acc.exp[...] += tn(s.second[...], s.bh[...])
    acc.red[...] += tn(up, s.act[...])


class Bag:
    def __init__(self, **kw):
        self.__dict__.update(kw)


SCRATCH = dict(
    mid=((R, D), F32), n1=((R, D), F32), n2=((R, D), F32), first=((R, D), BF), second=((R, D), BF),
    q=((R, D), BF), k=((R, D), BF), v=((R, D), BF), qm=((G, H * L, D), BF), dom=((G, H * L, D), BF),
    p=((G, L, H * L), F32), pb=((G, L, H * L), BF), ds=((G, L, H * L), BF),
    ot=((D, R), BF), o=((R, D), BF), dqt=((G, D, L), BF),
    act=((R, 4 * D), BF), bh=((R, 4 * D), BF), branch=((R, D), BF), do=((R, D), BF), bt=((R, 3 * D), BF),
)
ACC = dict(
    lift=(8, 4 * D), trail=(8, D), midnorm=(8, D), midshift=(8, D), recenter=(8, D), offsets=(8, 2 * D),
    scale=(8, D), shift=(8, D), hidden=(8, D), time=(L, D),
)
COLUMNS = dict(proj=(0, 3 * D), mix=(3 * D, D), exp=(4 * D, 4 * D), red=(8 * D, 4 * D))
WIDE = 12 * D
WEIGHTS = dict(
    hidden=((1, D), F32), stamped=((L, D), F32), gain1=((1, D), F32), shift1=((1, D), F32), qkv=((D, 3 * D), BF),
    bqkv=((1, 3 * D), F32), out=((D, D), BF), bout=((1, D), F32), gain2=((1, D), F32), shift2=((1, D), F32),
    wide=((D, 4 * D), BF), bwide=((1, 4 * D), F32), narrow=((4 * D, D), BF), bnarrow=((1, D), F32),
)


RAW = ("hidden", "stamped", "gain1", "shift1", "qkv", "bqkv", "out", "bout", "gain2", "shift2", "wide", "bwide", "narrow", "bnarrow")
MATRICES = ("qkv", "out", "wide", "narrow")


def spread(raw, w):
    for k in RAW:
        if k == "stamped":
            v = raw[k][...].astype(F32)
            w.stamped[...] = jnp.broadcast_to(v[:, None, :], (L // 2, 2, D)).reshape(L, D)
        elif k == "bqkv":
            v = raw[k][...].astype(F32)
            w.bqkv[:, :D] = v[:1]
            w.bqkv[:, D:2 * D] = jnp.zeros((1, D), F32)
            w.bqkv[:, 2 * D:] = v[1:]
        elif k not in MATRICES:
            v = raw[k][...].astype(F32)
            getattr(w, k)[...] = v.reshape(1, -1)


N = 128
PHASES = 4
EACH = 8
TRAJ = 4096
CHIPS = 64
CW = 384
VECTORS = dict(lift=4, trail=1, midnorm=1, midshift=1, recenter=1, offsets=2, scale=1, shift=1, hidden=1)
SMALL = 80
HALF = SMALL // 2


def prep_kernel(unroll, slot, obs, enc, perm, out, pown, oown, src, dst, owner, sem):
    me = lax.axis_index("dp")
    x = enc[...].astype(F32)
    src[:TRAJ] = x[:, :L]
    src[TRAJ:] = x[:, L:]

    def block(i, _):
        js = [slot[i * unroll + u] for u in range(unroll)]
        vs = [(src[pl.ds(i * unroll + u, 1), :], src[pl.ds(TRAJ + i * unroll + u, 1), :]) for u in range(unroll)]
        for u in range(unroll):
            dst[pl.ds(js[u], 1), :] = vs[u][0]
            dst[pl.ds(TRAJ + js[u], 1), :] = vs[u][1]
            owner[js[u]] = i * unroll + u
        return 0

    lax.fori_loop(0, TRAJ // unroll, block, 0)
    copies = []
    for j in range(32):
        b = owner[me * 32 + j]
        copy = pltpu.make_async_copy(perm.at[pl.ds(b, 1)], pown.at[pl.ds(j, 1)], sem.at[j])
        copy.start()
        copies.append(copy)
        oown[j] = obs[b]
    for g in range(4):
        at = pl.ds(g * 1024, 1024)
        y = jnp.concatenate([dst[at, :], dst[pl.ds(TRAJ + g * 1024, 1024), :]], axis=1)
        out[g * 32:(g + 1) * 32] = y.astype(BF).reshape(32, PHASES, EACH, D)
    for copy in copies:
        copy.wait()


def prep(slot, obs, enc, perm):
    vm, sm, an = (pl.BlockSpec(memory_space=m) for m in (pltpu.VMEM, pltpu.SMEM, pl.ANY))
    return pl.pallas_call(
        functools.partial(prep_kernel, 16),
        out_shape=[
            jax.ShapeDtypeStruct((N, PHASES, EACH, D), BF),
            jax.ShapeDtypeStruct((32, L), jnp.int32),
            jax.ShapeDtypeStruct((32,), jnp.int32),
        ],
        in_specs=[sm, sm, vm, an],
        out_specs=[vm, vm, sm],
        scratch_shapes=[
            pltpu.VMEM((2 * TRAJ, L), F32),
            pltpu.VMEM((2 * TRAJ, L), F32),
            pltpu.SMEM((TRAJ,), jnp.int32),
            pltpu.SemaphoreType.DMA((32,)),
        ],
        compiler_params=pltpu.CompilerParams(vmem_limit_bytes=56 << 20),
    )(slot, obs, enc, perm)


def others(me, step):
    cs = [me % 2, 1 - me % 2]
    xs = [(me // 2 + d) % 4 * 2 for d in range(4)]
    ys = [(me // 8 + d) % 4 * 8 for d in range(4)]
    zs = [(me // 32 + d) % 4 * 32 for d in range(4)]
    return [zs[k // 32] + ys[k // 8 % 4] + xs[k // 2 % 4] + cs[k % 2] for k in range(step, N, step)]


def remote(src, dst, send, recv, to):
    return pltpu.make_async_remote_copy(src, dst, send, recv, device_id=(to,), device_id_type=MESH)


def landed_all(ref, sem):
    pltpu.make_async_copy(ref, ref, sem).wait()


MAIN_SCRATCH = dict(
    recv=((PHASES, N, EACH, D), BF), ret=((PHASES, N, EACH, D), BF), land=((N, PHASES, EACH, D), BF),
    mask=((32, L, L), F32), x32=((2, N * EACH, L), F32), ret32=((2, N * EACH, L), F32),
    land32=((2 * TRAJ, L), F32), out32=((2 * TRAJ, L), F32), ga=((D, WIDE), F32),
    sib_send=((CHIPS, 16, CW), BF), sib_recv=((CHIPS, 16, CW), BF),
    rs_send=((CHIPS, 16, CW), BF), rs_recv=((CHIPS, 16, CW), BF), ag_send=((16, CW), BF),
    dec_v=((32, L, D), BF), genc_v=((TRAJ, D), BF), up=((32, L, D), BF),
    small=((SMALL, D), F32), small_sib=((HALF, D), F32), hop_send=((3, HALF, D), F32), hop=((3, 4, HALF, D), F32),
)


def main_kernel(*refs):
    outgoing, pown, oown, slot, up_hbm = refs[:5]
    raw = dict(zip(RAW, refs[5:5 + len(RAW)]))
    refs = refs[5 + len(RAW):]
    dec, genc, ag, small_out = refs[:4]
    refs = refs[4:]
    m = Bag(**dict(zip(MAIN_SCRATCH, refs)))
    refs = refs[len(MAIN_SCRATCH):]
    s = Bag(**dict(zip(SCRATCH, refs)))
    refs = refs[len(SCRATCH):]
    w = Bag(**dict(zip(WEIGHTS, refs)))
    refs = refs[len(WEIGHTS):]
    acc = Bag(**dict(zip(ACC, refs)))
    in_send, in_recv, out_send, out_recv, one_send, one_recv, rs_sem, ag_sem, local = refs[len(ACC):]
    for k, (at, width) in COLUMNS.items():
        setattr(acc, k, m.ga.at[:, pl.ds(at, width)])
    me = lax.axis_index("dp")
    core, chip = me % 2, me // 2
    sibling = me + 1 - 2 * core

    def send_in(g):
        pltpu.make_async_copy(outgoing.at[me, g], m.recv.at[g, me], in_recv.at[g]).start()
        for to in others(me, 1):
            remote(outgoing.at[to, g], m.recv.at[g, me], in_send.at[g], in_recv.at[g], to).start()

    send_in(0)
    loads = [pltpu.make_async_copy(up_hbm, m.up, local.at[0])]
    loads += [pltpu.make_async_copy(raw[k], getattr(w, k), local.at[1 + i]) for i, k in enumerate(MATRICES)]
    for copy in loads:
        copy.start()
    spread(raw, w)
    m.ga[...] = jnp.zeros_like(m.ga)
    for k in ACC:
        r = getattr(acc, k)
        r[...] = jnp.zeros_like(r)

    def one_mask(j, _):
        order = pown[pl.ds(j, 1), :]
        hot = (order == lax.broadcasted_iota(jnp.int32, (L, L), 0)).astype(F32).astype(BF)
        early = (lax.broadcasted_iota(jnp.int32, (L, L), 0) < oown[j]).astype(F32).astype(BF)
        m.mask[j] = nn(hot, early)
        return 0

    lax.fori_loop(0, 32, one_mask, 0)
    for copy in loads:
        copy.wait()

    def phase(g, _):
        landed_all(m.recv.at[g], in_recv.at[g])

        @pl.when(g < PHASES - 1)
        def _():
            send_in(g + 1)

        a = m.recv[g].reshape(N * EACH, D).astype(F32)
        m.x32[0] = a[:, :L]
        m.x32[1] = a[:, L:]

        def half(hf, _):
            base = g * EACH + hf * G
            own = lambda t: pl.ds(hf * G + t, L, stride=EACH)
            s.up_all = lambda: m.up[pl.ds(base, G)].reshape(R, D)

            def store_out(t, v):
                m.dec_v[base + t] = v

            def store_ret(t, v):
                for i in range(2):
                    m.ret32[i, own(t), :] = v[:, i * L:(i + 1) * L]

            group(
                w, s, acc,
                load_x=lambda t: jnp.concatenate([m.x32[i, own(t), :] for i in range(2)], axis=1),
                load_mask=lambda t: m.mask[base + t],
                load_up=lambda t: m.up[base + t],
                store_out=store_out,
                store_ret=store_ret,
            )
            return 0

        lax.fori_loop(0, EACH // G, half, 0)
        m.ret[g] = jnp.concatenate([m.ret32[0], m.ret32[1]], axis=1).astype(BF).reshape(N, EACH, D)
        pltpu.make_async_copy(m.ret.at[g, me], m.land.at[me, g], out_recv.at[0]).start()
        for to in others(me, 1):
            remote(m.ret.at[g, to], m.land.at[me, g], out_send.at[g], out_recv.at[0], to).start()
        mine = pl.ds(g * EACH, EACH)
        pltpu.make_async_copy(m.dec_v.at[mine], dec.at[mine], local.at[5]).start()
        return 0

    lax.fori_loop(0, PHASES, phase, 0)

    for r in range(16):
        for j in range(4):
            at = pl.multiple_of((2 * j + 1 - core) * CW, L)
            m.sib_send[r * 4 + j] = m.ga[r * 16:(r + 1) * 16, pl.ds(at, CW)].astype(BF)
    big_sib = remote(m.sib_send, m.sib_recv, one_send.at[0], one_recv.at[0], sibling)
    big_sib.start()
    t3 = acc.time[...].reshape(64, 2, D)
    m.small[:64] = t3[:, 0] + t3[:, 1]
    m.small[64:] = jnp.zeros((16, D), F32)
    at = 64
    for k, rows in VECTORS.items():
        v = jnp.sum(getattr(acc, k)[...], axis=0, keepdims=True)
        for i in range(rows):
            m.small[at:at + 1, :] = v[:, i * D:(i + 1) * D]
            at += 1
    mine = pl.ds(pl.multiple_of(core * HALF, 8), HALF)
    other = pl.ds(pl.multiple_of((1 - core) * HALF, 8), HALF)
    small_sib = remote(m.small.at[other], m.small_sib, one_send.at[1], one_recv.at[1], sibling)
    small_sib.start()
    small_sib.wait()
    value = m.small[mine, :] + m.small_sib[...]

    def hop_start(axis, value):
        unit = (2, 8, 32)[axis]
        here = (me // unit) % 4
        m.hop_send[axis] = value
        m.hop[axis, here] = value
        copies = []
        for d in (1, 3, 2):
            to = me + ((here + d) % 4 - here) * unit
            c = remote(m.hop_send.at[axis], m.hop.at[axis, here], one_send.at[2 + 3 * axis + d - 1], one_recv.at[2 + 3 * axis + d - 1], to)
            c.start()
            copies.append(c)
        return copies

    def hop_end(axis, copies):
        for c in copies:
            c.wait()
        return (m.hop[axis, 0] + m.hop[axis, 1]) + (m.hop[axis, 2] + m.hop[axis, 3])

    copies = hop_start(0, value)
    big_sib.wait()
    for r in range(16):
        for j in range(4):
            at = pl.multiple_of((2 * j + core) * CW, L)
            v = m.ga[r * 16:(r + 1) * 16, pl.ds(at, CW)] + m.sib_recv[r * 4 + j].astype(F32)
            m.rs_send[r * 4 + j] = v.astype(BF)
    pltpu.make_async_copy(m.rs_send.at[chip], m.rs_recv.at[chip], rs_sem.at[1]).start()
    for to in others(me, 2):
        remote(m.rs_send.at[to // 2], m.rs_recv.at[chip], rs_sem.at[0], rs_sem.at[1], to).start()
    value = hop_end(0, copies)
    copies = hop_start(1, value)

    landed_all(m.land, out_recv.at[0])
    for g in range(4):
        a = m.land[g * 32:(g + 1) * 32].reshape(1024, D).astype(F32)
        m.land32[g * 1024:(g + 1) * 1024] = a[:, :L]
        m.land32[TRAJ + g * 1024:TRAJ + (g + 1) * 1024] = a[:, L:]
    value = hop_end(1, copies)
    copies = hop_start(2, value)
    landed_all(m.rs_recv, rs_sem.at[1])
    m.ag_send[...] = jnp.sum(m.rs_recv[...].astype(F32), axis=0).astype(BF)
    pltpu.make_async_copy(m.ag_send, ag.at[core, chip], ag_sem.at[1]).start()
    for to in others(me, 2):
        remote(m.ag_send, ag.at[core, chip], ag_sem.at[0], ag_sem.at[1], to).start()
    value = hop_end(2, copies)
    small_out[mine, :] = value
    small_last = remote(small_out.at[mine], small_out.at[mine], one_send.at[11], one_recv.at[11], sibling)
    small_last.start()

    def gather(i, _):
        js = [slot[i * 16 + u] for u in range(16)]
        vs = [(m.land32[pl.ds(j, 1), :], m.land32[pl.ds(TRAJ + j, 1), :]) for j in js]
        for u in range(16):
            m.out32[pl.ds(i * 16 + u, 1), :] = vs[u][0]
            m.out32[pl.ds(TRAJ + i * 16 + u, 1), :] = vs[u][1]
        return 0

    lax.fori_loop(0, TRAJ // 16, gather, 0)
    m.genc_v[...] = jnp.concatenate([m.out32[:TRAJ], m.out32[TRAJ:]], axis=1).astype(BF)
    genc_copy = pltpu.make_async_copy(m.genc_v, genc, local.at[6])
    genc_copy.start()
    landed_all(ag.at[core], ag_sem.at[1])
    big_last = remote(ag.at[core], ag.at[core], one_send.at[12], one_recv.at[12], sibling)
    big_last.start()
    small_last.wait()
    genc_copy.wait()
    landed_all(m.dec_v, local.at[5])
    for g in range(PHASES):
        landed_all(m.recv.at[g, pl.ds(0, N - 1)], in_send.at[g])
        landed_all(m.ret.at[g, pl.ds(0, N - 1)], out_send.at[g])
    landed_all(m.rs_send.at[pl.ds(0, CHIPS - 1)], rs_sem.at[0])
    landed_all(m.rs_send.at[pl.ds(0, CHIPS - 1)], ag_sem.at[0])
    big_last.wait()


def main(outgoing, pown, oown, slot, up, raw):
    vm, sm, an = (pl.BlockSpec(memory_space=m) for m in (pltpu.VMEM, pltpu.SMEM, pl.ANY))
    scratch = [pltpu.VMEM(shape, kind) for shape, kind in MAIN_SCRATCH.values()]
    scratch += [pltpu.VMEM(shape, kind) for shape, kind in SCRATCH.values()]
    scratch += [pltpu.VMEM(shape, kind) for shape, kind in WEIGHTS.values()]
    scratch += [pltpu.VMEM(shape, F32) for shape in ACC.values()]
    scratch += [pltpu.SemaphoreType.DMA((n,)) for n in (PHASES, PHASES, PHASES, 1, 13, 13, 2, 2, 7)]
    return pl.pallas_call(
        main_kernel,
        out_shape=[
            jax.ShapeDtypeStruct((32, L, D), BF),
            jax.ShapeDtypeStruct((TRAJ, D), BF),
            jax.ShapeDtypeStruct((2, CHIPS, 16, CW), BF),
            jax.ShapeDtypeStruct((SMALL, D), F32),
        ],
        in_specs=[an, vm, sm, sm, an] + [an if k in MATRICES else vm for k in RAW],
        out_specs=[an, an, vm, vm],
        scratch_shapes=scratch,
        compiler_params=pltpu.CompilerParams(vmem_limit_bytes=62 << 20, has_side_effects=True),
    )(outgoing, pown, oown, slot, up, *raw)


LAST = dict(time=64, **VECTORS)


def last_kernel(dec, genc, ag, small, dec_out, genc_out, proj, mix, exp, red, *rest):
    outs, (ga, dec_v, genc_v, sem_in, sem_out) = rest[:len(LAST)], rest[len(LAST):]
    moves = [(dec.at[pl.ds(i * 8, 8)], dec_v.at[pl.ds(i * 8, 8)], dec_out.at[pl.ds(i * 8, 8)]) for i in range(4)]
    moves += [(genc.at[pl.ds(i * 1024, 1024)], genc_v.at[pl.ds(i * 1024, 1024)], genc_out.at[pl.ds(i * 1024, 1024)]) for i in range(4)]
    copies_in = [pltpu.make_async_copy(a, b, sem_in.at[i]) for i, (a, b, _) in enumerate(moves)]
    copies_out = [pltpu.make_async_copy(b, c, sem_out.at[i]) for i, (_, b, c) in enumerate(moves)]
    for copy in copies_in:
        copy.start()
    for a, b in zip(copies_in, copies_out):
        a.wait()
        b.start()
    for r in range(16):
        for c in range(8):
            ga[r * 16:(r + 1) * 16, c * CW:(c + 1) * CW] = ag[c % 2, r * 4 + c // 2].astype(F32)
    proj[...] = ga[:, :3 * D]
    mix[...] = ga[:, 3 * D:4 * D]
    exp[...] = ga[:, 4 * D:8 * D]
    red[...] = ga[:, 8 * D:].T
    at = 0
    for out, rows in zip(outs, LAST.values()):
        if len(out.shape) == 1:
            for i in range(rows):
                out[pl.ds(i * D, D)] = small[at + i:at + i + 1, :].reshape(D)
        else:
            out[...] = small[at:at + rows, :]
        at += rows
    for copy in copies_out:
        copy.wait()


def last(dec, genc, ag, small):
    vm, an = (pl.BlockSpec(memory_space=m) for m in (pltpu.VMEM, pl.ANY))
    shapes = [((32, L, D), BF), ((TRAJ, D), BF), ((D, 3 * D), F32), ((D, D), F32), ((D, 4 * D), F32), ((4 * D, D), F32)]
    shapes += [((rows, D) if k in ("time", "offsets") else (rows * D,), F32) for k, rows in LAST.items()]
    return pl.pallas_call(
        last_kernel,
        out_shape=[jax.ShapeDtypeStruct(*s) for s in shapes],
        in_specs=[an, an, vm, vm],
        out_specs=[an, an] + [vm] * (len(shapes) - 2),
        scratch_shapes=[
            pltpu.VMEM((D, WIDE), F32), pltpu.VMEM((32, L, D), BF), pltpu.VMEM((TRAJ, D), BF),
            pltpu.SemaphoreType.DMA((8,)), pltpu.SemaphoreType.DMA((8,)),
        ],
        compiler_params=pltpu.CompilerParams(vmem_limit_bytes=62 << 20),
    )(dec, genc, ag, small)


def on_device(encoder_states, position_permutation, observed_tokens, decoder_slot, *rest):
    raw, sensitivity = rest[:-1], rest[-1]
    outgoing, pown, oown = prep(decoder_slot, observed_tokens, encoder_states.reshape(TRAJ, D), position_permutation)
    dec, genc, ag, small = main(outgoing, pown, oown, decoder_slot, sensitivity, raw)
    dec, genc, proj, mix, exp, red, *vectors = last(dec, genc, ag, small)
    v = dict(zip(LAST, vectors))
    return (
        dec, genc.reshape(TRAJ, 1, D), v["hidden"], v["time"], v["scale"], v["shift"], proj, v["offsets"], mix,
        v["recenter"], v["midnorm"], v["midshift"], exp, v["lift"], red, v["trail"],
    )


def solution(mesh):
    in_specs = (P(None, "dp", None),) + (P(),) * 17 + (P("dp", None, None),)
    out_specs = (P("dp", None, None), P(None, "dp", None)) + (P(),) * 14
    return jax.shard_map(on_device, mesh=mesh, in_specs=in_specs, out_specs=out_specs, check_vma=False)
```

```python
import functools
import math

import jax
import jax.numpy as jnp
from jax import lax
from jax.experimental import pallas as pl
from jax.experimental.pallas import tpu as pltpu
from jax.sharding import PartitionSpec as P

MESH = pl.DeviceIdType.MESH

F32 = jnp.float32
BF = jnp.bfloat16
EPSILON = 1e-05
G = 4
L = 128
D = 256
H = 4
R = G * L
D1 = D + 16


def nn(a, b):
    return lax.dot_general(a, b, (((1,), (0,)), ((), ())), preferred_element_type=F32)


def nt(a, b):
    return lax.dot_general(a, b, (((1,), (1,)), ((), ())), preferred_element_type=F32)


def tn(a, b):
    return lax.dot_general(a, b, (((0,), (0,)), ((), ())), preferred_element_type=F32)


def fold(x):
    return jnp.sum(x.reshape(x.shape[0] // 8, 8, x.shape[1]), axis=0)


def norm(x):
    c = x - jnp.mean(x, axis=-1, keepdims=True)
    inv = lax.rsqrt(jnp.mean(c * c, axis=-1, keepdims=True) + EPSILON)
    return c * inv, inv


def norm_back(up, n, inv, gain):
    e = up * gain
    return inv * (e - jnp.mean(e, axis=-1, keepdims=True) - n * jnp.mean(e * n, axis=-1, keepdims=True))


SHIFT = 3.87
POLY = (146.76783278249778, -48.81607899847526, 12.01133916341042, -0.5829371368710288, 0.036552147836326994)
CP = 1.0 / math.sqrt(2.0 * math.pi)
HALF_LOG2E = -0.5 / math.log(2.0)


def gelu_parts(h):
    t = pl.reciprocal(jnp.abs(h) + SHIFT, approx=True)
    e = jnp.exp2(h * h * HALF_LOG2E)
    q = POLY[0]
    for c in POLY[1:]:
        q = q * t + c
    q = q * e
    phi = jnp.where(h >= 0.0, 1.0 - q, q)
    return h * phi, phi + (CP * h) * e


def head_masks():
    lane = lax.broadcasted_iota(jnp.int32, (1, D), 1) // 64
    return [(lane == h).astype(F32).astype(BF) for h in range(H)]


def rows(t, n=1):
    return slice(t * L, (t + n) * L)


def wide2(m):
    return jnp.concatenate([m, m], axis=1)


def before(w, s, acc, io):
    masks = head_masks()
    for t in range(G):
        x = jnp.where(wide2(io.mask(t)) > 0.5, io.x(t), w.hidden[...]) + w.stamped[...]
        s.mid[rows(t), :] = x
        n, inv = norm(x)
        s.inv1[rows(t), :] = jnp.broadcast_to(inv, (L, L))
        s.n1[rows(t), :] = n
        s.first[rows(t), :] = (n * w.gain1[...] + w.shift1[...]).astype(BF)
        yield
    s.firstt[:D, :] = s.first[...].T
    s.upt[...] = io.up_all().T
    for c, ref in enumerate((s.q, s.k, s.v)):
        y = nn(s.first[...], w.qkv[:, c * D:(c + 1) * D]) + w.bqkv[:, c * D:(c + 1) * D]
        y = y.astype(BF)
        if c == 0:
            y = y * BF(0.125)
        ref[...] = y
        yield
    for t in range(G):
        q = s.q[rows(t), :]
        for h in range(H):
            s.qm[t, h * L:(h + 1) * L, :] = q * masks[h]
        st = nt(s.k[rows(t), :], s.qm[t])
        e = jnp.exp(st - jnp.max(st, axis=0, keepdims=True))
        p = e * (1.0 / jnp.sum(e, axis=0, keepdims=True))
        s.p[t] = p
        s.pb[t] = p.astype(BF)
        yield
    for t in range(G):
        vt = s.v[rows(t), :].T
        for h in range(H):
            o = nn(vt[h * 64:(h + 1) * 64, :], s.pb[t, :, h * L:(h + 1) * L])
            s.ot[h * 64:(h + 1) * 64, rows(t)] = o.astype(BF)
        s.o[rows(t), :] = s.ot[:D, rows(t)].T
        yield
    for t in range(0, G, 2):
        proj = nn(s.o[rows(t, 2), :], w.out[...])
        for i in range(2):
            mid = s.mid[rows(t + i), :] + proj[rows(i), :] + w.bout[...]
            s.mid[rows(t + i), :] = mid
            n, inv = norm(mid)
            s.inv2[rows(t + i), :] = jnp.broadcast_to(inv, (L, L))
            s.n2[rows(t + i), :] = n
            s.second[rows(t + i), :] = (n * w.gain2[...] + w.shift2[...]).astype(BF)
        yield
    s.sect[:D, :] = s.second[...].T
    yield


def feed(w, s, acc, io):
    for c in range(4):
        cols = slice(c * D, (c + 1) * D)
        for t in range(G):
            h = nn(s.second[rows(t), :], w.wide[:, cols]) + w.bwide[:, cols]
            ba = nt(io.up(t), w.narrow[cols, :])
            a, da = gelu_parts(h)
            s.act[rows(t), cols] = a.astype(BF)
            s.bh[rows(t), cols] = (ba * da).astype(BF)
            yield


def after(w, s, acc, io):
    masks = head_masks()
    for t in range(0, G, 2):
        dec = nn(s.act[rows(t, 2), :], w.narrow[...])
        for i in range(2):
            io.out(t + i, (s.mid[rows(t + i), :] + dec[rows(i), :] + w.bnarrow[...]).astype(BF))
        yield
        bsec = nt(s.bh[rows(t, 2), :], w.wide[...])
        for i in range(2):
            up = io.up(t + i).astype(F32)
            n, b = s.n2[rows(t + i), :], bsec[rows(i), :]
            acc.trail[...] += fold(up)
            acc.midnorm[...] += fold(b * n)
            acc.midshift[...] += fold(b)
            bm = up + norm_back(b, n, wide2(s.inv2[rows(t + i), :]), w.gain2[...])
            s.mid[rows(t + i), :] = bm
            s.branch[rows(t + i), :] = bm.astype(BF)
            yield
        s.do[rows(t, 2), :] = nt(s.branch[rows(t, 2), :], w.out[...]).astype(BF)
        yield
    for c in range(4):
        cols = slice(c * D, (c + 1) * D)
        acc.exp[:, cols] += nn(s.sect[...], s.bh[:, cols])
        yield
        acc.red[:, cols] += nn(s.upt[...], s.act[:, cols])
        yield
    for t in range(G):
        do = s.do[rows(t), :]
        for h in range(H):
            s.dom[t, h * L:(h + 1) * L, :] = do * masks[h]
        dp = nt(s.v[rows(t), :], s.dom[t])
        p = s.p[t]
        pd = p * dp
        ds = pd - p * jnp.sum(pd, axis=0, keepdims=True)
        s.ds[t] = ds.astype(BF)
        yield
    for t in range(G):
        s.bt[rows(t), 2 * D:] = nn(s.pb[t], s.dom[t]).astype(BF)
        yield
        s.bt[rows(t), D:2 * D] = nn(s.ds[t], s.qm[t]).astype(BF)
        yield
        kt = s.k[rows(t), :].T
        for h in range(H):
            dq = nn(kt[h * 64:(h + 1) * 64, :], s.ds[t, :, h * L:(h + 1) * L]) * 0.125
            s.dqt[t, h * 64:(h + 1) * 64, :] = dq.astype(BF)
        s.bt[rows(t), :D] = s.dqt[t].T
        yield
    acc.mix[...] += nn(s.ot[...], s.branch[...])
    yield
    for t in range(0, G, 2):
        bfirst = nt(s.bt[rows(t, 2), :], w.qkv[...])
        for i in range(2):
            n, b = s.n1[rows(t + i), :], bfirst[rows(i), :]
            acc.scale[...] += fold(b * n)
            acc.shift[...] += fold(b)
            bi = s.mid[rows(t + i), :] + norm_back(b, n, wide2(s.inv1[rows(t + i), :]), w.gain1[...])
            acc.time[...] += bi
            ret = jnp.where(wide2(io.mask(t + i)) > 0.5, bi, 0.0)
            acc.hidden[...] += fold(bi - ret)
            io.ret(t + i, ret)
            yield
    for c in range(3):
        cols = slice(c * D, (c + 1) * D)
        acc.proj[:, cols] += nn(s.firstt[...], s.bt[:, cols])
        yield


def chain(*parts):
    for part in parts:
        yield from part


def weave(one, other):
    one, other = list_pieces(one), list_pieces(other)
    total = max(one.count, other.count)
    for i in range(total):
        one.upto(-(-(i + 1) * one.count // total))
        other.upto(-(-(i + 1) * other.count // total))


class list_pieces:
    def __init__(self, make):
        self.steps, self.count, self.done = make[0](), make[1], 0

    def upto(self, n):
        while self.done < n:
            next(self.steps, None)
            self.done += 1
            if self.done == self.count:
                for _ in self.steps:
                    pass


BEFORE, FEED, AFTER = 18, 16, 47


class Bag:
    def __init__(self, **kw):
        self.__dict__.update(kw)


SCRATCH = dict(
    inv1=((R, L), F32), inv2=((R, L), F32), mid=((R, D), F32), n1=((R, D), F32), n2=((R, D), F32), first=((R, D), BF), second=((R, D), BF),
    q=((R, D), BF), k=((R, D), BF), v=((R, D), BF), qm=((G, H * L, D), BF), dom=((G, H * L, D), BF),
    p=((G, L, H * L), F32), pb=((G, L, H * L), BF), ds=((G, L, H * L), BF),
    ot=((D1, R), BF), sect=((D1, R), BF), firstt=((D1, R), BF), upt=((D, R), BF), o=((R, D), BF), dqt=((G, D, L), BF),
    act=((R, 4 * D), BF), bh=((R, 4 * D), BF), branch=((R, D), BF), do=((R, D), BF), bt=((R, 3 * D), BF),
)
ACC = dict(
    trail=(8, D), midnorm=(8, D), midshift=(8, D), scale=(8, D), shift=(8, D), hidden=(8, D), time=(L, D),
)
COLUMNS = dict(proj=(0, 3 * D), mix=(3 * D, D), exp=(4 * D, 4 * D), red=(8 * D, 4 * D))
WIDE = 12 * D
WEIGHTS = dict(
    hidden=((1, D), F32), stamped=((L, D), F32), gain1=((1, D), F32), shift1=((1, D), F32), qkv=((D, 3 * D), BF),
    bqkv=((1, 3 * D), F32), out=((D, D), BF), bout=((1, D), F32), gain2=((1, D), F32), shift2=((1, D), F32),
    wide=((D, 4 * D), BF), bwide=((1, 4 * D), F32), narrow=((4 * D, D), BF), bnarrow=((1, D), F32),
)


RAW = ("hidden", "stamped", "gain1", "shift1", "qkv", "bqkv", "out", "bout", "gain2", "shift2", "wide", "bwide", "narrow", "bnarrow")
MATRICES = ("qkv", "out", "wide", "narrow")


def spread(raw, w):
    for k in RAW:
        if k == "stamped":
            v = raw[k][...].astype(F32)
            w.stamped[...] = jnp.broadcast_to(v[:, None, :], (L // 2, 2, D)).reshape(L, D)
        elif k == "bqkv":
            v = raw[k][...].astype(F32)
            w.bqkv[:, :D] = v[:1]
            w.bqkv[:, D:2 * D] = jnp.zeros((1, D), F32)
            w.bqkv[:, 2 * D:] = v[1:]
        elif k not in MATRICES:
            v = raw[k][...].astype(F32)
            getattr(w, k)[...] = v.reshape(1, -1)


N = 128
PHASES = 4
EACH = 8
TRAJ = 4096
CHIPS = 64
CW = 384
VECTORS = dict(lift=4, trail=1, midnorm=1, midshift=1, recenter=1, offsets=2, scale=1, shift=1, hidden=1)
SMALL = 80
HALF = SMALL // 2


def prep_kernel(unroll, slot, enc, out, src, dst):
    x = enc[...].astype(F32)
    src[0] = x[:, :L]
    src[1] = x[:, L:]

    def block(i, _):
        js = [slot[i * unroll + u] for u in range(unroll)]
        vs = [[src[k, pl.ds(i * unroll + u, 1), :] for k in range(2)] for u in range(unroll)]
        for u in range(unroll):
            for k in range(2):
                dst[k, pl.ds(js[u], 1), :] = vs[u][k]
        return 0

    lax.fori_loop(0, TRAJ // unroll, block, 0)
    for g in range(4):
        at = pl.ds(g * 1024, 1024)
        y = jnp.concatenate([dst[0, at, :], dst[1, at, :]], axis=1)
        out[g * 32:(g + 1) * 32] = y.astype(BF).reshape(32, PHASES, EACH, D)


def prep(slot, enc):
    vm, sm = (pl.BlockSpec(memory_space=m) for m in (pltpu.VMEM, pltpu.SMEM))
    return pl.pallas_call(
        functools.partial(prep_kernel, 32),
        out_shape=jax.ShapeDtypeStruct((N, PHASES, EACH, D), BF),
        in_specs=[sm, vm],
        out_specs=vm,
        scratch_shapes=[pltpu.VMEM((2, TRAJ, L), F32), pltpu.VMEM((2, TRAJ, L), F32)],
        compiler_params=pltpu.CompilerParams(vmem_limit_bytes=56 << 20),
    )(slot, enc)


def others(me, step):
    cs = [me % 2, 1 - me % 2]
    xs = [(me // 2 + d) % 4 * 2 for d in range(4)]
    ys = [(me // 8 + d) % 4 * 8 for d in range(4)]
    zs = [(me // 32 + d) % 4 * 32 for d in range(4)]
    hops = lambda k: sum((0, 1, 2, 1)[k // unit % 4] for unit in (2, 8, 32))
    far_first = sorted(range(step, N, step), key=hops, reverse=True)
    return [zs[k // 32] + ys[k // 8 % 4] + xs[k // 2 % 4] + cs[k % 2] for k in far_first]


def remote(src, dst, send, recv, to):
    return pltpu.make_async_remote_copy(src, dst, send, recv, device_id=(to,), device_id_type=MESH)


def landed_all(ref, sem):
    pltpu.make_async_copy(ref, ref, sem).wait()


MAIN_SCRATCH = dict(
    recv=((PHASES, N, EACH, D), BF), ret=((PHASES, N, EACH, D), BF), land=((N, PHASES, EACH, D), BF),
    mask=((32, L, L), F32), x32=((2, N * EACH, L), F32), ret32=((2, N * EACH, L), F32),
    land32=((2, TRAJ, L), F32), out32=((2, TRAJ, L), F32), perm=((TRAJ, L), jnp.int32), hot=((32, TRAJ), BF),
    counts=((32, L), F32), order=((32, L), F32), ga=((D1, WIDE), F32),
    sib_send=((CHIPS, 16, CW), BF), sib_recv=((CHIPS, 16, CW), BF),
    rs_send=((CHIPS, 16, CW), BF), rs_recv=((CHIPS, 16, CW), BF), ag_send=((16, CW), BF),
    dec_v=((32, L, D), BF), genc_v=((TRAJ, D), BF), up=((32, L, D), BF),
    small=((SMALL, D), F32), small_sib=((HALF, D), F32), hop_send=((3, HALF, D), F32), hop=((3, 4, HALF, D), F32),
)


def main_kernel(*refs):
    outgoing, perm_hbm, obs, slots, slot, up_hbm = refs[:6]
    raw = dict(zip(RAW, refs[6:6 + len(RAW)]))
    refs = refs[6 + len(RAW):]
    dec, genc, ag, small_out = refs[:4]
    refs = refs[4:]
    m = Bag(**dict(zip(MAIN_SCRATCH, refs)))
    refs = refs[len(MAIN_SCRATCH):]
    pair = []
    for _ in range(2):
        pair.append(Bag(**dict(zip(SCRATCH, refs))))
        refs = refs[len(SCRATCH):]
    w = Bag(**dict(zip(WEIGHTS, refs)))
    refs = refs[len(WEIGHTS):]
    acc = Bag(**dict(zip(ACC, refs)))
    in_send, in_recv, out_send, out_recv, one_send, one_recv, rs_sem, ag_sem, local = refs[len(ACC):]
    for k, (at, width) in COLUMNS.items():
        setattr(acc, k, m.ga.at[pl.ds(0, D if k == "red" else D1), pl.ds(at, width)])
    me = lax.axis_index("dp")
    core, chip = me % 2, me // 2
    sibling = me + 1 - 2 * core

    def send_in(g):
        pltpu.make_async_copy(outgoing.at[me, g], m.recv.at[g, me], in_recv.at[g]).start()
        for to in others(me, 1):
            remote(outgoing.at[to, g], m.recv.at[g, me], in_send.at[g], in_recv.at[g], to).start()

    send_in(0)
    order_load = pltpu.make_async_copy(perm_hbm, m.perm, local.at[7])
    order_load.start()
    loads = [pltpu.make_async_copy(up_hbm, m.up, local.at[0])]
    loads += [pltpu.make_async_copy(raw[k], getattr(w, k), local.at[1 + i]) for i, k in enumerate(MATRICES)]
    for copy in loads:
        copy.start()
    spread(raw, w)
    for s in pair:
        for r in (s.ot, s.sect, s.firstt):
            r[D:, :] = jnp.ones((16, R), BF)

    mine = me * 32 + lax.broadcasted_iota(jnp.int32, (32, L), 0)
    counts = jnp.zeros((32, L), F32)
    for r in range(TRAJ // L):
        hot = (slots[r:r + 1, :] == mine).astype(F32)
        counts += hot * obs[r:r + 1, :].astype(F32)
        m.hot[:, r * L:(r + 1) * L] = hot.astype(BF)
    m.counts[...] = jnp.broadcast_to(jnp.sum(counts, axis=1, keepdims=True), (32, L))
    order_load.wait()
    m.order[...] = nn(m.hot[...], m.perm[...].astype(F32).astype(BF))

    def one_mask(j, _):
        place = lax.broadcasted_iota(jnp.int32, (L, L), 0).astype(F32)
        hot = (m.order[pl.ds(j, 1), :] == place).astype(F32).astype(BF)
        early = (place < m.counts[pl.ds(j, 1), :]).astype(F32).astype(BF)
        m.mask[j] = nn(hot, early)
        return 0

    lax.fori_loop(0, 32, one_mask, 0)
    for copy in loads:
        copy.wait()

    def io_of(g, half):
        base = g * EACH + half * G
        own = lambda t: pl.ds(half * G + t, L, stride=EACH)

        def out(t, v):
            m.dec_v[base + t] = v

        def ret(t, v):
            for i in range(2):
                m.ret32[i, own(t), :] = v[:, i * L:(i + 1) * L]

        return Bag(
            x=lambda t: jnp.concatenate([m.x32[i, own(t), :] for i in range(2)], axis=1),
            mask=lambda t: m.mask[base + t],
            up=lambda t: m.up[base + t],
            up_all=lambda: m.up[pl.ds(base, G)].reshape(R, D),
            out=out,
            ret=ret,
        )

    def forward(half, io):
        return lambda: chain(before(w, pair[half], acc, io), feed(w, pair[half], acc, io)), BEFORE + FEED

    def backward(half, io):
        return lambda: after(w, pair[half], acc, io), AFTER

    def send_out(g):
        m.ret[g] = jnp.concatenate([m.ret32[0], m.ret32[1]], axis=1).astype(BF).reshape(N, EACH, D)
        pltpu.make_async_copy(m.ret.at[g, me], m.land.at[me, g], out_recv.at[0]).start()
        for to in others(me, 1):
            remote(m.ret.at[g, to], m.land.at[me, g], out_send.at[g], out_recv.at[0], to).start()
        mine = pl.ds(g * EACH, EACH)
        pltpu.make_async_copy(m.dec_v.at[mine], dec.at[mine], local.at[5]).start()

    def phase(g, _):
        landed_all(m.recv.at[g], in_recv.at[g])

        @pl.when(g < PHASES - 1)
        def _():
            send_in(g + 1)

        a = m.recv[g].reshape(N * EACH, D).astype(F32)
        m.x32[0] = a[:, :L]
        m.x32[1] = a[:, L:]
        earlier = g - (g + PHASES - 1) // PHASES
        weave(forward(0, io_of(g, 0)), backward(1, io_of(earlier, 1)))

        @pl.when(g == 0)
        def _():
            m.ga[...] = jnp.zeros_like(m.ga)
            for k in ACC:
                r = getattr(acc, k)
                r[...] = jnp.zeros_like(r)

        @pl.when(g > 0)
        def _():
            send_out(g - 1)

        weave(forward(1, io_of(g, 1)), backward(0, io_of(g, 0)))
        return 0

    lax.fori_loop(0, PHASES, phase, 0)
    for _ in after(w, pair[1], acc, io_of(PHASES - 1, 1)):
        pass
    send_out(PHASES - 1)

    for r in range(16):
        for j in range(4):
            at = pl.multiple_of((2 * j + 1 - core) * CW, L)
            m.sib_send[r * 4 + j] = m.ga[r * 16:(r + 1) * 16, pl.ds(at, CW)].astype(BF)
    big_sib = remote(m.sib_send, m.sib_recv, one_send.at[0], one_recv.at[0], sibling)
    big_sib.start()
    t3 = acc.time[...].reshape(64, 2, D)
    m.small[:64] = t3[:, 0] + t3[:, 1]
    m.small[64:] = jnp.zeros((16, D), F32)
    at = 64
    for k, rows in VECTORS.items():
        if k == "lift":
            v = acc.exp[D:D + 1, :]
        elif k == "recenter":
            v = acc.mix[D:D + 1, :]
        elif k == "offsets":
            v = jnp.concatenate([acc.proj[D:D + 1, :D], acc.proj[D:D + 1, 2 * D:]], axis=1)
        else:
            v = jnp.sum(getattr(acc, k)[...], axis=0, keepdims=True)
        for i in range(rows):
            m.small[at:at + 1, :] = v[:, i * D:(i + 1) * D]
            at += 1
    mine = pl.ds(pl.multiple_of(core * HALF, 8), HALF)
    other = pl.ds(pl.multiple_of((1 - core) * HALF, 8), HALF)
    small_sib = remote(m.small.at[other], m.small_sib, one_send.at[1], one_recv.at[1], sibling)
    small_sib.start()
    small_sib.wait()
    value = m.small[mine, :] + m.small_sib[...]

    def hop_start(axis, value):
        unit = (2, 8, 32)[axis]
        here = (me // unit) % 4
        m.hop_send[axis] = value
        m.hop[axis, here] = value
        copies = []
        for d in (1, 3, 2):
            to = me + ((here + d) % 4 - here) * unit
            c = remote(m.hop_send.at[axis], m.hop.at[axis, here], one_send.at[2 + 3 * axis + d - 1], one_recv.at[2 + 3 * axis + d - 1], to)
            c.start()
            copies.append(c)
        return copies

    def hop_end(axis, copies):
        for c in copies:
            c.wait()
        return (m.hop[axis, 0] + m.hop[axis, 1]) + (m.hop[axis, 2] + m.hop[axis, 3])

    copies = hop_start(0, value)
    big_sib.wait()
    for r in range(16):
        for j in range(4):
            at = pl.multiple_of((2 * j + core) * CW, L)
            v = m.ga[r * 16:(r + 1) * 16, pl.ds(at, CW)] + m.sib_recv[r * 4 + j].astype(F32)
            m.rs_send[r * 4 + j] = v.astype(BF)
    pltpu.make_async_copy(m.rs_send.at[chip], m.rs_recv.at[chip], rs_sem.at[1]).start()
    for to in others(me, 2):
        remote(m.rs_send.at[to // 2], m.rs_recv.at[chip], rs_sem.at[0], rs_sem.at[1], to).start()
    value = hop_end(0, copies)
    copies = hop_start(1, value)

    landed_all(m.land, out_recv.at[0])
    for g in range(4):
        a = m.land[g * 32:(g + 1) * 32].reshape(1024, D).astype(F32)
        m.land32[0, g * 1024:(g + 1) * 1024] = a[:, :L]
        m.land32[1, g * 1024:(g + 1) * 1024] = a[:, L:]
    value = hop_end(1, copies)
    copies = hop_start(2, value)
    landed_all(m.rs_recv, rs_sem.at[1])
    m.ag_send[...] = jnp.sum(m.rs_recv[...].astype(F32), axis=0).astype(BF)
    pltpu.make_async_copy(m.ag_send, ag.at[core, chip], ag_sem.at[1]).start()
    for to in others(me, 2):
        remote(m.ag_send, ag.at[core, chip], ag_sem.at[0], ag_sem.at[1], to).start()
    value = hop_end(2, copies)
    small_out[mine, :] = value
    small_last = remote(small_out.at[mine], small_out.at[mine], one_send.at[11], one_recv.at[11], sibling)
    small_last.start()

    def gather(i, _):
        js = [slot[i * 32 + u] for u in range(32)]
        vs = [[m.land32[k, pl.ds(j, 1), :] for k in range(2)] for j in js]
        for u in range(32):
            for k in range(2):
                m.out32[k, pl.ds(i * 32 + u, 1), :] = vs[u][k]
        return 0

    lax.fori_loop(0, TRAJ // 32, gather, 0)
    m.genc_v[...] = jnp.concatenate([m.out32[0], m.out32[1]], axis=1).astype(BF)
    genc_copy = pltpu.make_async_copy(m.genc_v, genc, local.at[6])
    genc_copy.start()
    landed_all(ag.at[core], ag_sem.at[1])
    big_last = remote(ag.at[core], ag.at[core], one_send.at[12], one_recv.at[12], sibling)
    big_last.start()
    small_last.wait()
    genc_copy.wait()
    landed_all(m.dec_v, local.at[5])
    for g in range(PHASES):
        landed_all(m.recv.at[g, pl.ds(0, N - 1)], in_send.at[g])
        landed_all(m.ret.at[g, pl.ds(0, N - 1)], out_send.at[g])
    landed_all(m.rs_send.at[pl.ds(0, CHIPS - 1)], rs_sem.at[0])
    landed_all(m.rs_send.at[pl.ds(0, CHIPS - 1)], ag_sem.at[0])
    big_last.wait()


def main(outgoing, perm, obs, slot, up, raw):
    vm, sm, an = (pl.BlockSpec(memory_space=m) for m in (pltpu.VMEM, pltpu.SMEM, pl.ANY))
    scratch = [pltpu.VMEM(shape, kind) for shape, kind in MAIN_SCRATCH.values()]
    scratch += [pltpu.VMEM(shape, kind) for shape, kind in SCRATCH.values()] * 2
    scratch += [pltpu.VMEM(shape, kind) for shape, kind in WEIGHTS.values()]
    scratch += [pltpu.VMEM(shape, F32) for shape in ACC.values()]
    scratch += [pltpu.SemaphoreType.DMA((n,)) for n in (PHASES, PHASES, PHASES, 1, 13, 13, 2, 2, 8)]
    return pl.pallas_call(
        main_kernel,
        out_shape=[
            jax.ShapeDtypeStruct((32, L, D), BF),
            jax.ShapeDtypeStruct((TRAJ, D), BF),
            jax.ShapeDtypeStruct((2, CHIPS, 16, CW), BF),
            jax.ShapeDtypeStruct((SMALL, D), F32),
        ],
        in_specs=[an, an, vm, vm, sm, an] + [an if k in MATRICES else vm for k in RAW],
        out_specs=[an, an, vm, vm],
        scratch_shapes=scratch,
        compiler_params=pltpu.CompilerParams(vmem_limit_bytes=62 << 20, has_side_effects=True),
    )(outgoing, perm, obs.reshape(32, L), slot.reshape(32, L), slot, up, *raw)


LAST = dict(time=64, **VECTORS)


def last_kernel(dec, genc, ag, small, dec_out, genc_out, proj, mix, exp, red, *rest):
    outs, (ga, dec_v, genc_v, sem_in, sem_out) = rest[:len(LAST)], rest[len(LAST):]
    moves = [(dec.at[pl.ds(i * 8, 8)], dec_v.at[pl.ds(i * 8, 8)], dec_out.at[pl.ds(i * 8, 8)]) for i in range(4)]
    moves += [(genc.at[pl.ds(i * 1024, 1024)], genc_v.at[pl.ds(i * 1024, 1024)], genc_out.at[pl.ds(i * 1024, 1024)]) for i in range(4)]
    copies_in = [pltpu.make_async_copy(a, b, sem_in.at[i]) for i, (a, b, _) in enumerate(moves)]
    copies_out = [pltpu.make_async_copy(b, c, sem_out.at[i]) for i, (_, b, c) in enumerate(moves)]
    for copy in copies_in:
        copy.start()
    for a, b in zip(copies_in, copies_out):
        a.wait()
        b.start()
    for r in range(16):
        for c in range(8):
            ga[r * 16:(r + 1) * 16, c * CW:(c + 1) * CW] = ag[c % 2, r * 4 + c // 2].astype(F32)
    proj[...] = ga[:, :3 * D]
    mix[...] = ga[:, 3 * D:4 * D]
    exp[...] = ga[:, 4 * D:8 * D]
    red[...] = ga[:, 8 * D:].T
    at = 0
    for out, rows in zip(outs, LAST.values()):
        if len(out.shape) == 1:
            for i in range(rows):
                out[pl.ds(i * D, D)] = small[at + i:at + i + 1, :].reshape(D)
        else:
            out[...] = small[at:at + rows, :]
        at += rows
    for copy in copies_out:
        copy.wait()


def last(dec, genc, ag, small):
    vm, an = (pl.BlockSpec(memory_space=m) for m in (pltpu.VMEM, pl.ANY))
    shapes = [((32, L, D), BF), ((TRAJ, D), BF), ((D, 3 * D), F32), ((D, D), F32), ((D, 4 * D), F32), ((4 * D, D), F32)]
    shapes += [((rows, D) if k in ("time", "offsets") else (rows * D,), F32) for k, rows in LAST.items()]
    return pl.pallas_call(
        last_kernel,
        out_shape=[jax.ShapeDtypeStruct(*s) for s in shapes],
        in_specs=[an, an, vm, vm],
        out_specs=[an, an] + [vm] * (len(shapes) - 2),
        scratch_shapes=[
            pltpu.VMEM((D, WIDE), F32), pltpu.VMEM((32, L, D), BF), pltpu.VMEM((TRAJ, D), BF),
            pltpu.SemaphoreType.DMA((8,)), pltpu.SemaphoreType.DMA((8,)),
        ],
        compiler_params=pltpu.CompilerParams(vmem_limit_bytes=62 << 20),
    )(dec, genc, ag, small)


def on_device(encoder_states, position_permutation, observed_tokens, decoder_slot, *rest):
    raw, sensitivity = rest[:-1], rest[-1]
    outgoing = prep(decoder_slot, encoder_states.reshape(TRAJ, D))
    dec, genc, ag, small = main(outgoing, position_permutation, observed_tokens, decoder_slot, sensitivity, raw)
    dec, genc, proj, mix, exp, red, *vectors = last(dec, genc, ag, small)
    v = dict(zip(LAST, vectors))
    return (
        dec, genc.reshape(TRAJ, 1, D), v["hidden"], v["time"], v["scale"], v["shift"], proj, v["offsets"], mix,
        v["recenter"], v["midnorm"], v["midshift"], exp, v["lift"], red, v["trail"],
    )


def solution(mesh):
    in_specs = (P(None, "dp", None),) + (P(),) * 17 + (P("dp", None, None),)
    out_specs = (P("dp", None, None), P(None, "dp", None)) + (P(),) * 14
    return jax.shard_map(on_device, mesh=mesh, in_specs=in_specs, out_specs=out_specs, check_vma=False)
```

```python
import functools
import math

import jax
import jax.numpy as jnp
from jax import lax
from jax.experimental import pallas as pl
from jax.experimental.pallas import tpu as pltpu
from jax.sharding import PartitionSpec as P

MESH = pl.DeviceIdType.MESH

F32 = jnp.float32
BF = jnp.bfloat16
EPSILON = 1e-05
G = 4
L = 128
D = 256
H = 4
R = G * L
D1 = D + 16


def nn(a, b):
    return lax.dot_general(a, b, (((1,), (0,)), ((), ())), preferred_element_type=F32)


def nt(a, b):
    return lax.dot_general(a, b, (((1,), (1,)), ((), ())), preferred_element_type=F32)


def tn(a, b):
    return lax.dot_general(a, b, (((0,), (0,)), ((), ())), preferred_element_type=F32)


def fold(x):
    return jnp.sum(x.reshape(x.shape[0] // 8, 8, x.shape[1]), axis=0)


def norm(x):
    c = x - jnp.mean(x, axis=-1, keepdims=True)
    inv = lax.rsqrt(jnp.mean(c * c, axis=-1, keepdims=True) + EPSILON)
    return c * inv, inv


def norm_back(up, n, inv, gain):
    e = up * gain
    return inv * (e - jnp.mean(e, axis=-1, keepdims=True) - n * jnp.mean(e * n, axis=-1, keepdims=True))


SHIFT = 3.87
POLY = (146.76783278249778, -48.81607899847526, 12.01133916341042, -0.5829371368710288, 0.036552147836326994)
CP = 1.0 / math.sqrt(2.0 * math.pi)
HALF_LOG2E = -0.5 / math.log(2.0)


def gelu_parts(h):
    t = pl.reciprocal(jnp.abs(h) + SHIFT, approx=True)
    e = jnp.exp2(h * h * HALF_LOG2E)
    q = POLY[0]
    for c in POLY[1:]:
        q = q * t + c
    q = q * e
    phi = jnp.where(h >= 0.0, 1.0 - q, q)
    return h * phi, phi + (CP * h) * e


def head_masks():
    lane = lax.broadcasted_iota(jnp.int32, (1, D), 1) // 64
    return [(lane == h).astype(F32).astype(BF) for h in range(H)]


def rows(t, n=1):
    return slice(t * L, (t + n) * L)


def wide2(m):
    return jnp.concatenate([m, m], axis=1)


def before(w, s, acc, io):
    masks = head_masks()
    for t in range(G):
        x = jnp.where(wide2(io.mask(t)) > 0.5, io.x(t), w.hidden[...]) + w.stamped[...]
        s.mid[rows(t), :] = x
        n, inv = norm(x)
        s.inv1[rows(t), :] = jnp.broadcast_to(inv, (L, L))
        s.n1[rows(t), :] = n
        s.first[rows(t), :] = (n * w.gain1[...] + w.shift1[...]).astype(BF)
        yield
    s.firstt[:D, :] = s.first[...].T
    s.upt[...] = io.up_all().T
    for c, ref in enumerate((s.q, s.k, s.v)):
        y = nn(s.first[...], w.qkv[:, c * D:(c + 1) * D]) + w.bqkv[:, c * D:(c + 1) * D]
        y = y.astype(BF)
        if c == 0:
            y = y * BF(0.125)
        ref[...] = y
        yield
    for t in range(G):
        q = s.q[rows(t), :]
        for h in range(H):
            s.qm[t, h * L:(h + 1) * L, :] = q * masks[h]
        st = nt(s.k[rows(t), :], s.qm[t])
        e = jnp.exp(st - jnp.max(st, axis=0, keepdims=True))
        p = e * (1.0 / jnp.sum(e, axis=0, keepdims=True))
        s.p[t] = p
        s.pb[t] = p.astype(BF)
        yield
    for t in range(G):
        vt = s.v[rows(t), :].T
        for h in range(H):
            o = nn(vt[h * 64:(h + 1) * 64, :], s.pb[t, :, h * L:(h + 1) * L])
            s.ot[h * 64:(h + 1) * 64, rows(t)] = o.astype(BF)
        s.o[rows(t), :] = s.ot[:D, rows(t)].T
        yield
    for t in range(0, G, 2):
        proj = nn(s.o[rows(t, 2), :], w.out[...])
        for i in range(2):
            mid = s.mid[rows(t + i), :] + proj[rows(i), :] + w.bout[...]
            s.mid[rows(t + i), :] = mid
            n, inv = norm(mid)
            s.inv2[rows(t + i), :] = jnp.broadcast_to(inv, (L, L))
            s.n2[rows(t + i), :] = n
            s.second[rows(t + i), :] = (n * w.gain2[...] + w.shift2[...]).astype(BF)
        yield
    s.sect[:D, :] = s.second[...].T
    yield


def feed(w, s, acc, io):
    for c in range(4):
        cols = slice(c * D, (c + 1) * D)
        for t in range(G):
            h = nn(s.second[rows(t), :], w.wide[:, cols]) + w.bwide[:, cols]
            ba = nt(io.up(t), w.narrow[cols, :])
            a, da = gelu_parts(h)
            s.act[rows(t), cols] = a.astype(BF)
            s.bh[rows(t), cols] = (ba * da).astype(BF)
            yield


def after(w, s, acc, io):
    masks = head_masks()
    for t in range(0, G, 2):
        dec = nn(s.act[rows(t, 2), :], w.narrow[...])
        for i in range(2):
            io.out(t + i, (s.mid[rows(t + i), :] + dec[rows(i), :] + w.bnarrow[...]).astype(BF))
        yield
        bsec = nt(s.bh[rows(t, 2), :], w.wide[...])
        for i in range(2):
            up = io.up(t + i).astype(F32)
            n, b = s.n2[rows(t + i), :], bsec[rows(i), :]
            acc.trail[...] += fold(up)
            acc.midnorm[...] += fold(b * n)
            acc.midshift[...] += fold(b)
            bm = up + norm_back(b, n, wide2(s.inv2[rows(t + i), :]), w.gain2[...])
            s.mid[rows(t + i), :] = bm
            s.branch[rows(t + i), :] = bm.astype(BF)
            yield
        s.do[rows(t, 2), :] = nt(s.branch[rows(t, 2), :], w.out[...]).astype(BF)
        yield
    for c in range(4):
        cols = slice(c * D, (c + 1) * D)
        acc.exp[:, cols] += nn(s.sect[...], s.bh[:, cols])
        yield
        acc.red[:, cols] += nn(s.upt[...], s.act[:, cols])
        yield
    for t in range(G):
        do = s.do[rows(t), :]
        for h in range(H):
            s.dom[t, h * L:(h + 1) * L, :] = do * masks[h]
        dp = nt(s.v[rows(t), :], s.dom[t])
        p = s.p[t]
        pd = p * dp
        ds = pd - p * jnp.sum(pd, axis=0, keepdims=True)
        s.ds[t] = ds.astype(BF)
        yield
    for t in range(G):
        s.bt[rows(t), 2 * D:] = nn(s.pb[t], s.dom[t]).astype(BF)
        yield
        s.bt[rows(t), D:2 * D] = nn(s.ds[t], s.qm[t]).astype(BF)
        yield
        kt = s.k[rows(t), :].T
        for h in range(H):
            dq = nn(kt[h * 64:(h + 1) * 64, :], s.ds[t, :, h * L:(h + 1) * L]) * 0.125
            s.dqt[t, h * 64:(h + 1) * 64, :] = dq.astype(BF)
        s.bt[rows(t), :D] = s.dqt[t].T
        yield
    acc.mix[...] += nn(s.ot[...], s.branch[...])
    yield
    for t in range(0, G, 2):
        bfirst = nt(s.bt[rows(t, 2), :], w.qkv[...])
        for i in range(2):
            n, b = s.n1[rows(t + i), :], bfirst[rows(i), :]
            acc.scale[...] += fold(b * n)
            acc.shift[...] += fold(b)
            bi = s.mid[rows(t + i), :] + norm_back(b, n, wide2(s.inv1[rows(t + i), :]), w.gain1[...])
            acc.time[...] += bi
            ret = jnp.where(wide2(io.mask(t + i)) > 0.5, bi, 0.0)
            acc.hidden[...] += fold(bi - ret)
            io.ret(t + i, ret)
            yield
    for c in range(3):
        cols = slice(c * D, (c + 1) * D)
        acc.proj[:, cols] += nn(s.firstt[...], s.bt[:, cols])
        yield


def chain(*parts):
    for part in parts:
        yield from part


def weave(one, other):
    one, other = list_pieces(one), list_pieces(other)
    total = max(one.count, other.count)
    for i in range(total):
        one.upto(-(-(i + 1) * one.count // total))
        other.upto(-(-(i + 1) * other.count // total))


class list_pieces:
    def __init__(self, make):
        self.steps, self.count, self.done = make[0](), make[1], 0

    def upto(self, n):
        while self.done < n:
            next(self.steps, None)
            self.done += 1
            if self.done == self.count:
                for _ in self.steps:
                    pass


BEFORE, FEED, AFTER = 18, 16, 47


class Bag:
    def __init__(self, **kw):
        self.__dict__.update(kw)


SCRATCH = dict(
    inv1=((R, L), F32), inv2=((R, L), F32), mid=((R, D), F32), n1=((R, D), F32), n2=((R, D), F32), first=((R, D), BF), second=((R, D), BF),
    q=((R, D), BF), k=((R, D), BF), v=((R, D), BF), qm=((G, H * L, D), BF), dom=((G, H * L, D), BF),
    p=((G, L, H * L), F32), pb=((G, L, H * L), BF), ds=((G, L, H * L), BF),
    ot=((D1, R), BF), sect=((D1, R), BF), firstt=((D1, R), BF), upt=((D, R), BF), o=((R, D), BF), dqt=((G, D, L), BF),
    act=((R, 4 * D), BF), bh=((R, 4 * D), BF), branch=((R, D), BF), do=((R, D), BF), bt=((R, 3 * D), BF),
)
ACC = dict(
    trail=(8, D), midnorm=(8, D), midshift=(8, D), scale=(8, D), shift=(8, D), hidden=(8, D), time=(L, D),
)
COLUMNS = dict(proj=(0, 3 * D), mix=(3 * D, D), exp=(4 * D, 4 * D), red=(8 * D, 4 * D))
WIDE = 12 * D
WEIGHTS = dict(
    hidden=((1, D), F32), stamped=((L, D), F32), gain1=((1, D), F32), shift1=((1, D), F32), qkv=((D, 3 * D), BF),
    bqkv=((1, 3 * D), F32), out=((D, D), BF), bout=((1, D), F32), gain2=((1, D), F32), shift2=((1, D), F32),
    wide=((D, 4 * D), BF), bwide=((1, 4 * D), F32), narrow=((4 * D, D), BF), bnarrow=((1, D), F32),
)


RAW = ("hidden", "stamped", "gain1", "shift1", "qkv", "bqkv", "out", "bout", "gain2", "shift2", "wide", "bwide", "narrow", "bnarrow")
MATRICES = ("qkv", "out", "wide", "narrow")


def spread(raw, w):
    for k in RAW:
        if k == "stamped":
            v = raw[k][...].astype(F32)
            w.stamped[...] = jnp.broadcast_to(v[:, None, :], (L // 2, 2, D)).reshape(L, D)
        elif k == "bqkv":
            v = raw[k][...].astype(F32)
            w.bqkv[:, :D] = v[:1]
            w.bqkv[:, D:2 * D] = jnp.zeros((1, D), F32)
            w.bqkv[:, 2 * D:] = v[1:]
        elif k not in MATRICES:
            v = raw[k][...].astype(F32)
            getattr(w, k)[...] = v.reshape(1, -1)


N = 128
PHASES = 4
EACH = 8
TRAJ = 4096
CW = 384
VECTORS = dict(lift=4, trail=1, midnorm=1, midshift=1, recenter=1, offsets=2, scale=1, shift=1, hidden=1)
SMALL = 80
HALF = SMALL // 2


def prep_kernel(unroll, slot, enc, out, src, dst):
    x = enc[...].astype(F32)
    src[0] = x[:, :L]
    src[1] = x[:, L:]

    def block(i, _):
        js = [slot[i * unroll + u] for u in range(unroll)]
        vs = [[src[k, pl.ds(i * unroll + u, 1), :] for k in range(2)] for u in range(unroll)]
        for u in range(unroll):
            for k in range(2):
                dst[k, pl.ds(js[u], 1), :] = vs[u][k]
        return 0

    lax.fori_loop(0, TRAJ // unroll, block, 0)
    for g in range(4):
        at = pl.ds(g * 1024, 1024)
        y = jnp.concatenate([dst[0, at, :], dst[1, at, :]], axis=1)
        out[g * 32:(g + 1) * 32] = y.astype(BF).reshape(32, PHASES, EACH, D)


def prep(slot, enc):
    vm, sm = (pl.BlockSpec(memory_space=m) for m in (pltpu.VMEM, pltpu.SMEM))
    return pl.pallas_call(
        functools.partial(prep_kernel, 32),
        out_shape=jax.ShapeDtypeStruct((N, PHASES, EACH, D), BF),
        in_specs=[sm, vm],
        out_specs=vm,
        scratch_shapes=[pltpu.VMEM((2, TRAJ, L), F32), pltpu.VMEM((2, TRAJ, L), F32)],
        compiler_params=pltpu.CompilerParams(vmem_limit_bytes=56 << 20),
    )(slot, enc)


def others(me):
    cs = [me % 2, 1 - me % 2]
    xs = [(me // 2 + d) % 4 * 2 for d in range(4)]
    ys = [(me // 8 + d) % 4 * 8 for d in range(4)]
    zs = [(me // 32 + d) % 4 * 32 for d in range(4)]
    hops = lambda k: sum((0, 1, 2, 1)[k // unit % 4] for unit in (2, 8, 32))
    far_first = sorted(range(1, N), key=hops, reverse=True)
    return [zs[k // 32] + ys[k // 8 % 4] + xs[k // 2 % 4] + cs[k % 2] for k in far_first]


def remote(src, dst, send, recv, to):
    return pltpu.make_async_remote_copy(src, dst, send, recv, device_id=(to,), device_id_type=MESH)


def landed_all(ref, sem):
    pltpu.make_async_copy(ref, ref, sem).wait()


MAIN_SCRATCH = dict(
    recv=((PHASES, N, EACH, D), BF), ret=((PHASES, N, EACH, D), BF), land=((N, PHASES, EACH, D), BF),
    mask=((32, L, L), F32), x32=((2, N * EACH, L), F32), ret32=((2, N * EACH, L), F32),
    land32=((2, TRAJ, L), F32), out32=((2, TRAJ, L), F32), perm=((TRAJ, L), jnp.int32), hot=((32, TRAJ), BF),
    counts=((32, L), F32), order=((32, L), F32), ga=((D1, WIDE), F32),
    sib_send=((3, 4, 4, 4, 16, L), BF), sib_recv=((3, 4, 4, 4, 16, L), BF), part0=((3, 4, 4, 4, 16, L), BF),
    came0=((3, 4, 4, 4, 16, L), BF), part1=((3, 4, 4, 16, L), BF), came1=((3, 4, 4, 16, L), BF), part2=((3, 4, 16, L), BF),
    came2=((3, 4, 16, L), BF), sum0=((3, 16, L), BF), sum1=((3, 4, 16, L), BF), sum2=((3, 4, 4, 16, L), BF),
    dec_v=((32, L, D), BF), genc_v=((TRAJ, D), BF), up=((32, L, D), BF),
    small=((SMALL, D), F32), small_sib=((HALF, D), F32), hop_send=((3, HALF, D), F32), hop=((3, 4, HALF, D), F32),
)


def main_kernel(*refs):
    outgoing, perm_hbm, obs, slots, slot, up_hbm = refs[:6]
    raw = dict(zip(RAW, refs[6:6 + len(RAW)]))
    refs = refs[6 + len(RAW):]
    dec, genc, ag, small_out = refs[:4]
    refs = refs[4:]
    m = Bag(**dict(zip(MAIN_SCRATCH, refs)))
    refs = refs[len(MAIN_SCRATCH):]
    pair = []
    for _ in range(2):
        pair.append(Bag(**dict(zip(SCRATCH, refs))))
        refs = refs[len(SCRATCH):]
    w = Bag(**dict(zip(WEIGHTS, refs)))
    refs = refs[len(WEIGHTS):]
    acc = Bag(**dict(zip(ACC, refs)))
    in_send, in_recv, out_send, out_recv, one_send, one_recv, hop_sent, hop_came, local = refs[len(ACC):]
    for k, (at, width) in COLUMNS.items():
        setattr(acc, k, m.ga.at[pl.ds(0, D if k == "red" else D1), pl.ds(at, width)])
    me = lax.axis_index("dp")
    core = me % 2
    sibling = me + 1 - 2 * core

    def send_in(g):
        pltpu.make_async_copy(outgoing.at[me, g], m.recv.at[g, me], in_recv.at[g]).start()
        for to in others(me):
            remote(outgoing.at[to, g], m.recv.at[g, me], in_send.at[g], in_recv.at[g], to).start()

    send_in(0)
    order_load = pltpu.make_async_copy(perm_hbm, m.perm, local.at[7])
    order_load.start()
    loads = [pltpu.make_async_copy(up_hbm, m.up, local.at[0])]
    loads += [pltpu.make_async_copy(raw[k], getattr(w, k), local.at[1 + i]) for i, k in enumerate(MATRICES)]
    for copy in loads:
        copy.start()
    spread(raw, w)
    for s in pair:
        for r in (s.ot, s.sect, s.firstt):
            r[D:, :] = jnp.ones((16, R), BF)

    mine = me * 32 + lax.broadcasted_iota(jnp.int32, (32, L), 0)
    counts = jnp.zeros((32, L), F32)
    for r in range(TRAJ // L):
        hot = (slots[r:r + 1, :] == mine).astype(F32)
        counts += hot * obs[r:r + 1, :].astype(F32)
        m.hot[:, r * L:(r + 1) * L] = hot.astype(BF)
    m.counts[...] = jnp.broadcast_to(jnp.sum(counts, axis=1, keepdims=True), (32, L))
    order_load.wait()
    m.order[...] = nn(m.hot[...], m.perm[...].astype(F32).astype(BF))

    def one_mask(j, _):
        place = lax.broadcasted_iota(jnp.int32, (L, L), 0).astype(F32)
        hot = (m.order[pl.ds(j, 1), :] == place).astype(F32).astype(BF)
        early = (place < m.counts[pl.ds(j, 1), :]).astype(F32).astype(BF)
        m.mask[j] = nn(hot, early)
        return 0

    lax.fori_loop(0, 32, one_mask, 0)
    for copy in loads:
        copy.wait()

    def io_of(g, half):
        base = g * EACH + half * G
        own = lambda t: pl.ds(half * G + t, L, stride=EACH)

        def out(t, v):
            m.dec_v[base + t] = v

        def ret(t, v):
            for i in range(2):
                m.ret32[i, own(t), :] = v[:, i * L:(i + 1) * L]

        return Bag(
            x=lambda t: jnp.concatenate([m.x32[i, own(t), :] for i in range(2)], axis=1),
            mask=lambda t: m.mask[base + t],
            up=lambda t: m.up[base + t],
            up_all=lambda: m.up[pl.ds(base, G)].reshape(R, D),
            out=out,
            ret=ret,
        )

    def forward(half, io):
        return lambda: chain(before(w, pair[half], acc, io), feed(w, pair[half], acc, io)), BEFORE + FEED

    def backward(half, io):
        return lambda: after(w, pair[half], acc, io), AFTER

    def send_out(g):
        m.ret[g] = jnp.concatenate([m.ret32[0], m.ret32[1]], axis=1).astype(BF).reshape(N, EACH, D)
        pltpu.make_async_copy(m.ret.at[g, me], m.land.at[me, g], out_recv.at[0]).start()
        for to in others(me):
            remote(m.ret.at[g, to], m.land.at[me, g], out_send.at[g], out_recv.at[0], to).start()
        mine = pl.ds(g * EACH, EACH)
        pltpu.make_async_copy(m.dec_v.at[mine], dec.at[mine], local.at[5]).start()

    def phase(g, _):
        landed_all(m.recv.at[g], in_recv.at[g])

        @pl.when(g < PHASES - 1)
        def _():
            send_in(g + 1)

        a = m.recv[g].reshape(N * EACH, D).astype(F32)
        m.x32[0] = a[:, :L]
        m.x32[1] = a[:, L:]
        earlier = g - (g + PHASES - 1) // PHASES
        weave(forward(0, io_of(g, 0)), backward(1, io_of(earlier, 1)))

        @pl.when(g == 0)
        def _():
            m.ga[...] = jnp.zeros_like(m.ga)
            for k in ACC:
                r = getattr(acc, k)
                r[...] = jnp.zeros_like(r)

        @pl.when(g > 0)
        def _():
            send_out(g - 1)

        weave(forward(1, io_of(g, 1)), backward(0, io_of(g, 0)))
        return 0

    lax.fori_loop(0, PHASES, phase, 0)
    for _ in after(w, pair[1], acc, io_of(PHASES - 1, 1)):
        pass
    send_out(PHASES - 1)

    units = (2, 8, 32)
    place = [(me // unit) % 4 for unit in units]

    def at_chip(j, r, x):
        coordinate = (x, r % 4, r // 4)
        return tuple(coordinate[(j + i) % 3] for i in range(3))

    def chunks(of_core):
        for r in range(16):
            for x in range(4):
                at = pl.multiple_of((2 * x + of_core) * CW, L)
                yield r, x, m.ga[r * 16:(r + 1) * 16, pl.ds(at, CW)]

    for r, x, v in chunks(1 - core):
        v = v.astype(BF)
        for j in range(3):
            m.sib_send[(j, *at_chip(j, r, x))] = v[:, j * L:(j + 1) * L]
    big_sib = remote(m.sib_send, m.sib_recv, one_send.at[0], one_recv.at[0], sibling)
    big_sib.start()
    t3 = acc.time[...].reshape(64, 2, D)
    m.small[:64] = t3[:, 0] + t3[:, 1]
    m.small[64:] = jnp.zeros((16, D), F32)
    at = 64
    for k, count in VECTORS.items():
        if k == "lift":
            v = acc.exp[D:D + 1, :]
        elif k == "recenter":
            v = acc.mix[D:D + 1, :]
        elif k == "offsets":
            v = jnp.concatenate([acc.proj[D:D + 1, :D], acc.proj[D:D + 1, 2 * D:]], axis=1)
        else:
            v = jnp.sum(getattr(acc, k)[...], axis=0, keepdims=True)
        for i in range(count):
            m.small[at:at + 1, :] = v[:, i * D:(i + 1) * D]
            at += 1
    mine = pl.ds(pl.multiple_of(core * HALF, 8), HALF)
    other = pl.ds(pl.multiple_of((1 - core) * HALF, 8), HALF)
    small_sib = remote(m.small.at[other], m.small_sib, one_send.at[1], one_recv.at[1], sibling)
    small_sib.start()

    def peers(axis):
        for d in (2, 1, 3):
            there = (place[axis] + d) % 4
            yield d - 1, there, me + (there - place[axis]) * units[axis]

    def small_hop(axis, value):
        m.hop_send[axis] = value
        m.hop[axis, place[axis]] = value
        copies = []
        for i, there, to in peers(axis):
            n = 2 + 3 * axis + i
            copies.append(remote(m.hop_send.at[axis], m.hop.at[axis, place[axis]], one_send.at[n], one_recv.at[n], to))
        return copies

    def small_sum(axis):
        return (m.hop[axis, 0] + m.hop[axis, 1]) + (m.hop[axis, 2] + m.hop[axis, 3])

    def hop(step, parts, arrive):
        copies = []
        axis_of = lambda j: (j + (step if step < 3 else 5 - step)) % 3
        for i in range(3):
            for j in range(3):
                d, there, to = list(peers(axis_of(j)))[i]
                n = step * 9 + j * 3 + d
                copies.append(remote(parts(j, there), arrive(j, place[axis_of(j)]), hop_sent.at[n], hop_came.at[n], to))
        return copies

    def start(copies):
        for c in copies:
            c.start()
        return copies

    def finish(copies):
        for c in copies:
            c.wait()

    big_sib.wait()
    for r, x, v in chunks(core):
        for j in range(3):
            at = (j, *at_chip(j, r, x))
            m.part0[at] = (v[:, j * L:(j + 1) * L] + m.sib_recv[at].astype(F32)).astype(BF)
    copies = start(hop(0, lambda j, there: m.part0.at[j, there], lambda j, here: m.came0.at[j, here]))
    small_sib.wait()
    small_copies = start(small_hop(0, m.small[mine, :] + m.small_sib[...]))

    def total(part, came, j, here):
        own = part[j, here].astype(F32)
        v = [jnp.where(here == i, own, came[j, i].astype(F32)) for i in range(4)]
        return ((v[0] + v[1]) + (v[2] + v[3])).astype(BF)

    finish(copies)
    for j in range(3):
        m.part1[j] = total(m.part0, m.came0, j, place[j])
    copies = start(hop(1, lambda j, there: m.part1.at[j, there], lambda j, here: m.came1.at[j, here]))
    finish(small_copies)
    small_copies = start(small_hop(1, small_sum(0)))
    finish(copies)
    for j in range(3):
        m.part2[j] = total(m.part1, m.came1, j, place[(j + 1) % 3])
    copies = start(hop(2, lambda j, there: m.part2.at[j, there], lambda j, here: m.came2.at[j, here]))
    finish(small_copies)
    small_copies = start(small_hop(2, small_sum(1)))
    finish(copies)
    for j in range(3):
        m.sum0[j] = total(m.part2, m.came2, j, place[(j + 2) % 3])
        m.sum1[j, place[(j + 2) % 3]] = m.sum0[j]
    copies = start(hop(3, lambda j, there: m.sum0.at[j], lambda j, here: m.sum1.at[j, here]))

    landed_all(m.land, out_recv.at[0])
    for g in range(4):
        a = m.land[g * 32:(g + 1) * 32].reshape(1024, D).astype(F32)
        m.land32[0, g * 1024:(g + 1) * 1024] = a[:, :L]
        m.land32[1, g * 1024:(g + 1) * 1024] = a[:, L:]

    def gather(i, _):
        js = [slot[i * 32 + u] for u in range(32)]
        vs = [[m.land32[k, pl.ds(j, 1), :] for k in range(2)] for j in js]
        for u in range(32):
            for k in range(2):
                m.out32[k, pl.ds(i * 32 + u, 1), :] = vs[u][k]
        return 0

    def gather_some(part):
        steps = TRAJ // 32 // 3
        lax.fori_loop(part * steps, (part + 1) * steps if part < 2 else TRAJ // 32, gather, 0)

    finish(copies)
    for j in range(3):
        m.sum2[j, place[(j + 1) % 3]] = m.sum1[j]
    copies = start(hop(4, lambda j, there: m.sum1.at[j], lambda j, here: m.sum2.at[j, here]))
    finish(small_copies)
    small_out[mine, :] = small_sum(2)
    small_last = remote(small_out.at[mine], small_out.at[mine], one_send.at[11], one_recv.at[11], sibling)
    small_last.start()
    gather_some(0)
    finish(copies)
    for j in range(3):
        ag[core, j, place[j]] = m.sum2[j]
    copies = start(hop(5, lambda j, there: m.sum2.at[j], lambda j, here: ag.at[core, j, here]))
    gather_some(1)
    finish(copies)
    big_last = remote(ag.at[core], ag.at[core], one_send.at[12], one_recv.at[12], sibling)
    big_last.start()
    gather_some(2)
    m.genc_v[...] = jnp.concatenate([m.out32[0], m.out32[1]], axis=1).astype(BF)
    genc_copy = pltpu.make_async_copy(m.genc_v, genc, local.at[6])
    genc_copy.start()
    small_last.wait()
    landed_all(m.dec_v, local.at[5])
    for g in range(PHASES):
        landed_all(m.recv.at[g, pl.ds(0, N - 1)], in_send.at[g])
        landed_all(m.ret.at[g, pl.ds(0, N - 1)], out_send.at[g])
    big_last.wait()
    genc_copy.wait()


def main(outgoing, perm, obs, slot, up, raw):
    vm, sm, an = (pl.BlockSpec(memory_space=m) for m in (pltpu.VMEM, pltpu.SMEM, pl.ANY))
    scratch = [pltpu.VMEM(shape, kind) for shape, kind in MAIN_SCRATCH.values()]
    scratch += [pltpu.VMEM(shape, kind) for shape, kind in SCRATCH.values()] * 2
    scratch += [pltpu.VMEM(shape, kind) for shape, kind in WEIGHTS.values()]
    scratch += [pltpu.VMEM(shape, F32) for shape in ACC.values()]
    scratch += [pltpu.SemaphoreType.DMA((n,)) for n in (PHASES, PHASES, PHASES, 1, 13, 13, 54, 54, 8)]
    return pl.pallas_call(
        main_kernel,
        out_shape=[
            jax.ShapeDtypeStruct((32, L, D), BF),
            jax.ShapeDtypeStruct((TRAJ, D), BF),
            jax.ShapeDtypeStruct((2, 3, 4, 4, 4, 16, L), BF),
            jax.ShapeDtypeStruct((SMALL, D), F32),
        ],
        in_specs=[an, an, vm, vm, sm, an] + [an if k in MATRICES else vm for k in RAW],
        out_specs=[an, an, vm, vm],
        scratch_shapes=scratch,
        compiler_params=pltpu.CompilerParams(vmem_limit_bytes=62 << 20, has_side_effects=True),
    )(outgoing, perm, obs.reshape(32, L), slot.reshape(32, L), slot, up, *raw)


LAST = dict(time=64, **VECTORS)


def last_kernel(dec, genc, ag, small, dec_out, genc_out, proj, mix, exp, red, *rest):
    outs, (ga, dec_v, genc_v, sem_in, sem_out) = rest[:len(LAST)], rest[len(LAST):]
    moves = [(dec.at[pl.ds(i * 8, 8)], dec_v.at[pl.ds(i * 8, 8)], dec_out.at[pl.ds(i * 8, 8)]) for i in range(4)]
    moves += [(genc.at[pl.ds(i * 1024, 1024)], genc_v.at[pl.ds(i * 1024, 1024)], genc_out.at[pl.ds(i * 1024, 1024)]) for i in range(4)]
    copies_in = [pltpu.make_async_copy(a, b, sem_in.at[i]) for i, (a, b, _) in enumerate(moves)]
    copies_out = [pltpu.make_async_copy(b, c, sem_out.at[i]) for i, (_, b, c) in enumerate(moves)]
    for copy in copies_in:
        copy.start()
    for a, b in zip(copies_in, copies_out):
        a.wait()
        b.start()
    for r in range(16):
        for c in range(8):
            coordinate = (c // 2, r % 4, r // 4)
            for j in range(3):
                at = c * CW + j * L
                where = tuple(coordinate[(j + i) % 3] for i in range(3))
                ga[r * 16:(r + 1) * 16, at:at + L] = ag[(c % 2, j, *where)].astype(F32)
    proj[...] = ga[:, :3 * D]
    mix[...] = ga[:, 3 * D:4 * D]
    exp[...] = ga[:, 4 * D:8 * D]
    red[...] = ga[:, 8 * D:].T
    at = 0
    for out, rows in zip(outs, LAST.values()):
        if len(out.shape) == 1:
            for i in range(rows):
                out[pl.ds(i * D, D)] = small[at + i:at + i + 1, :].reshape(D)
        else:
            out[...] = small[at:at + rows, :]
        at += rows
    for copy in copies_out:
        copy.wait()


def last(dec, genc, ag, small):
    vm, an = (pl.BlockSpec(memory_space=m) for m in (pltpu.VMEM, pl.ANY))
    shapes = [((32, L, D), BF), ((TRAJ, D), BF), ((D, 3 * D), F32), ((D, D), F32), ((D, 4 * D), F32), ((4 * D, D), F32)]
    shapes += [((rows, D) if k in ("time", "offsets") else (rows * D,), F32) for k, rows in LAST.items()]
    return pl.pallas_call(
        last_kernel,
        out_shape=[jax.ShapeDtypeStruct(*s) for s in shapes],
        in_specs=[an, an, vm, vm],
        out_specs=[an, an] + [vm] * (len(shapes) - 2),
        scratch_shapes=[
            pltpu.VMEM((D, WIDE), F32), pltpu.VMEM((32, L, D), BF), pltpu.VMEM((TRAJ, D), BF),
            pltpu.SemaphoreType.DMA((8,)), pltpu.SemaphoreType.DMA((8,)),
        ],
        compiler_params=pltpu.CompilerParams(vmem_limit_bytes=62 << 20),
    )(dec, genc, ag, small)


def on_device(encoder_states, position_permutation, observed_tokens, decoder_slot, *rest):
    raw, sensitivity = rest[:-1], rest[-1]
    outgoing = prep(decoder_slot, encoder_states.reshape(TRAJ, D))
    dec, genc, ag, small = main(outgoing, position_permutation, observed_tokens, decoder_slot, sensitivity, raw)
    dec, genc, proj, mix, exp, red, *vectors = last(dec, genc, ag, small)
    v = dict(zip(LAST, vectors))
    return (
        dec, genc.reshape(TRAJ, 1, D), v["hidden"], v["time"], v["scale"], v["shift"], proj, v["offsets"], mix,
        v["recenter"], v["midnorm"], v["midshift"], exp, v["lift"], red, v["trail"],
    )


def solution(mesh):
    in_specs = (P(None, "dp", None),) + (P(),) * 17 + (P("dp", None, None),)
    out_specs = (P("dp", None, None), P(None, "dp", None)) + (P(),) * 14
    return jax.shard_map(on_device, mesh=mesh, in_specs=in_specs, out_specs=out_specs, check_vma=False)
```

```python
import functools
import math

import jax
import jax.numpy as jnp
from jax import lax
from jax.experimental import pallas as pl
from jax.experimental.pallas import tpu as pltpu
from jax.sharding import PartitionSpec as P

MESH = pl.DeviceIdType.MESH

F32 = jnp.float32
BF = jnp.bfloat16
EPSILON = 1e-05
G = 4
L = 128
D = 256
H = 4
R = G * L
D1 = D + 16


def nn(a, b):
    return lax.dot_general(a, b, (((1,), (0,)), ((), ())), preferred_element_type=F32)


def nt(a, b):
    return lax.dot_general(a, b, (((1,), (1,)), ((), ())), preferred_element_type=F32)


def tn(a, b):
    return lax.dot_general(a, b, (((0,), (0,)), ((), ())), preferred_element_type=F32)


def fold(x):
    return jnp.sum(x.reshape(x.shape[0] // 8, 8, x.shape[1]), axis=0)


def norm(x):
    c = x - jnp.mean(x, axis=-1, keepdims=True)
    inv = lax.rsqrt(jnp.mean(c * c, axis=-1, keepdims=True) + EPSILON)
    return c * inv, inv


def norm_back(up, n, inv, gain):
    e = up * gain
    return inv * (e - jnp.mean(e, axis=-1, keepdims=True) - n * jnp.mean(e * n, axis=-1, keepdims=True))


SHIFT = 3.87
POLY = (146.76783278249778, -48.81607899847526, 12.01133916341042, -0.5829371368710288, 0.036552147836326994)
CP = 1.0 / math.sqrt(2.0 * math.pi)
HALF_LOG2E = -0.5 / math.log(2.0)


def gelu_parts(h):
    t = pl.reciprocal(jnp.abs(h) + SHIFT, approx=True)
    e = jnp.exp2(h * h * HALF_LOG2E)
    q = POLY[0]
    for c in POLY[1:]:
        q = q * t + c
    q = q * e
    phi = jnp.where(h >= 0.0, 1.0 - q, q)
    return h * phi, phi + (CP * h) * e


def head_masks():
    lane = lax.broadcasted_iota(jnp.int32, (1, D), 1) // 64
    return [(lane == h).astype(F32).astype(BF) for h in range(H)]


def rows(t, n=1):
    return slice(t * L, (t + n) * L)


def wide2(m):
    return jnp.concatenate([m, m], axis=1)


def before(w, s, acc, io):
    masks = head_masks()
    for t in range(G):
        x = jnp.where(wide2(io.mask(t)) > 0.5, io.x(t), w.hidden[...]) + w.stamped[...]
        s.mid[rows(t), :] = x
        n, inv = norm(x)
        s.inv1[rows(t), :] = jnp.broadcast_to(inv, (L, L))
        s.n1[rows(t), :] = n
        s.first[rows(t), :] = (n * w.gain1[...] + w.shift1[...]).astype(BF)
        yield
    s.firstt[:D, :] = s.first[...].T
    s.upt[...] = io.up_all().T
    for c, ref in enumerate((s.q, s.k, s.v)):
        y = nn(s.first[...], w.qkv[:, c * D:(c + 1) * D]) + w.bqkv[:, c * D:(c + 1) * D]
        y = y.astype(BF)
        if c == 0:
            y = y * BF(0.125)
        ref[...] = y
        yield
    for t in range(G):
        q = s.q[rows(t), :]
        for h in range(H):
            s.qm[t, h * L:(h + 1) * L, :] = q * masks[h]
        st = nt(s.k[rows(t), :], s.qm[t])
        e = jnp.exp(st - jnp.max(st, axis=0, keepdims=True))
        p = e * (1.0 / jnp.sum(e, axis=0, keepdims=True))
        s.p[t] = p
        s.pb[t] = p.astype(BF)
        yield
    for t in range(G):
        vt = s.v[rows(t), :].T
        for h in range(H):
            o = nn(vt[h * 64:(h + 1) * 64, :], s.pb[t, :, h * L:(h + 1) * L])
            s.ot[h * 64:(h + 1) * 64, rows(t)] = o.astype(BF)
        s.o[rows(t), :] = s.ot[:D, rows(t)].T
        yield
    for t in range(0, G, 2):
        proj = nn(s.o[rows(t, 2), :], w.out[...])
        for i in range(2):
            mid = s.mid[rows(t + i), :] + proj[rows(i), :] + w.bout[...]
            s.mid[rows(t + i), :] = mid
            n, inv = norm(mid)
            s.inv2[rows(t + i), :] = jnp.broadcast_to(inv, (L, L))
            s.n2[rows(t + i), :] = n
            s.second[rows(t + i), :] = (n * w.gain2[...] + w.shift2[...]).astype(BF)
        yield
    s.sect[:D, :] = s.second[...].T
    yield


def feed(w, s, acc, io):
    for c in range(4):
        cols = slice(c * D, (c + 1) * D)
        for t in range(G):
            h = nn(s.second[rows(t), :], w.wide[:, cols]) + w.bwide[:, cols]
            ba = nt(io.up(t), w.narrow[cols, :])
            a, da = gelu_parts(h)
            s.act[rows(t), cols] = a.astype(BF)
            s.bh[rows(t), cols] = (ba * da).astype(BF)
            yield


def after(w, s, acc, io):
    masks = head_masks()
    for t in range(0, G, 2):
        dec = nn(s.act[rows(t, 2), :], w.narrow[...])
        for i in range(2):
            io.out(t + i, (s.mid[rows(t + i), :] + dec[rows(i), :] + w.bnarrow[...]).astype(BF))
        yield
        bsec = nt(s.bh[rows(t, 2), :], w.wide[...])
        for i in range(2):
            up = io.up(t + i).astype(F32)
            n, b = s.n2[rows(t + i), :], bsec[rows(i), :]
            acc.trail[...] += fold(up)
            acc.midnorm[...] += fold(b * n)
            acc.midshift[...] += fold(b)
            bm = up + norm_back(b, n, wide2(s.inv2[rows(t + i), :]), w.gain2[...])
            s.mid[rows(t + i), :] = bm
            s.branch[rows(t + i), :] = bm.astype(BF)
            yield
        s.do[rows(t, 2), :] = nt(s.branch[rows(t, 2), :], w.out[...]).astype(BF)
        yield
    for c in range(4):
        cols = slice(c * D, (c + 1) * D)
        acc.exp[:, cols] += nn(s.sect[...], s.bh[:, cols])
        yield
        acc.red[:, cols] += nn(s.upt[...], s.act[:, cols])
        yield
    for t in range(G):
        do = s.do[rows(t), :]
        for h in range(H):
            s.dom[t, h * L:(h + 1) * L, :] = do * masks[h]
        dp = nt(s.v[rows(t), :], s.dom[t])
        p = s.p[t]
        pd = p * dp
        ds = pd - p * jnp.sum(pd, axis=0, keepdims=True)
        s.ds[t] = ds.astype(BF)
        yield
    for t in range(G):
        s.bt[rows(t), 2 * D:] = nn(s.pb[t], s.dom[t]).astype(BF)
        yield
        s.bt[rows(t), D:2 * D] = nn(s.ds[t], s.qm[t]).astype(BF)
        yield
        kt = s.k[rows(t), :].T
        for h in range(H):
            dq = nn(kt[h * 64:(h + 1) * 64, :], s.ds[t, :, h * L:(h + 1) * L]) * 0.125
            s.dqt[t, h * 64:(h + 1) * 64, :] = dq.astype(BF)
        s.bt[rows(t), :D] = s.dqt[t].T
        yield
    acc.mix[...] += nn(s.ot[...], s.branch[...])
    yield
    for t in range(0, G, 2):
        bfirst = nt(s.bt[rows(t, 2), :], w.qkv[...])
        for i in range(2):
            n, b = s.n1[rows(t + i), :], bfirst[rows(i), :]
            acc.scale[...] += fold(b * n)
            acc.shift[...] += fold(b)
            bi = s.mid[rows(t + i), :] + norm_back(b, n, wide2(s.inv1[rows(t + i), :]), w.gain1[...])
            acc.time[...] += bi
            ret = jnp.where(wide2(io.mask(t + i)) > 0.5, bi, 0.0)
            acc.hidden[...] += fold(bi - ret)
            io.ret(t + i, ret)
            yield
    for c in range(3):
        cols = slice(c * D, (c + 1) * D)
        acc.proj[:, cols] += nn(s.firstt[...], s.bt[:, cols])
        yield


def chain(*parts):
    for part in parts:
        yield from part


def weave(one, other):
    one, other = list_pieces(one), list_pieces(other)
    total = max(one.count, other.count)
    for i in range(total):
        one.upto(-(-(i + 1) * one.count // total))
        other.upto(-(-(i + 1) * other.count // total))


class list_pieces:
    def __init__(self, make):
        self.steps, self.count, self.done = make[0](), make[1], 0

    def upto(self, n):
        while self.done < n:
            next(self.steps, None)
            self.done += 1
            if self.done == self.count:
                for _ in self.steps:
                    pass


BEFORE, FEED, AFTER = 18, 16, 47


class Bag:
    def __init__(self, **kw):
        self.__dict__.update(kw)


SCRATCH = dict(
    inv1=((R, L), F32), inv2=((R, L), F32), mid=((R, D), F32), n1=((R, D), F32), n2=((R, D), F32), first=((R, D), BF), second=((R, D), BF),
    q=((R, D), BF), k=((R, D), BF), v=((R, D), BF), qm=((G, H * L, D), BF), dom=((G, H * L, D), BF),
    p=((G, L, H * L), F32), pb=((G, L, H * L), BF), ds=((G, L, H * L), BF),
    ot=((D1, R), BF), sect=((D1, R), BF), firstt=((D1, R), BF), upt=((D, R), BF), o=((R, D), BF), dqt=((G, D, L), BF),
    act=((R, 4 * D), BF), bh=((R, 4 * D), BF), branch=((R, D), BF), do=((R, D), BF), bt=((R, 3 * D), BF),
)
ACC = dict(
    trail=(8, D), midnorm=(8, D), midshift=(8, D), scale=(8, D), shift=(8, D), hidden=(8, D), time=(L, D),
)
COLUMNS = dict(proj=(0, 3 * D), mix=(3 * D, D), exp=(4 * D, 4 * D), red=(8 * D, 4 * D))
WIDE = 12 * D
WEIGHTS = dict(
    hidden=((1, D), F32), stamped=((L, D), F32), gain1=((1, D), F32), shift1=((1, D), F32), qkv=((D, 3 * D), BF),
    bqkv=((1, 3 * D), F32), out=((D, D), BF), bout=((1, D), F32), gain2=((1, D), F32), shift2=((1, D), F32),
    wide=((D, 4 * D), BF), bwide=((1, 4 * D), F32), narrow=((4 * D, D), BF), bnarrow=((1, D), F32),
)


RAW = ("hidden", "stamped", "gain1", "shift1", "qkv", "bqkv", "out", "bout", "gain2", "shift2", "wide", "bwide", "narrow", "bnarrow")
MATRICES = ("qkv", "out", "wide", "narrow")


def spread(raw, w):
    for k in RAW:
        if k == "stamped":
            v = raw[k][...].astype(F32)
            w.stamped[...] = jnp.broadcast_to(v[:, None, :], (L // 2, 2, D)).reshape(L, D)
        elif k == "bqkv":
            v = raw[k][...].astype(F32)
            w.bqkv[:, :D] = v[:1]
            w.bqkv[:, D:2 * D] = jnp.zeros((1, D), F32)
            w.bqkv[:, 2 * D:] = v[1:]
        elif k not in MATRICES:
            v = raw[k][...].astype(F32)
            getattr(w, k)[...] = v.reshape(1, -1)


N = 128
PHASES = 4
EACH = 8
TRAJ = 4096
CW = 384
VECTORS = dict(lift=4, trail=1, midnorm=1, midshift=1, recenter=1, offsets=2, scale=1, shift=1, hidden=1)
SMALL = 80
HALF = SMALL // 2


def prep_kernel(unroll, slot, enc, out, src, dst):
    x = enc[...].astype(F32)
    src[0] = x[:, :L]
    src[1] = x[:, L:]

    def block(i, _):
        js = [slot[i * unroll + u] for u in range(unroll)]
        vs = [[src[k, pl.ds(i * unroll + u, 1), :] for k in range(2)] for u in range(unroll)]
        for u in range(unroll):
            for k in range(2):
                dst[k, pl.ds(js[u], 1), :] = vs[u][k]
        return 0

    lax.fori_loop(0, TRAJ // unroll, block, 0)
    for g in range(4):
        at = pl.ds(g * 1024, 1024)
        y = jnp.concatenate([dst[0, at, :], dst[1, at, :]], axis=1)
        out[g * 32:(g + 1) * 32] = y.astype(BF).reshape(32, PHASES, EACH, D)


def prep(slot, enc):
    vm, sm = (pl.BlockSpec(memory_space=m) for m in (pltpu.VMEM, pltpu.SMEM))
    return pl.pallas_call(
        functools.partial(prep_kernel, 32),
        out_shape=jax.ShapeDtypeStruct((N, PHASES, EACH, D), BF),
        in_specs=[sm, vm],
        out_specs=vm,
        scratch_shapes=[pltpu.VMEM((2, TRAJ, L), F32), pltpu.VMEM((2, TRAJ, L), F32)],
        compiler_params=pltpu.CompilerParams(vmem_limit_bytes=56 << 20),
    )(slot, enc)


def others(me):
    cs = [me % 2, 1 - me % 2]
    xs = [(me // 2 + d) % 4 * 2 for d in range(4)]
    ys = [(me // 8 + d) % 4 * 8 for d in range(4)]
    zs = [(me // 32 + d) % 4 * 32 for d in range(4)]
    hops = lambda k: sum((0, 1, 2, 1)[k // unit % 4] for unit in (2, 8, 32))
    far_first = sorted(range(1, N), key=hops, reverse=True)
    return [zs[k // 32] + ys[k // 8 % 4] + xs[k // 2 % 4] + cs[k % 2] for k in far_first]


def remote(src, dst, send, recv, to):
    return pltpu.make_async_remote_copy(src, dst, send, recv, device_id=(to,), device_id_type=MESH)


def landed_all(ref, sem):
    pltpu.make_async_copy(ref, ref, sem).wait()


MAIN_SCRATCH = dict(
    recv=((PHASES, N, EACH, D), BF), ret=((PHASES, N, EACH, D), BF), land=((N, PHASES, EACH, D), BF),
    mask=((32, L, L), F32), x32=((2, N * EACH, L), F32), ret32=((2, N * EACH, L), F32),
    land32=((2, TRAJ, L), F32), out32=((2, TRAJ, L), F32), perm=((TRAJ, L), jnp.int32), hot=((32, TRAJ), BF),
    counts=((32, L), F32), order=((32, L), F32), ga=((D1, WIDE), F32),
    sib_send=((3, 4, 16, 16, L), BF), sib_recv=((3, 4, 16, 16, L), BF), part0=((3, 4, 16, 16, L), BF),
    came0=((3, 4, 16, 16, L), BF), part1=((3, 16, 16, L), BF), came1=((3, 16, 16, L), BF),
    sum0=((3, 16, L), BF), sum2=((3, 16, 16, L), BF),
    dec_v=((32, L, D), BF), genc_v=((TRAJ, D), BF), up=((32, L, D), BF),
    small=((SMALL, D), F32), small_sib=((HALF, D), F32), hop_send=((3, HALF, D), F32), hop=((3, 4, HALF, D), F32),
)


def main_kernel(*refs):
    outgoing, perm_hbm, obs, slots, slot, up_hbm = refs[:6]
    raw = dict(zip(RAW, refs[6:6 + len(RAW)]))
    refs = refs[6 + len(RAW):]
    dec, genc, ag, small_out = refs[:4]
    refs = refs[4:]
    m = Bag(**dict(zip(MAIN_SCRATCH, refs)))
    refs = refs[len(MAIN_SCRATCH):]
    pair = []
    for _ in range(2):
        pair.append(Bag(**dict(zip(SCRATCH, refs))))
        refs = refs[len(SCRATCH):]
    w = Bag(**dict(zip(WEIGHTS, refs)))
    refs = refs[len(WEIGHTS):]
    acc = Bag(**dict(zip(ACC, refs)))
    in_send, in_recv, out_send, out_recv, one_send, one_recv, hop_sent, hop_came, plane_sem, local = refs[len(ACC):]
    for k, (at, width) in COLUMNS.items():
        setattr(acc, k, m.ga.at[pl.ds(0, D if k == "red" else D1), pl.ds(at, width)])
    me = lax.axis_index("dp")
    core = me % 2
    sibling = me + 1 - 2 * core

    def send_in(g):
        pltpu.make_async_copy(outgoing.at[me, g], m.recv.at[g, me], in_recv.at[g]).start()
        for to in others(me):
            remote(outgoing.at[to, g], m.recv.at[g, me], in_send.at[g], in_recv.at[g], to).start()

    send_in(0)
    order_load = pltpu.make_async_copy(perm_hbm, m.perm, local.at[7])
    order_load.start()
    loads = [pltpu.make_async_copy(up_hbm, m.up, local.at[0])]
    loads += [pltpu.make_async_copy(raw[k], getattr(w, k), local.at[1 + i]) for i, k in enumerate(MATRICES)]
    for copy in loads:
        copy.start()
    spread(raw, w)
    for s in pair:
        for r in (s.ot, s.sect, s.firstt):
            r[D:, :] = jnp.ones((16, R), BF)

    mine = me * 32 + lax.broadcasted_iota(jnp.int32, (32, L), 0)
    counts = jnp.zeros((32, L), F32)
    for r in range(TRAJ // L):
        hot = (slots[r:r + 1, :] == mine).astype(F32)
        counts += hot * obs[r:r + 1, :].astype(F32)
        m.hot[:, r * L:(r + 1) * L] = hot.astype(BF)
    m.counts[...] = jnp.broadcast_to(jnp.sum(counts, axis=1, keepdims=True), (32, L))
    order_load.wait()
    m.order[...] = nn(m.hot[...], m.perm[...].astype(F32).astype(BF))

    def one_mask(j, _):
        place = lax.broadcasted_iota(jnp.int32, (L, L), 0).astype(F32)
        hot = (m.order[pl.ds(j, 1), :] == place).astype(F32).astype(BF)
        early = (place < m.counts[pl.ds(j, 1), :]).astype(F32).astype(BF)
        m.mask[j] = nn(hot, early)
        return 0

    lax.fori_loop(0, 32, one_mask, 0)
    for copy in loads:
        copy.wait()

    def io_of(g, half):
        base = g * EACH + half * G
        own = lambda t: pl.ds(half * G + t, L, stride=EACH)

        def out(t, v):
            m.dec_v[base + t] = v

        def ret(t, v):
            for i in range(2):
                m.ret32[i, own(t), :] = v[:, i * L:(i + 1) * L]

        return Bag(
            x=lambda t: jnp.concatenate([m.x32[i, own(t), :] for i in range(2)], axis=1),
            mask=lambda t: m.mask[base + t],
            up=lambda t: m.up[base + t],
            up_all=lambda: m.up[pl.ds(base, G)].reshape(R, D),
            out=out,
            ret=ret,
        )

    def forward(half, io):
        return lambda: chain(before(w, pair[half], acc, io), feed(w, pair[half], acc, io)), BEFORE + FEED

    def backward(half, io):
        return lambda: after(w, pair[half], acc, io), AFTER

    def send_out(g):
        m.ret[g] = jnp.concatenate([m.ret32[0], m.ret32[1]], axis=1).astype(BF).reshape(N, EACH, D)
        pltpu.make_async_copy(m.ret.at[g, me], m.land.at[me, g], out_recv.at[0]).start()
        for to in others(me):
            remote(m.ret.at[g, to], m.land.at[me, g], out_send.at[g], out_recv.at[0], to).start()
        mine = pl.ds(g * EACH, EACH)
        pltpu.make_async_copy(m.dec_v.at[mine], dec.at[mine], local.at[5]).start()

    def phase(g, _):
        landed_all(m.recv.at[g], in_recv.at[g])

        @pl.when(g < PHASES - 1)
        def _():
            send_in(g + 1)

        a = m.recv[g].reshape(N * EACH, D).astype(F32)
        m.x32[0] = a[:, :L]
        m.x32[1] = a[:, L:]
        earlier = g - (g + PHASES - 1) // PHASES
        weave(forward(0, io_of(g, 0)), backward(1, io_of(earlier, 1)))

        @pl.when(g == 0)
        def _():
            m.ga[...] = jnp.zeros_like(m.ga)
            for k in ACC:
                r = getattr(acc, k)
                r[...] = jnp.zeros_like(r)

        @pl.when(g > 0)
        def _():
            send_out(g - 1)

        weave(forward(1, io_of(g, 1)), backward(0, io_of(g, 0)))
        return 0

    lax.fori_loop(0, PHASES, phase, 0)
    for _ in after(w, pair[1], acc, io_of(PHASES - 1, 1)):
        pass

    units = (2, 8, 32)
    place = [(me // unit) % 4 for unit in units]

    def at_chip(j, r, x):
        coordinate = (x, r % 4, r // 4)
        a, b, c = (coordinate[(j + i) % 3] for i in range(3))
        return a, b * 4 + c

    def chunks(of_core):
        for r in range(16):
            for x in range(4):
                at = pl.multiple_of((2 * x + of_core) * CW, L)
                yield r, x, m.ga[r * 16:(r + 1) * 16, pl.ds(at, CW)]

    for r, x, v in chunks(1 - core):
        v = v.astype(BF)
        for j in range(3):
            m.sib_send[(j, *at_chip(j, r, x))] = v[:, j * L:(j + 1) * L]
    big_sib = remote(m.sib_send, m.sib_recv, one_send.at[0], one_recv.at[0], sibling)
    big_sib.start()
    send_out(PHASES - 1)
    t3 = acc.time[...].reshape(64, 2, D)
    m.small[:64] = t3[:, 0] + t3[:, 1]
    m.small[64:] = jnp.zeros((16, D), F32)
    at = 64
    for k, count in VECTORS.items():
        if k == "lift":
            v = acc.exp[D:D + 1, :]
        elif k == "recenter":
            v = acc.mix[D:D + 1, :]
        elif k == "offsets":
            v = jnp.concatenate([acc.proj[D:D + 1, :D], acc.proj[D:D + 1, 2 * D:]], axis=1)
        else:
            v = jnp.sum(getattr(acc, k)[...], axis=0, keepdims=True)
        for i in range(count):
            m.small[at:at + 1, :] = v[:, i * D:(i + 1) * D]
            at += 1
    mine = pl.ds(pl.multiple_of(core * HALF, 8), HALF)
    other = pl.ds(pl.multiple_of((1 - core) * HALF, 8), HALF)
    small_sib = remote(m.small.at[other], m.small_sib, one_send.at[1], one_recv.at[1], sibling)
    small_sib.start()

    def peers(axis):
        for d in (2, 1, 3):
            there = (place[axis] + d) % 4
            yield d - 1, there, me + (there - place[axis]) * units[axis]

    def small_hop(axis, value):
        m.hop_send[axis] = value
        m.hop[axis, place[axis]] = value
        copies = []
        for i, there, to in peers(axis):
            n = 2 + 3 * axis + i
            copies.append(remote(m.hop_send.at[axis], m.hop.at[axis, place[axis]], one_send.at[n], one_recv.at[n], to))
        return copies

    def small_sum(axis):
        return (m.hop[axis, 0] + m.hop[axis, 1]) + (m.hop[axis, 2] + m.hop[axis, 3])

    def hop(step, parts, arrive):
        copies = []
        axis_of = lambda j: j
        for i in range(3):
            for j in range(3):
                d, there, to = list(peers(axis_of(j)))[i]
                n = step * 9 + j * 3 + d
                copies.append(remote(parts(j, there), arrive(j, place[axis_of(j)]), hop_sent.at[n], hop_came.at[n], to))
        return copies

    def start(copies):
        for c in copies:
            c.start()
        return copies

    def finish(copies):
        for c in copies:
            c.wait()

    big_sib.wait()
    for r, x, v in chunks(core):
        for j in range(3):
            at = (j, *at_chip(j, r, x))
            m.part0[at] = (v[:, j * L:(j + 1) * L] + m.sib_recv[at].astype(F32)).astype(BF)
    copies = start(hop(0, lambda j, there: m.part0.at[j, there], lambda j, here: m.came0.at[j, here]))
    small_sib.wait()
    small_copies = start(small_hop(0, m.small[mine, :] + m.small_sib[...]))

    def total(part, came, j, here):
        own = part[j, here].astype(F32)
        v = [jnp.where(here == i, own, came[j, i].astype(F32)) for i in range(4)]
        return ((v[0] + v[1]) + (v[2] + v[3])).astype(BF)

    def plane(part, arrive, sent, came):
        copies = []
        for d2, d3 in sorted(((a, b) for a in range(4) for b in range(4) if a or b), key=lambda d: -(d[0] == 2) - (d[1] == 2)):
            for j in range(3):
                second, third = (j + 1) % 3, (j + 2) % 3
                p2, p3 = (place[second] + d2) % 4, (place[third] + d3) % 4
                to = me + (p2 - place[second]) * units[second] + (p3 - place[third]) * units[third]
                copies.append(remote(part(j, p2 * 4 + p3), arrive.at[j, in_plane(j)], sent, came, to))
        return start(copies)

    in_plane = lambda j: place[(j + 1) % 3] * 4 + place[(j + 2) % 3]
    finish(copies)
    for j in range(3):
        m.part1[j] = total(m.part0, m.came0, j, place[j])
        m.came1[j, in_plane(j)] = m.part1[j, in_plane(j)]
    plane(lambda j, there: m.part1.at[j, there], m.came1, plane_sem.at[0], plane_sem.at[1])
    finish(small_copies)
    small_copies = start(small_hop(1, small_sum(0)))
    landed_all(m.came1.at[:, pl.ds(0, 15)], plane_sem.at[1])
    for j in range(3):
        m.sum0[j] = jnp.sum(m.came1[j].astype(F32), axis=0).astype(BF)
        m.sum2[j, in_plane(j)] = m.sum0[j]
    plane(lambda j, there: m.sum0.at[j], m.sum2, plane_sem.at[2], plane_sem.at[3])
    finish(small_copies)
    small_copies = start(small_hop(2, small_sum(1)))

    landed_all(m.land, out_recv.at[0])
    for g in range(4):
        a = m.land[g * 32:(g + 1) * 32].reshape(1024, D).astype(F32)
        m.land32[0, g * 1024:(g + 1) * 1024] = a[:, :L]
        m.land32[1, g * 1024:(g + 1) * 1024] = a[:, L:]

    def gather(i, _):
        js = [slot[i * 32 + u] for u in range(32)]
        vs = [[m.land32[k, pl.ds(j, 1), :] for k in range(2)] for j in js]
        for u in range(32):
            for k in range(2):
                m.out32[k, pl.ds(i * 32 + u, 1), :] = vs[u][k]
        return 0

    def gather_some(part):
        steps = TRAJ // 32 // 3
        lax.fori_loop(part * steps, (part + 1) * steps if part < 2 else TRAJ // 32, gather, 0)

    gather_some(0)
    finish(small_copies)
    small_out[mine, :] = small_sum(2)
    small_last = remote(small_out.at[mine], small_out.at[mine], one_send.at[11], one_recv.at[11], sibling)
    small_last.start()
    landed_all(m.sum2.at[:, pl.ds(0, 15)], plane_sem.at[3])
    for j in range(3):
        ag[core, j, place[j]] = m.sum2[j]
    copies = start(hop(1, lambda j, there: m.sum2.at[j], lambda j, here: ag.at[core, j, here]))
    gather_some(1)
    finish(copies)
    big_last = remote(ag.at[core], ag.at[core], one_send.at[12], one_recv.at[12], sibling)
    big_last.start()
    gather_some(2)
    m.genc_v[...] = jnp.concatenate([m.out32[0], m.out32[1]], axis=1).astype(BF)
    genc_copy = pltpu.make_async_copy(m.genc_v, genc, local.at[6])
    genc_copy.start()
    small_last.wait()
    landed_all(m.dec_v, local.at[5])
    for g in range(PHASES):
        landed_all(m.recv.at[g, pl.ds(0, N - 1)], in_send.at[g])
        landed_all(m.ret.at[g, pl.ds(0, N - 1)], out_send.at[g])
    for i in (0, 2):
        landed_all(m.came1.at[:, pl.ds(0, 15)], plane_sem.at[i])
    big_last.wait()
    genc_copy.wait()


def main(outgoing, perm, obs, slot, up, raw):
    vm, sm, an = (pl.BlockSpec(memory_space=m) for m in (pltpu.VMEM, pltpu.SMEM, pl.ANY))
    scratch = [pltpu.VMEM(shape, kind) for shape, kind in MAIN_SCRATCH.values()]
    scratch += [pltpu.VMEM(shape, kind) for shape, kind in SCRATCH.values()] * 2
    scratch += [pltpu.VMEM(shape, kind) for shape, kind in WEIGHTS.values()]
    scratch += [pltpu.VMEM(shape, F32) for shape in ACC.values()]
    scratch += [pltpu.SemaphoreType.DMA((n,)) for n in (PHASES, PHASES, PHASES, 1, 13, 13, 18, 18, 4, 8)]
    return pl.pallas_call(
        main_kernel,
        out_shape=[
            jax.ShapeDtypeStruct((32, L, D), BF),
            jax.ShapeDtypeStruct((TRAJ, D), BF),
            jax.ShapeDtypeStruct((2, 3, 4, 16, 16, L), BF),
            jax.ShapeDtypeStruct((SMALL, D), F32),
        ],
        in_specs=[an, an, vm, vm, sm, an] + [an if k in MATRICES else vm for k in RAW],
        out_specs=[an, an, vm, vm],
        scratch_shapes=scratch,
        compiler_params=pltpu.CompilerParams(vmem_limit_bytes=62 << 20, has_side_effects=True),
    )(outgoing, perm, obs.reshape(32, L), slot.reshape(32, L), slot, up, *raw)


LAST = dict(time=64, **VECTORS)


def last_kernel(dec, genc, ag, small, dec_out, genc_out, proj, mix, exp, red, *rest):
    outs, (ga, dec_v, genc_v, sem_in, sem_out) = rest[:len(LAST)], rest[len(LAST):]
    moves = [(dec.at[pl.ds(i * 8, 8)], dec_v.at[pl.ds(i * 8, 8)], dec_out.at[pl.ds(i * 8, 8)]) for i in range(4)]
    moves += [(genc.at[pl.ds(i * 1024, 1024)], genc_v.at[pl.ds(i * 1024, 1024)], genc_out.at[pl.ds(i * 1024, 1024)]) for i in range(4)]
    copies_in = [pltpu.make_async_copy(a, b, sem_in.at[i]) for i, (a, b, _) in enumerate(moves)]
    copies_out = [pltpu.make_async_copy(b, c, sem_out.at[i]) for i, (_, b, c) in enumerate(moves)]
    for copy in copies_in:
        copy.start()
    for a, b in zip(copies_in, copies_out):
        a.wait()
        b.start()
    for r in range(16):
        for c in range(8):
            coordinate = (c // 2, r % 4, r // 4)
            for j in range(3):
                at = c * CW + j * L
                p1, p2, p3 = (coordinate[(j + i) % 3] for i in range(3))
                ga[r * 16:(r + 1) * 16, at:at + L] = ag[c % 2, j, p1, p2 * 4 + p3].astype(F32)
    proj[...] = ga[:, :3 * D]
    mix[...] = ga[:, 3 * D:4 * D]
    exp[...] = ga[:, 4 * D:8 * D]
    red[...] = ga[:, 8 * D:].T
    at = 0
    for out, rows in zip(outs, LAST.values()):
        if len(out.shape) == 1:
            for i in range(rows):
                out[pl.ds(i * D, D)] = small[at + i:at + i + 1, :].reshape(D)
        else:
            out[...] = small[at:at + rows, :]
        at += rows
    for copy in copies_out:
        copy.wait()


def last(dec, genc, ag, small):
    vm, an = (pl.BlockSpec(memory_space=m) for m in (pltpu.VMEM, pl.ANY))
    shapes = [((32, L, D), BF), ((TRAJ, D), BF), ((D, 3 * D), F32), ((D, D), F32), ((D, 4 * D), F32), ((4 * D, D), F32)]
    shapes += [((rows, D) if k in ("time", "offsets") else (rows * D,), F32) for k, rows in LAST.items()]
    return pl.pallas_call(
        last_kernel,
        out_shape=[jax.ShapeDtypeStruct(*s) for s in shapes],
        in_specs=[an, an, vm, vm],
        out_specs=[an, an] + [vm] * (len(shapes) - 2),
        scratch_shapes=[
            pltpu.VMEM((D, WIDE), F32), pltpu.VMEM((32, L, D), BF), pltpu.VMEM((TRAJ, D), BF),
            pltpu.SemaphoreType.DMA((8,)), pltpu.SemaphoreType.DMA((8,)),
        ],
        compiler_params=pltpu.CompilerParams(vmem_limit_bytes=62 << 20),
    )(dec, genc, ag, small)


def on_device(encoder_states, position_permutation, observed_tokens, decoder_slot, *rest):
    raw, sensitivity = rest[:-1], rest[-1]
    outgoing = prep(decoder_slot, encoder_states.reshape(TRAJ, D))
    dec, genc, ag, small = main(outgoing, position_permutation, observed_tokens, decoder_slot, sensitivity, raw)
    dec, genc, proj, mix, exp, red, *vectors = last(dec, genc, ag, small)
    v = dict(zip(LAST, vectors))
    return (
        dec, genc.reshape(TRAJ, 1, D), v["hidden"], v["time"], v["scale"], v["shift"], proj, v["offsets"], mix,
        v["recenter"], v["midnorm"], v["midshift"], exp, v["lift"], red, v["trail"],
    )


def solution(mesh):
    in_specs = (P(None, "dp", None),) + (P(),) * 17 + (P("dp", None, None),)
    out_specs = (P("dp", None, None), P(None, "dp", None)) + (P(),) * 14
    return jax.shard_map(on_device, mesh=mesh, in_specs=in_specs, out_specs=out_specs, check_vma=False)
```

```python
import functools
import math

import jax
import jax.numpy as jnp
from jax import lax
from jax.experimental import pallas as pl
from jax.experimental.pallas import tpu as pltpu
from jax.sharding import PartitionSpec as P

MESH = pl.DeviceIdType.MESH

F32 = jnp.float32
BF = jnp.bfloat16
EPSILON = 1e-05
G = 4
L = 128
D = 256
H = 4
R = G * L
D1 = D + 16


def nn(a, b):
    return lax.dot_general(a, b, (((1,), (0,)), ((), ())), preferred_element_type=F32)


def nt(a, b):
    return lax.dot_general(a, b, (((1,), (1,)), ((), ())), preferred_element_type=F32)


def tn(a, b):
    return lax.dot_general(a, b, (((0,), (0,)), ((), ())), preferred_element_type=F32)


def fold(x):
    return jnp.sum(x.reshape(x.shape[0] // 8, 8, x.shape[1]), axis=0)


def norm(x):
    c = x - jnp.mean(x, axis=-1, keepdims=True)
    inv = lax.rsqrt(jnp.mean(c * c, axis=-1, keepdims=True) + EPSILON)
    return c * inv, inv


def norm_back(up, n, inv, gain):
    e = up * gain
    return inv * (e - jnp.mean(e, axis=-1, keepdims=True) - n * jnp.mean(e * n, axis=-1, keepdims=True))


SHIFT = 3.87
POLY = (146.76783278249778, -48.81607899847526, 12.01133916341042, -0.5829371368710288, 0.036552147836326994)
CP = 1.0 / math.sqrt(2.0 * math.pi)
HALF_LOG2E = -0.5 / math.log(2.0)


def gelu_parts(h):
    t = pl.reciprocal(jnp.abs(h) + SHIFT, approx=True)
    e = jnp.exp2(h * h * HALF_LOG2E)
    q = POLY[0]
    for c in POLY[1:]:
        q = q * t + c
    q = q * e
    phi = jnp.where(h >= 0.0, 1.0 - q, q)
    return h * phi, phi + (CP * h) * e


def head_masks():
    lane = lax.broadcasted_iota(jnp.int32, (1, D), 1) // 64
    return [(lane == h).astype(F32).astype(BF) for h in range(H)]


def rows(t, n=1):
    return slice(t * L, (t + n) * L)


def wide2(m):
    return jnp.concatenate([m, m], axis=1)


def before(w, s, acc, io):
    masks = head_masks()
    for t in range(G):
        x = jnp.where(wide2(io.mask(t)) > 0.5, io.x(t), w.hidden[...]) + w.stamped[...]
        s.mid[rows(t), :] = x
        n, inv = norm(x)
        s.inv1[rows(t), :] = jnp.broadcast_to(inv, (L, L))
        s.n1[rows(t), :] = n
        s.first[rows(t), :] = (n * w.gain1[...] + w.shift1[...]).astype(BF)
        yield
    s.firstt[:D, :] = s.first[...].T
    s.upt[...] = io.up_all().T
    for c, ref in enumerate((s.q, s.k, s.v)):
        y = nn(s.first[...], w.qkv[:, c * D:(c + 1) * D]) + w.bqkv[:, c * D:(c + 1) * D]
        y = y.astype(BF)
        if c == 0:
            y = y * BF(0.125)
        ref[...] = y
        yield
    for t in range(G):
        q = s.q[rows(t), :]
        for h in range(H):
            s.qm[t, h * L:(h + 1) * L, :] = q * masks[h]
        st = nt(s.k[rows(t), :], s.qm[t])
        e = jnp.exp(st - jnp.max(st, axis=0, keepdims=True))
        p = e * (1.0 / jnp.sum(e, axis=0, keepdims=True))
        s.p[t] = p
        s.pb[t] = p.astype(BF)
        yield
    for t in range(G):
        vt = s.v[rows(t), :].T
        for h in range(H):
            o = nn(vt[h * 64:(h + 1) * 64, :], s.pb[t, :, h * L:(h + 1) * L])
            s.ot[h * 64:(h + 1) * 64, rows(t)] = o.astype(BF)
        s.o[rows(t), :] = s.ot[:D, rows(t)].T
        yield
    for t in range(0, G, 2):
        proj = nn(s.o[rows(t, 2), :], w.out[...])
        for i in range(2):
            mid = s.mid[rows(t + i), :] + proj[rows(i), :] + w.bout[...]
            s.mid[rows(t + i), :] = mid
            n, inv = norm(mid)
            s.inv2[rows(t + i), :] = jnp.broadcast_to(inv, (L, L))
            s.n2[rows(t + i), :] = n
            s.second[rows(t + i), :] = (n * w.gain2[...] + w.shift2[...]).astype(BF)
        yield
    s.sect[:D, :] = s.second[...].T
    yield


def feed(w, s, acc, io):
    for c in range(4):
        cols = slice(c * D, (c + 1) * D)
        for t in range(G):
            h = nn(s.second[rows(t), :], w.wide[:, cols]) + w.bwide[:, cols]
            ba = nt(io.up(t), w.narrow[cols, :])
            a, da = gelu_parts(h)
            s.act[rows(t), cols] = a.astype(BF)
            s.bh[rows(t), cols] = (ba * da).astype(BF)
            yield


def after(w, s, acc, io):
    masks = head_masks()
    for t in range(0, G, 2):
        dec = nn(s.act[rows(t, 2), :], w.narrow[...])
        for i in range(2):
            io.out(t + i, (s.mid[rows(t + i), :] + dec[rows(i), :] + w.bnarrow[...]).astype(BF))
        yield
        bsec = nt(s.bh[rows(t, 2), :], w.wide[...])
        for i in range(2):
            up = io.up(t + i).astype(F32)
            n, b = s.n2[rows(t + i), :], bsec[rows(i), :]
            acc.trail[...] += fold(up)
            acc.midnorm[...] += fold(b * n)
            acc.midshift[...] += fold(b)
            bm = up + norm_back(b, n, wide2(s.inv2[rows(t + i), :]), w.gain2[...])
            s.mid[rows(t + i), :] = bm
            s.branch[rows(t + i), :] = bm.astype(BF)
            yield
        s.do[rows(t, 2), :] = nt(s.branch[rows(t, 2), :], w.out[...]).astype(BF)
        yield
    for c in range(4):
        cols = slice(c * D, (c + 1) * D)
        acc.exp[:, cols] += nn(s.sect[...], s.bh[:, cols])
        yield
        acc.red[:, cols] += nn(s.upt[...], s.act[:, cols])
        yield
    for t in range(G):
        do = s.do[rows(t), :]
        for h in range(H):
            s.dom[t, h * L:(h + 1) * L, :] = do * masks[h]
        dp = nt(s.v[rows(t), :], s.dom[t])
        p = s.p[t]
        pd = p * dp
        ds = pd - p * jnp.sum(pd, axis=0, keepdims=True)
        s.ds[t] = ds.astype(BF)
        yield
    for t in range(G):
        s.bt[rows(t), 2 * D:] = nn(s.pb[t], s.dom[t]).astype(BF)
        yield
        s.bt[rows(t), D:2 * D] = nn(s.ds[t], s.qm[t]).astype(BF)
        yield
        kt = s.k[rows(t), :].T
        for h in range(H):
            dq = nn(kt[h * 64:(h + 1) * 64, :], s.ds[t, :, h * L:(h + 1) * L]) * 0.125
            s.dqt[t, h * 64:(h + 1) * 64, :] = dq.astype(BF)
        s.bt[rows(t), :D] = s.dqt[t].T
        yield
    acc.mix[...] += nn(s.ot[...], s.branch[...])
    yield
    for t in range(0, G, 2):
        bfirst = nt(s.bt[rows(t, 2), :], w.qkv[...])
        for i in range(2):
            n, b = s.n1[rows(t + i), :], bfirst[rows(i), :]
            acc.scale[...] += fold(b * n)
            acc.shift[...] += fold(b)
            bi = s.mid[rows(t + i), :] + norm_back(b, n, wide2(s.inv1[rows(t + i), :]), w.gain1[...])
            acc.time[...] += bi
            ret = jnp.where(wide2(io.mask(t + i)) > 0.5, bi, 0.0)
            acc.hidden[...] += fold(bi - ret)
            io.ret(t + i, ret)
            yield
    for c in range(3):
        cols = slice(c * D, (c + 1) * D)
        acc.proj[:, cols] += nn(s.firstt[...], s.bt[:, cols])
        yield


def chain(*parts):
    for part in parts:
        yield from part


def weave(one, other):
    one, other = list_pieces(one), list_pieces(other)
    total = max(one.count, other.count)
    for i in range(total):
        one.upto(-(-(i + 1) * one.count // total))
        other.upto(-(-(i + 1) * other.count // total))


class list_pieces:
    def __init__(self, make):
        self.steps, self.count, self.done = make[0](), make[1], 0

    def upto(self, n):
        while self.done < n:
            next(self.steps, None)
            self.done += 1
            if self.done == self.count:
                for _ in self.steps:
                    pass


BEFORE, FEED, AFTER = 18, 16, 47


class Bag:
    def __init__(self, **kw):
        self.__dict__.update(kw)


SCRATCH = dict(
    inv1=((R, L), F32), inv2=((R, L), F32), mid=((R, D), F32), n1=((R, D), F32), n2=((R, D), F32), first=((R, D), BF), second=((R, D), BF),
    q=((R, D), BF), k=((R, D), BF), v=((R, D), BF), qm=((G, H * L, D), BF), dom=((G, H * L, D), BF),
    p=((G, L, H * L), F32), pb=((G, L, H * L), BF), ds=((G, L, H * L), BF),
    ot=((D1, R), BF), sect=((D1, R), BF), firstt=((D1, R), BF), upt=((D, R), BF), o=((R, D), BF), dqt=((G, D, L), BF),
    act=((R, 4 * D), BF), bh=((R, 4 * D), BF), branch=((R, D), BF), do=((R, D), BF), bt=((R, 3 * D), BF),
)
ACC = dict(
    trail=(8, D), midnorm=(8, D), midshift=(8, D), scale=(8, D), shift=(8, D), hidden=(8, D), time=(L, D),
)
COLUMNS = dict(proj=(0, 3 * D), mix=(3 * D, D), exp=(4 * D, 4 * D), red=(8 * D, 4 * D))
WIDE = 12 * D
WEIGHTS = dict(
    hidden=((1, D), F32), stamped=((L, D), F32), gain1=((1, D), F32), shift1=((1, D), F32), qkv=((D, 3 * D), BF),
    bqkv=((1, 3 * D), F32), out=((D, D), BF), bout=((1, D), F32), gain2=((1, D), F32), shift2=((1, D), F32),
    wide=((D, 4 * D), BF), bwide=((1, 4 * D), F32), narrow=((4 * D, D), BF), bnarrow=((1, D), F32),
)


RAW = ("hidden", "stamped", "gain1", "shift1", "qkv", "bqkv", "out", "bout", "gain2", "shift2", "wide", "bwide", "narrow", "bnarrow")
MATRICES = ("qkv", "out", "wide", "narrow")


def spread(raw, w):
    for k in RAW:
        if k == "stamped":
            v = raw[k][...].astype(F32)
            w.stamped[...] = jnp.broadcast_to(v[:, None, :], (L // 2, 2, D)).reshape(L, D)
        elif k == "bqkv":
            v = raw[k][...].astype(F32)
            w.bqkv[:, :D] = v[:1]
            w.bqkv[:, D:2 * D] = jnp.zeros((1, D), F32)
            w.bqkv[:, 2 * D:] = v[1:]
        elif k not in MATRICES:
            v = raw[k][...].astype(F32)
            getattr(w, k)[...] = v.reshape(1, -1)


N = 128
PHASES = 4
EACH = 8
TRAJ = 4096
CW = 384
VECTORS = dict(lift=4, trail=1, midnorm=1, midshift=1, recenter=1, offsets=2, scale=1, shift=1, hidden=1)
SMALL = 80
HALF = SMALL // 2


def prep_kernel(unroll, slot, enc, out, src, dst):
    x = enc[...].astype(F32)
    src[0] = x[:, :L]
    src[1] = x[:, L:]

    def block(i, _):
        js = [slot[i * unroll + u] for u in range(unroll)]
        vs = [[src[k, pl.ds(i * unroll + u, 1), :] for k in range(2)] for u in range(unroll)]
        for u in range(unroll):
            for k in range(2):
                dst[k, pl.ds(js[u], 1), :] = vs[u][k]
        return 0

    lax.fori_loop(0, TRAJ // unroll, block, 0)
    for g in range(4):
        at = pl.ds(g * 1024, 1024)
        y = jnp.concatenate([dst[0, at, :], dst[1, at, :]], axis=1)
        out[g * 32:(g + 1) * 32] = y.astype(BF).reshape(32, PHASES, EACH, D)


def prep(slot, enc):
    vm, sm = (pl.BlockSpec(memory_space=m) for m in (pltpu.VMEM, pltpu.SMEM))
    return pl.pallas_call(
        functools.partial(prep_kernel, 32),
        out_shape=jax.ShapeDtypeStruct((N, PHASES, EACH, D), BF),
        in_specs=[sm, vm],
        out_specs=vm,
        scratch_shapes=[pltpu.VMEM((2, TRAJ, L), F32), pltpu.VMEM((2, TRAJ, L), F32)],
        compiler_params=pltpu.CompilerParams(vmem_limit_bytes=56 << 20),
    )(slot, enc)


def others(me):
    cs = [me % 2, 1 - me % 2]
    xs = [(me // 2 + d) % 4 * 2 for d in range(4)]
    ys = [(me // 8 + d) % 4 * 8 for d in range(4)]
    zs = [(me // 32 + d) % 4 * 32 for d in range(4)]
    hops = lambda k: sum((0, 1, 2, 1)[k // unit % 4] for unit in (2, 8, 32))
    far_first = sorted(range(1, N), key=hops, reverse=True)
    return [zs[k // 32] + ys[k // 8 % 4] + xs[k // 2 % 4] + cs[k % 2] for k in far_first]


def remote(src, dst, send, recv, to):
    return pltpu.make_async_remote_copy(src, dst, send, recv, device_id=(to,), device_id_type=MESH)


def landed_all(ref, sem):
    pltpu.make_async_copy(ref, ref, sem).wait()


MAIN_SCRATCH = dict(
    recv=((PHASES, N, EACH, D), BF), ret=((PHASES, N, EACH, D), BF), land=((N, PHASES, EACH, D), BF),
    mask=((32, L, L), F32), x32=((2, N * EACH, L), F32), ret32=((2, N * EACH, L), F32),
    land32=((2, TRAJ, L), F32), out32=((2, TRAJ, L), F32), perm=((TRAJ, L), jnp.int32), hot=((32, TRAJ), BF),
    counts=((32, L), F32), order=((32, L), F32), ga=((D1, WIDE), F32),
    sib_send=((3, 4, 16, 16, L), BF), sib_recv=((3, 4, 16, 16, L), BF), part0=((3, 4, 16, 16, L), BF),
    came0=((3, 4, 16, 16, L), BF), part1=((3, 16, 16, L), BF), came1=((3, 16, 16, L), BF),
    sum0=((3, 16, L), BF), sum2=((3, 16, 16, L), BF),
    dec_v=((32, L, D), BF), genc_v=((TRAJ, D), BF), up=((32, L, D), BF),
    small=((SMALL, D), F32), small_sib=((HALF, D), F32), hop_send=((3, HALF, D), F32), hop=((3, 4, HALF, D), F32),
)


def main_kernel(*refs):
    outgoing, perm_hbm, obs, slots, slot, up_hbm = refs[:6]
    raw = dict(zip(RAW, refs[6:6 + len(RAW)]))
    refs = refs[6 + len(RAW):]
    dec, genc, ag, small_out = refs[:4]
    refs = refs[4:]
    m = Bag(**dict(zip(MAIN_SCRATCH, refs)))
    refs = refs[len(MAIN_SCRATCH):]
    pair = []
    for _ in range(2):
        pair.append(Bag(**dict(zip(SCRATCH, refs))))
        refs = refs[len(SCRATCH):]
    w = Bag(**dict(zip(WEIGHTS, refs)))
    refs = refs[len(WEIGHTS):]
    acc = Bag(**dict(zip(ACC, refs)))
    in_send, in_recv, out_send, out_recv, one_send, one_recv, hop_sent, hop_came, plane_sem, local = refs[len(ACC):]
    for k, (at, width) in COLUMNS.items():
        setattr(acc, k, m.ga.at[pl.ds(0, D if k == "red" else D1), pl.ds(at, width)])
    me = lax.axis_index("dp")
    core = me % 2
    sibling = me + 1 - 2 * core

    barrier = pltpu.get_barrier_semaphore()
    for to in others(me):
        pl.semaphore_signal(barrier, inc=1, device_id=(to,), device_id_type=MESH)
    pl.semaphore_wait(barrier, N - 1)

    def send_in(g):
        pltpu.make_async_copy(outgoing.at[me, g], m.recv.at[g, me], in_recv.at[g]).start()
        for to in others(me):
            remote(outgoing.at[to, g], m.recv.at[g, me], in_send.at[g], in_recv.at[g], to).start()

    send_in(0)
    order_load = pltpu.make_async_copy(perm_hbm, m.perm, local.at[7])
    order_load.start()
    loads = [pltpu.make_async_copy(up_hbm, m.up, local.at[0])]
    loads += [pltpu.make_async_copy(raw[k], getattr(w, k), local.at[1 + i]) for i, k in enumerate(MATRICES)]
    for copy in loads:
        copy.start()
    spread(raw, w)
    for s in pair:
        for r in (s.ot, s.sect, s.firstt):
            r[D:, :] = jnp.ones((16, R), BF)

    mine = me * 32 + lax.broadcasted_iota(jnp.int32, (32, L), 0)
    counts = jnp.zeros((32, L), F32)
    for r in range(TRAJ // L):
        hot = (slots[r:r + 1, :] == mine).astype(F32)
        counts += hot * obs[r:r + 1, :].astype(F32)
        m.hot[:, r * L:(r + 1) * L] = hot.astype(BF)
    m.counts[...] = jnp.broadcast_to(jnp.sum(counts, axis=1, keepdims=True), (32, L))
    order_load.wait()
    m.order[...] = nn(m.hot[...], m.perm[...].astype(F32).astype(BF))

    def one_mask(j, _):
        place = lax.broadcasted_iota(jnp.int32, (L, L), 0).astype(F32)
        hot = (m.order[pl.ds(j, 1), :] == place).astype(F32).astype(BF)
        early = (place < m.counts[pl.ds(j, 1), :]).astype(F32).astype(BF)
        m.mask[j] = nn(hot, early)
        return 0

    lax.fori_loop(0, 32, one_mask, 0)
    for copy in loads:
        copy.wait()
    send_in(1)

    def io_of(g, half):
        base = g * EACH + half * G
        own = lambda t: pl.ds(half * G + t, L, stride=EACH)

        def out(t, v):
            m.dec_v[base + t] = v

        def ret(t, v):
            for i in range(2):
                m.ret32[i, own(t), :] = v[:, i * L:(i + 1) * L]

        return Bag(
            x=lambda t: jnp.concatenate([m.x32[i, own(t), :] for i in range(2)], axis=1),
            mask=lambda t: m.mask[base + t],
            up=lambda t: m.up[base + t],
            up_all=lambda: m.up[pl.ds(base, G)].reshape(R, D),
            out=out,
            ret=ret,
        )

    def forward(half, io):
        return lambda: chain(before(w, pair[half], acc, io), feed(w, pair[half], acc, io)), BEFORE + FEED

    def backward(half, io):
        return lambda: after(w, pair[half], acc, io), AFTER

    def send_out(g):
        m.ret[g] = jnp.concatenate([m.ret32[0], m.ret32[1]], axis=1).astype(BF).reshape(N, EACH, D)
        pltpu.make_async_copy(m.ret.at[g, me], m.land.at[me, g], out_recv.at[0]).start()
        for to in others(me):
            remote(m.ret.at[g, to], m.land.at[me, g], out_send.at[g], out_recv.at[0], to).start()
        mine = pl.ds(g * EACH, EACH)
        pltpu.make_async_copy(m.dec_v.at[mine], dec.at[mine], local.at[5]).start()

    def phase(g, _):
        landed_all(m.recv.at[g], in_recv.at[g])

        @pl.when(g < PHASES - 2)
        def _():
            send_in(g + 2)

        a = m.recv[g].reshape(N * EACH, D).astype(F32)
        m.x32[0] = a[:, :L]
        m.x32[1] = a[:, L:]
        earlier = g - (g + PHASES - 1) // PHASES
        weave(forward(0, io_of(g, 0)), backward(1, io_of(earlier, 1)))

        @pl.when(g == 0)
        def _():
            m.ga[...] = jnp.zeros_like(m.ga)
            for k in ACC:
                r = getattr(acc, k)
                r[...] = jnp.zeros_like(r)

        @pl.when(g > 0)
        def _():
            send_out(g - 1)

        weave(forward(1, io_of(g, 1)), backward(0, io_of(g, 0)))
        return 0

    lax.fori_loop(0, PHASES, phase, 0)
    for _ in after(w, pair[1], acc, io_of(PHASES - 1, 1)):
        pass

    units = (2, 8, 32)
    place = [(me // unit) % 4 for unit in units]

    def at_chip(j, r, x):
        coordinate = (x, r % 4, r // 4)
        a, b, c = (coordinate[(j + i) % 3] for i in range(3))
        return a, b * 4 + c

    def chunks(of_core):
        for r in range(16):
            for x in range(4):
                at = pl.multiple_of((2 * x + of_core) * CW, L)
                yield r, x, m.ga[r * 16:(r + 1) * 16, pl.ds(at, CW)]

    for r, x, v in chunks(1 - core):
        v = v.astype(BF)
        for j in range(3):
            m.sib_send[(j, *at_chip(j, r, x))] = v[:, j * L:(j + 1) * L]
    big_sib = remote(m.sib_send, m.sib_recv, one_send.at[0], one_recv.at[0], sibling)
    big_sib.start()
    send_out(PHASES - 1)
    t3 = acc.time[...].reshape(64, 2, D)
    m.small[:64] = t3[:, 0] + t3[:, 1]
    m.small[64:] = jnp.zeros((16, D), F32)
    at = 64
    for k, count in VECTORS.items():
        if k == "lift":
            v = acc.exp[D:D + 1, :]
        elif k == "recenter":
            v = acc.mix[D:D + 1, :]
        elif k == "offsets":
            v = jnp.concatenate([acc.proj[D:D + 1, :D], acc.proj[D:D + 1, 2 * D:]], axis=1)
        else:
            v = jnp.sum(getattr(acc, k)[...], axis=0, keepdims=True)
        for i in range(count):
            m.small[at:at + 1, :] = v[:, i * D:(i + 1) * D]
            at += 1
    mine = pl.ds(pl.multiple_of(core * HALF, 8), HALF)
    other = pl.ds(pl.multiple_of((1 - core) * HALF, 8), HALF)
    small_sib = remote(m.small.at[other], m.small_sib, one_send.at[1], one_recv.at[1], sibling)
    small_sib.start()

    def peers(axis):
        for d in (2, 1, 3):
            there = (place[axis] + d) % 4
            yield d - 1, there, me + (there - place[axis]) * units[axis]

    def small_hop(axis, value):
        m.hop_send[axis] = value
        m.hop[axis, place[axis]] = value
        copies = []
        for i, there, to in peers(axis):
            n = 2 + 3 * axis + i
            copies.append(remote(m.hop_send.at[axis], m.hop.at[axis, place[axis]], one_send.at[n], one_recv.at[n], to))
        return copies

    def small_sum(axis):
        return (m.hop[axis, 0] + m.hop[axis, 1]) + (m.hop[axis, 2] + m.hop[axis, 3])

    def hop(step, parts, arrive):
        copies = []
        axis_of = lambda j: j
        for i in range(3):
            for j in range(3):
                d, there, to = list(peers(axis_of(j)))[i]
                n = step * 9 + j * 3 + d
                copies.append(remote(parts(j, there), arrive(j, place[axis_of(j)]), hop_sent.at[n], hop_came.at[n], to))
        return copies

    def start(copies):
        for c in copies:
            c.start()
        return copies

    def finish(copies):
        for c in copies:
            c.wait()

    big_sib.wait()
    for r, x, v in chunks(core):
        for j in range(3):
            at = (j, *at_chip(j, r, x))
            m.part0[at] = (v[:, j * L:(j + 1) * L] + m.sib_recv[at].astype(F32)).astype(BF)
    copies = start(hop(0, lambda j, there: m.part0.at[j, there], lambda j, here: m.came0.at[j, here]))
    small_sib.wait()
    small_copies = start(small_hop(0, m.small[mine, :] + m.small_sib[...]))

    def total(part, came, j, here):
        own = part[j, here].astype(F32)
        v = [jnp.where(here == i, own, came[j, i].astype(F32)) for i in range(4)]
        return ((v[0] + v[1]) + (v[2] + v[3])).astype(BF)

    def plane(part, arrive, sent, came):
        copies = []
        for d2, d3 in sorted(((a, b) for a in range(4) for b in range(4) if a or b), key=lambda d: -(d[0] == 2) - (d[1] == 2)):
            for j in range(3):
                second, third = (j + 1) % 3, (j + 2) % 3
                p2, p3 = (place[second] + d2) % 4, (place[third] + d3) % 4
                to = me + (p2 - place[second]) * units[second] + (p3 - place[third]) * units[third]
                copies.append(remote(part(j, p2 * 4 + p3), arrive.at[j, in_plane(j)], sent, came, to))
        return start(copies)

    in_plane = lambda j: place[(j + 1) % 3] * 4 + place[(j + 2) % 3]
    finish(copies)
    for j in range(3):
        m.part1[j] = total(m.part0, m.came0, j, place[j])
        m.came1[j, in_plane(j)] = m.part1[j, in_plane(j)]
    plane(lambda j, there: m.part1.at[j, there], m.came1, plane_sem.at[0], plane_sem.at[1])
    finish(small_copies)
    small_copies = start(small_hop(1, small_sum(0)))
    landed_all(m.came1.at[:, pl.ds(0, 15)], plane_sem.at[1])
    for j in range(3):
        m.sum0[j] = jnp.sum(m.came1[j].astype(F32), axis=0).astype(BF)
        m.sum2[j, in_plane(j)] = m.sum0[j]
    plane(lambda j, there: m.sum0.at[j], m.sum2, plane_sem.at[2], plane_sem.at[3])
    finish(small_copies)
    small_copies = start(small_hop(2, small_sum(1)))

    landed_all(m.land, out_recv.at[0])
    for g in range(4):
        a = m.land[g * 32:(g + 1) * 32].reshape(1024, D).astype(F32)
        m.land32[0, g * 1024:(g + 1) * 1024] = a[:, :L]
        m.land32[1, g * 1024:(g + 1) * 1024] = a[:, L:]

    def gather(i, _):
        js = [slot[i * 32 + u] for u in range(32)]
        vs = [[m.land32[k, pl.ds(j, 1), :] for k in range(2)] for j in js]
        for u in range(32):
            for k in range(2):
                m.out32[k, pl.ds(i * 32 + u, 1), :] = vs[u][k]
        return 0

    def gather_some(part):
        steps = TRAJ // 32 // 3
        lax.fori_loop(part * steps, (part + 1) * steps if part < 2 else TRAJ // 32, gather, 0)

    gather_some(0)
    finish(small_copies)
    small_out[mine, :] = small_sum(2)
    small_last = remote(small_out.at[mine], small_out.at[mine], one_send.at[11], one_recv.at[11], sibling)
    small_last.start()
    landed_all(m.sum2.at[:, pl.ds(0, 15)], plane_sem.at[3])
    for j in range(3):
        ag[core, j, place[j]] = m.sum2[j]
    copies = start(hop(1, lambda j, there: m.sum2.at[j], lambda j, here: ag.at[core, j, here]))
    gather_some(1)
    finish(copies)
    big_last = remote(ag.at[core], ag.at[core], one_send.at[12], one_recv.at[12], sibling)
    big_last.start()
    gather_some(2)
    m.genc_v[...] = jnp.concatenate([m.out32[0], m.out32[1]], axis=1).astype(BF)
    genc_copy = pltpu.make_async_copy(m.genc_v, genc, local.at[6])
    genc_copy.start()
    small_last.wait()
    landed_all(m.dec_v, local.at[5])
    for g in range(PHASES):
        landed_all(m.recv.at[g, pl.ds(0, N - 1)], in_send.at[g])
        landed_all(m.ret.at[g, pl.ds(0, N - 1)], out_send.at[g])
    for i in (0, 2):
        landed_all(m.came1.at[:, pl.ds(0, 15)], plane_sem.at[i])
    big_last.wait()
    genc_copy.wait()


def main(outgoing, perm, obs, slot, up, raw):
    vm, sm, an = (pl.BlockSpec(memory_space=m) for m in (pltpu.VMEM, pltpu.SMEM, pl.ANY))
    scratch = [pltpu.VMEM(shape, kind) for shape, kind in MAIN_SCRATCH.values()]
    scratch += [pltpu.VMEM(shape, kind) for shape, kind in SCRATCH.values()] * 2
    scratch += [pltpu.VMEM(shape, kind) for shape, kind in WEIGHTS.values()]
    scratch += [pltpu.VMEM(shape, F32) for shape in ACC.values()]
    scratch += [pltpu.SemaphoreType.DMA((n,)) for n in (PHASES, PHASES, PHASES, 1, 13, 13, 18, 18, 4, 8)]
    return pl.pallas_call(
        main_kernel,
        out_shape=[
            jax.ShapeDtypeStruct((32, L, D), BF),
            jax.ShapeDtypeStruct((TRAJ, D), BF),
            jax.ShapeDtypeStruct((2, 3, 4, 16, 16, L), BF),
            jax.ShapeDtypeStruct((SMALL, D), F32),
        ],
        in_specs=[an, an, vm, vm, sm, an] + [an if k in MATRICES else vm for k in RAW],
        out_specs=[an, an, vm, vm],
        scratch_shapes=scratch,
        compiler_params=pltpu.CompilerParams(vmem_limit_bytes=62 << 20, has_side_effects=True, collective_id=0),
    )(outgoing, perm, obs.reshape(32, L), slot.reshape(32, L), slot, up, *raw)


LAST = dict(time=64, **VECTORS)


def last_kernel(dec, genc, ag, small, dec_out, genc_out, proj, mix, exp, red, *rest):
    outs, (ga, dec_v, genc_v, sem_in, sem_out) = rest[:len(LAST)], rest[len(LAST):]
    moves = [(dec.at[pl.ds(i * 8, 8)], dec_v.at[pl.ds(i * 8, 8)], dec_out.at[pl.ds(i * 8, 8)]) for i in range(4)]
    moves += [(genc.at[pl.ds(i * 1024, 1024)], genc_v.at[pl.ds(i * 1024, 1024)], genc_out.at[pl.ds(i * 1024, 1024)]) for i in range(4)]
    copies_in = [pltpu.make_async_copy(a, b, sem_in.at[i]) for i, (a, b, _) in enumerate(moves)]
    copies_out = [pltpu.make_async_copy(b, c, sem_out.at[i]) for i, (_, b, c) in enumerate(moves)]
    for copy in copies_in:
        copy.start()
    for a, b in zip(copies_in, copies_out):
        a.wait()
        b.start()
    for r in range(16):
        for c in range(8):
            coordinate = (c // 2, r % 4, r // 4)
            for j in range(3):
                at = c * CW + j * L
                p1, p2, p3 = (coordinate[(j + i) % 3] for i in range(3))
                ga[r * 16:(r + 1) * 16, at:at + L] = ag[c % 2, j, p1, p2 * 4 + p3].astype(F32)
    proj[...] = ga[:, :3 * D]
    mix[...] = ga[:, 3 * D:4 * D]
    exp[...] = ga[:, 4 * D:8 * D]
    red[...] = ga[:, 8 * D:].T
    at = 0
    for out, rows in zip(outs, LAST.values()):
        if len(out.shape) == 1:
            for i in range(rows):
                out[pl.ds(i * D, D)] = small[at + i:at + i + 1, :].reshape(D)
        else:
            out[...] = small[at:at + rows, :]
        at += rows
    for copy in copies_out:
        copy.wait()


def last(dec, genc, ag, small):
    vm, an = (pl.BlockSpec(memory_space=m) for m in (pltpu.VMEM, pl.ANY))
    shapes = [((32, L, D), BF), ((TRAJ, D), BF), ((D, 3 * D), F32), ((D, D), F32), ((D, 4 * D), F32), ((4 * D, D), F32)]
    shapes += [((rows, D) if k in ("time", "offsets") else (rows * D,), F32) for k, rows in LAST.items()]
    return pl.pallas_call(
        last_kernel,
        out_shape=[jax.ShapeDtypeStruct(*s) for s in shapes],
        in_specs=[an, an, vm, vm],
        out_specs=[an, an] + [vm] * (len(shapes) - 2),
        scratch_shapes=[
            pltpu.VMEM((D, WIDE), F32), pltpu.VMEM((32, L, D), BF), pltpu.VMEM((TRAJ, D), BF),
            pltpu.SemaphoreType.DMA((8,)), pltpu.SemaphoreType.DMA((8,)),
        ],
        compiler_params=pltpu.CompilerParams(vmem_limit_bytes=62 << 20),
    )(dec, genc, ag, small)


def on_device(encoder_states, position_permutation, observed_tokens, decoder_slot, *rest):
    raw, sensitivity = rest[:-1], rest[-1]
    outgoing = prep(decoder_slot, encoder_states.reshape(TRAJ, D))
    dec, genc, ag, small = main(outgoing, position_permutation, observed_tokens, decoder_slot, sensitivity, raw)
    dec, genc, proj, mix, exp, red, *vectors = last(dec, genc, ag, small)
    v = dict(zip(LAST, vectors))
    return (
        dec, genc.reshape(TRAJ, 1, D), v["hidden"], v["time"], v["scale"], v["shift"], proj, v["offsets"], mix,
        v["recenter"], v["midnorm"], v["midshift"], exp, v["lift"], red, v["trail"],
    )


def solution(mesh):
    in_specs = (P(None, "dp", None),) + (P(),) * 17 + (P("dp", None, None),)
    out_specs = (P("dp", None, None), P(None, "dp", None)) + (P(),) * 14
    return jax.shard_map(on_device, mesh=mesh, in_specs=in_specs, out_specs=out_specs, check_vma=False)
```

```python
import functools
import math

import jax
import jax.numpy as jnp
from jax import lax
from jax.experimental import pallas as pl
from jax.experimental.pallas import tpu as pltpu
from jax.sharding import PartitionSpec as P

MESH = pl.DeviceIdType.MESH

F32 = jnp.float32
BF = jnp.bfloat16
EPSILON = 1e-05
G = 4
L = 128
D = 256
H = 4
R = G * L
D1 = D + 16


def nn(a, b):
    return lax.dot_general(a, b, (((1,), (0,)), ((), ())), preferred_element_type=F32)


def nt(a, b):
    return lax.dot_general(a, b, (((1,), (1,)), ((), ())), preferred_element_type=F32)


def tn(a, b):
    return lax.dot_general(a, b, (((0,), (0,)), ((), ())), preferred_element_type=F32)


def fold(x):
    return jnp.sum(x.reshape(x.shape[0] // 8, 8, x.shape[1]), axis=0)


def norm(x):
    c = x - jnp.mean(x, axis=-1, keepdims=True)
    inv = lax.rsqrt(jnp.mean(c * c, axis=-1, keepdims=True) + EPSILON)
    return c * inv, inv


def norm_back(up, n, inv, gain):
    e = up * gain
    return inv * (e - jnp.mean(e, axis=-1, keepdims=True) - n * jnp.mean(e * n, axis=-1, keepdims=True))


SHIFT = 3.87
POLY = (146.76783278249778, -48.81607899847526, 12.01133916341042, -0.5829371368710288, 0.036552147836326994)
CP = 1.0 / math.sqrt(2.0 * math.pi)
HALF_LOG2E = -0.5 / math.log(2.0)


def gelu_parts(h):
    t = pl.reciprocal(jnp.abs(h) + SHIFT, approx=True)
    e = jnp.exp2(h * h * HALF_LOG2E)
    q = POLY[0]
    for c in POLY[1:]:
        q = q * t + c
    q = q * e
    phi = jnp.where(h >= 0.0, 1.0 - q, q)
    return h * phi, phi + (CP * h) * e


def head_masks():
    lane = lax.broadcasted_iota(jnp.int32, (1, D), 1) // 64
    return [(lane == h).astype(F32).astype(BF) for h in range(H)]


def rows(t, n=1):
    return slice(t * L, (t + n) * L)


def wide2(m):
    return jnp.concatenate([m, m], axis=1)


def before(w, s, acc, io):
    masks = head_masks()
    for t in range(G):
        x = jnp.where(wide2(io.mask(t)) > 0.5, io.x(t), w.hidden[...]) + w.stamped[...]
        s.mid[rows(t), :] = x
        n, inv = norm(x)
        s.inv1[rows(t), :] = jnp.broadcast_to(inv, (L, L))
        s.n1[rows(t), :] = n
        s.first[rows(t), :] = (n * w.gain1[...] + w.shift1[...]).astype(BF)
        yield
    s.firstt[:D, :] = s.first[...].T
    s.upt[...] = io.up_all().T
    for c, ref in enumerate((s.q, s.k, s.v)):
        y = nn(s.first[...], w.qkv[:, c * D:(c + 1) * D]) + w.bqkv[:, c * D:(c + 1) * D]
        y = y.astype(BF)
        if c == 0:
            y = y * BF(0.125)
        ref[...] = y
        yield
    for t in range(G):
        q = s.q[rows(t), :]
        for h in range(H):
            s.qm[t, h * L:(h + 1) * L, :] = q * masks[h]
        st = nt(s.k[rows(t), :], s.qm[t])
        e = jnp.exp(st - jnp.max(st, axis=0, keepdims=True))
        p = e * (1.0 / jnp.sum(e, axis=0, keepdims=True))
        s.p[t] = p
        s.pb[t] = p.astype(BF)
        yield
    for t in range(G):
        vt = s.v[rows(t), :].T
        for h in range(H):
            o = nn(vt[h * 64:(h + 1) * 64, :], s.pb[t, :, h * L:(h + 1) * L])
            s.ot[h * 64:(h + 1) * 64, rows(t)] = o.astype(BF)
        s.o[rows(t), :] = s.ot[:D, rows(t)].T
        yield
    for t in range(0, G, 2):
        proj = nn(s.o[rows(t, 2), :], w.out[...])
        for i in range(2):
            mid = s.mid[rows(t + i), :] + proj[rows(i), :] + w.bout[...]
            s.mid[rows(t + i), :] = mid
            n, inv = norm(mid)
            s.inv2[rows(t + i), :] = jnp.broadcast_to(inv, (L, L))
            s.n2[rows(t + i), :] = n
            s.second[rows(t + i), :] = (n * w.gain2[...] + w.shift2[...]).astype(BF)
        yield
    s.sect[:D, :] = s.second[...].T
    yield


def feed(w, s, acc, io):
    for c in range(4):
        cols = slice(c * D, (c + 1) * D)
        for t in range(G):
            h = nn(s.second[rows(t), :], w.wide[:, cols]) + w.bwide[:, cols]
            ba = nt(io.up(t), w.narrow[cols, :])
            a, da = gelu_parts(h)
            s.act[rows(t), cols] = a.astype(BF)
            s.bh[rows(t), cols] = (ba * da).astype(BF)
            yield


def after(w, s, acc, io):
    masks = head_masks()
    for t in range(0, G, 2):
        dec = nn(s.act[rows(t, 2), :], w.narrow[...])
        for i in range(2):
            io.out(t + i, (s.mid[rows(t + i), :] + dec[rows(i), :] + w.bnarrow[...]).astype(BF))
        yield
        bsec = nt(s.bh[rows(t, 2), :], w.wide[...])
        for i in range(2):
            up = io.up(t + i).astype(F32)
            n, b = s.n2[rows(t + i), :], bsec[rows(i), :]
            acc.trail[...] += fold(up)
            acc.midnorm[...] += fold(b * n)
            acc.midshift[...] += fold(b)
            bm = up + norm_back(b, n, wide2(s.inv2[rows(t + i), :]), w.gain2[...])
            s.mid[rows(t + i), :] = bm
            s.branch[rows(t + i), :] = bm.astype(BF)
            yield
        s.do[rows(t, 2), :] = nt(s.branch[rows(t, 2), :], w.out[...]).astype(BF)
        yield
    for c in range(4):
        cols = slice(c * D, (c + 1) * D)
        acc.exp[:, cols] += nn(s.sect[...], s.bh[:, cols])
        yield
        acc.red[:, cols] += nn(s.upt[...], s.act[:, cols])
        yield
    for t in range(G):
        do = s.do[rows(t), :]
        for h in range(H):
            s.dom[t, h * L:(h + 1) * L, :] = do * masks[h]
        dp = nt(s.v[rows(t), :], s.dom[t])
        p = s.p[t]
        pd = p * dp
        ds = pd - p * jnp.sum(pd, axis=0, keepdims=True)
        s.ds[t] = ds.astype(BF)
        yield
    for t in range(G):
        s.bt[rows(t), 2 * D:] = nn(s.pb[t], s.dom[t]).astype(BF)
        yield
        s.bt[rows(t), D:2 * D] = nn(s.ds[t], s.qm[t]).astype(BF)
        yield
        kt = s.k[rows(t), :].T
        for h in range(H):
            dq = nn(kt[h * 64:(h + 1) * 64, :], s.ds[t, :, h * L:(h + 1) * L]) * 0.125
            s.dqt[t, h * 64:(h + 1) * 64, :] = dq.astype(BF)
        s.bt[rows(t), :D] = s.dqt[t].T
        yield
    acc.mix[...] += nn(s.ot[...], s.branch[...])
    yield
    for t in range(0, G, 2):
        bfirst = nt(s.bt[rows(t, 2), :], w.qkv[...])
        for i in range(2):
            n, b = s.n1[rows(t + i), :], bfirst[rows(i), :]
            acc.scale[...] += fold(b * n)
            acc.shift[...] += fold(b)
            bi = s.mid[rows(t + i), :] + norm_back(b, n, wide2(s.inv1[rows(t + i), :]), w.gain1[...])
            acc.time[...] += bi
            ret = jnp.where(wide2(io.mask(t + i)) > 0.5, bi, 0.0)
            acc.hidden[...] += fold(bi - ret)
            io.ret(t + i, ret)
            yield
    for c in range(3):
        cols = slice(c * D, (c + 1) * D)
        acc.proj[:, cols] += nn(s.firstt[...], s.bt[:, cols])
        yield


def weave(first, second, other, early):
    first, second, other = list_pieces(first), list_pieces(second), list_pieces(other)
    for i in range(first.count):
        first.upto(i + 1)
        other.upto(-(-(i + 1) * early // first.count))
    for i in range(second.count):
        second.upto(i + 1)
        other.upto(early - (-(i + 1) * (other.count - early) // second.count))


class list_pieces:
    def __init__(self, make):
        self.steps, self.count, self.done = make[0](), make[1], 0

    def upto(self, n):
        while self.done < n:
            next(self.steps, None)
            self.done += 1
            if self.done == self.count:
                for _ in self.steps:
                    pass


BEFORE, FEED, AFTER, EARLY = 18, 16, 47, 8


class Bag:
    def __init__(self, **kw):
        self.__dict__.update(kw)


SCRATCH = dict(
    inv1=((R, L), F32), inv2=((R, L), F32), mid=((R, D), F32), n1=((R, D), F32), n2=((R, D), F32), first=((R, D), BF), second=((R, D), BF),
    q=((R, D), BF), k=((R, D), BF), v=((R, D), BF), qm=((G, H * L, D), BF), dom=((G, H * L, D), BF),
    p=((G, L, H * L), F32), pb=((G, L, H * L), BF), ds=((G, L, H * L), BF),
    ot=((D1, R), BF), sect=((D1, R), BF), firstt=((D1, R), BF), upt=((D, R), BF), o=((R, D), BF), dqt=((G, D, L), BF),
    act=((R, 4 * D), BF), bh=((R, 4 * D), BF), branch=((R, D), BF), do=((R, D), BF), bt=((R, 3 * D), BF),
)
ACC = dict(
    trail=(8, D), midnorm=(8, D), midshift=(8, D), scale=(8, D), shift=(8, D), hidden=(8, D), time=(L, D),
)
COLUMNS = dict(proj=(0, 3 * D), mix=(3 * D, D), exp=(4 * D, 4 * D), red=(8 * D, 4 * D))
WIDE = 12 * D
WEIGHTS = dict(
    hidden=((1, D), F32), stamped=((L, D), F32), gain1=((1, D), F32), shift1=((1, D), F32), qkv=((D, 3 * D), BF),
    bqkv=((1, 3 * D), F32), out=((D, D), BF), bout=((1, D), F32), gain2=((1, D), F32), shift2=((1, D), F32),
    wide=((D, 4 * D), BF), bwide=((1, 4 * D), F32), narrow=((4 * D, D), BF), bnarrow=((1, D), F32),
)


RAW = ("hidden", "stamped", "gain1", "shift1", "qkv", "bqkv", "out", "bout", "gain2", "shift2", "wide", "bwide", "narrow", "bnarrow")
MATRICES = ("qkv", "out", "wide", "narrow")


def spread(raw, w):
    for k in RAW:
        if k == "stamped":
            v = raw[k][...].astype(F32)
            w.stamped[...] = jnp.broadcast_to(v[:, None, :], (L // 2, 2, D)).reshape(L, D)
        elif k == "bqkv":
            v = raw[k][...].astype(F32)
            w.bqkv[:, :D] = v[:1]
            w.bqkv[:, D:2 * D] = jnp.zeros((1, D), F32)
            w.bqkv[:, 2 * D:] = v[1:]
        elif k not in MATRICES:
            v = raw[k][...].astype(F32)
            getattr(w, k)[...] = v.reshape(1, -1)


N = 128
PHASES = 4
EACH = 8
TRAJ = 4096
CW = 384
VECTORS = dict(lift=4, trail=1, midnorm=1, midshift=1, recenter=1, offsets=2, scale=1, shift=1, hidden=1)
SMALL = 80
HALF = SMALL // 2


def prep_kernel(unroll, slot, enc, out, src, dst):
    x = enc[...].astype(F32)
    src[0] = x[:, :L]
    src[1] = x[:, L:]

    def block(i, _):
        js = [slot[i * unroll + u] for u in range(unroll)]
        vs = [[src[k, pl.ds(i * unroll + u, 1), :] for k in range(2)] for u in range(unroll)]
        for u in range(unroll):
            for k in range(2):
                dst[k, pl.ds(js[u], 1), :] = vs[u][k]
        return 0

    lax.fori_loop(0, TRAJ // unroll, block, 0)
    for g in range(4):
        at = pl.ds(g * 1024, 1024)
        y = jnp.concatenate([dst[0, at, :], dst[1, at, :]], axis=1)
        out[g * 32:(g + 1) * 32] = y.astype(BF).reshape(32, PHASES, EACH, D)


def prep(slot, enc):
    vm, sm = (pl.BlockSpec(memory_space=m) for m in (pltpu.VMEM, pltpu.SMEM))
    return pl.pallas_call(
        functools.partial(prep_kernel, 32),
        out_shape=jax.ShapeDtypeStruct((N, PHASES, EACH, D), BF),
        in_specs=[sm, vm],
        out_specs=vm,
        scratch_shapes=[pltpu.VMEM((2, TRAJ, L), F32), pltpu.VMEM((2, TRAJ, L), F32)],
        compiler_params=pltpu.CompilerParams(vmem_limit_bytes=56 << 20),
    )(slot, enc)


def others(me):
    cs = [me % 2, 1 - me % 2]
    xs = [(me // 2 + d) % 4 * 2 for d in range(4)]
    ys = [(me // 8 + d) % 4 * 8 for d in range(4)]
    zs = [(me // 32 + d) % 4 * 32 for d in range(4)]
    hops = lambda k: sum((0, 1, 2, 1)[k // unit % 4] for unit in (2, 8, 32))
    far_first = sorted(range(1, N), key=hops, reverse=True)
    return [zs[k // 32] + ys[k // 8 % 4] + xs[k // 2 % 4] + cs[k % 2] for k in far_first]


def remote(src, dst, send, recv, to):
    return pltpu.make_async_remote_copy(src, dst, send, recv, device_id=(to,), device_id_type=MESH)


def landed_all(ref, sem):
    pltpu.make_async_copy(ref, ref, sem).wait()


MAIN_SCRATCH = dict(
    recv=((PHASES, N, EACH, D), BF), ret=((PHASES, N, EACH, D), BF), land=((N, PHASES, EACH, D), BF),
    mask=((32, L, L), F32), x32=((2, N * EACH, L), F32), ret32=((2, N * EACH, L), F32),
    land32=((2, TRAJ, L), F32), out32=((2, TRAJ, L), F32), perm=((TRAJ, L), jnp.int32), hot=((32, TRAJ), BF),
    counts=((32, L), F32), order=((32, L), F32), ga=((D1, WIDE), F32),
    sib_send=((3, 4, 16, 16, L), BF), sib_recv=((3, 4, 16, 16, L), BF), part0=((3, 4, 16, 16, L), BF),
    came0=((3, 4, 16, 16, L), BF), part1=((3, 16, 16, L), BF), came1=((3, 16, 16, L), BF),
    sum0=((3, 16, L), BF), sum2=((3, 16, 16, L), BF),
    dec_v=((32, L, D), BF), genc_v=((TRAJ, D), BF), up=((32, L, D), BF),
    small=((SMALL, D), F32), small_sib=((HALF, D), F32), hop_send=((3, HALF, D), F32), hop=((3, 4, HALF, D), F32),
)


def main_kernel(*refs):
    outgoing, perm_hbm, obs, slots, slot, up_hbm = refs[:6]
    raw = dict(zip(RAW, refs[6:6 + len(RAW)]))
    refs = refs[6 + len(RAW):]
    dec, genc, ag, small_out = refs[:4]
    refs = refs[4:]
    m = Bag(**dict(zip(MAIN_SCRATCH, refs)))
    refs = refs[len(MAIN_SCRATCH):]
    pair = []
    for _ in range(2):
        pair.append(Bag(**dict(zip(SCRATCH, refs))))
        refs = refs[len(SCRATCH):]
    w = Bag(**dict(zip(WEIGHTS, refs)))
    refs = refs[len(WEIGHTS):]
    acc = Bag(**dict(zip(ACC, refs)))
    in_send, in_recv, out_send, out_recv, one_send, one_recv, hop_sent, hop_came, plane_sem, local = refs[len(ACC):]
    for k, (at, width) in COLUMNS.items():
        setattr(acc, k, m.ga.at[pl.ds(0, D if k == "red" else D1), pl.ds(at, width)])
    me = lax.axis_index("dp")
    core = me % 2
    sibling = me + 1 - 2 * core

    barrier = pltpu.get_barrier_semaphore()
    for to in others(me):
        pl.semaphore_signal(barrier, inc=1, device_id=(to,), device_id_type=MESH)
    pl.semaphore_wait(barrier, N - 1)

    def send_in(g):
        pltpu.make_async_copy(outgoing.at[me, g], m.recv.at[g, me], in_recv.at[g]).start()
        for to in others(me):
            remote(outgoing.at[to, g], m.recv.at[g, me], in_send.at[g], in_recv.at[g], to).start()

    send_in(0)
    order_load = pltpu.make_async_copy(perm_hbm, m.perm, local.at[7])
    order_load.start()
    loads = [pltpu.make_async_copy(up_hbm, m.up, local.at[0])]
    loads += [pltpu.make_async_copy(raw[k], getattr(w, k), local.at[1 + i]) for i, k in enumerate(MATRICES)]
    for copy in loads:
        copy.start()
    spread(raw, w)
    for s in pair:
        for r in (s.ot, s.sect, s.firstt):
            r[D:, :] = jnp.ones((16, R), BF)

    mine = me * 32 + lax.broadcasted_iota(jnp.int32, (32, L), 0)
    counts = jnp.zeros((32, L), F32)
    for r in range(TRAJ // L):
        hot = (slots[r:r + 1, :] == mine).astype(F32)
        counts += hot * obs[r:r + 1, :].astype(F32)
        m.hot[:, r * L:(r + 1) * L] = hot.astype(BF)
    m.counts[...] = jnp.broadcast_to(jnp.sum(counts, axis=1, keepdims=True), (32, L))
    order_load.wait()
    m.order[...] = nn(m.hot[...], m.perm[...].astype(F32).astype(BF))

    def one_mask(j, _):
        place = lax.broadcasted_iota(jnp.int32, (L, L), 0).astype(F32)
        hot = (m.order[pl.ds(j, 1), :] == place).astype(F32).astype(BF)
        early = (place < m.counts[pl.ds(j, 1), :]).astype(F32).astype(BF)
        m.mask[j] = nn(hot, early)
        return 0

    lax.fori_loop(0, 32, one_mask, 0)
    for copy in loads:
        copy.wait()
    send_in(1)

    def io_of(g, half):
        base = g * EACH + half * G
        own = lambda t: pl.ds(half * G + t, L, stride=EACH)

        def out(t, v):
            m.dec_v[base + t] = v

        def ret(t, v):
            for i in range(2):
                m.ret32[i, own(t), :] = v[:, i * L:(i + 1) * L]

        return Bag(
            x=lambda t: jnp.concatenate([m.x32[i, own(t), :] for i in range(2)], axis=1),
            mask=lambda t: m.mask[base + t],
            up=lambda t: m.up[base + t],
            up_all=lambda: m.up[pl.ds(base, G)].reshape(R, D),
            out=out,
            ret=ret,
        )

    def forward(half, io):
        return (lambda: before(w, pair[half], acc, io), BEFORE), (lambda: feed(w, pair[half], acc, io), FEED)

    def backward(half, io):
        return lambda: after(w, pair[half], acc, io), AFTER

    def send_out(g):
        m.ret[g] = jnp.concatenate([m.ret32[0], m.ret32[1]], axis=1).astype(BF).reshape(N, EACH, D)
        pltpu.make_async_copy(m.ret.at[g, me], m.land.at[me, g], out_recv.at[0]).start()
        for to in others(me):
            remote(m.ret.at[g, to], m.land.at[me, g], out_send.at[g], out_recv.at[0], to).start()
        mine = pl.ds(g * EACH, EACH)
        pltpu.make_async_copy(m.dec_v.at[mine], dec.at[mine], local.at[5]).start()

    def phase(g, _):
        landed_all(m.recv.at[g], in_recv.at[g])

        @pl.when(g < PHASES - 2)
        def _():
            send_in(g + 2)

        a = m.recv[g].reshape(N * EACH, D).astype(F32)
        m.x32[0] = a[:, :L]
        m.x32[1] = a[:, L:]
        earlier = g - (g + PHASES - 1) // PHASES
        weave(*forward(0, io_of(g, 0)), backward(1, io_of(earlier, 1)), EARLY)

        @pl.when(g == 0)
        def _():
            m.ga[...] = jnp.zeros_like(m.ga)
            for k in ACC:
                r = getattr(acc, k)
                r[...] = jnp.zeros_like(r)

        @pl.when(g > 0)
        def _():
            send_out(g - 1)

        weave(*forward(1, io_of(g, 1)), backward(0, io_of(g, 0)), EARLY)
        return 0

    lax.fori_loop(0, PHASES, phase, 0)
    for _ in after(w, pair[1], acc, io_of(PHASES - 1, 1)):
        pass

    units = (2, 8, 32)
    place = [(me // unit) % 4 for unit in units]

    def at_chip(j, r, x):
        coordinate = (x, r % 4, r // 4)
        a, b, c = (coordinate[(j + i) % 3] for i in range(3))
        return a, b * 4 + c

    def chunks(of_core):
        for r in range(16):
            for x in range(4):
                at = pl.multiple_of((2 * x + of_core) * CW, L)
                yield r, x, m.ga[r * 16:(r + 1) * 16, pl.ds(at, CW)]

    for r, x, v in chunks(1 - core):
        v = v.astype(BF)
        for j in range(3):
            m.sib_send[(j, *at_chip(j, r, x))] = v[:, j * L:(j + 1) * L]
    big_sib = remote(m.sib_send, m.sib_recv, one_send.at[0], one_recv.at[0], sibling)
    big_sib.start()
    send_out(PHASES - 1)
    t3 = acc.time[...].reshape(64, 2, D)
    m.small[:64] = t3[:, 0] + t3[:, 1]
    m.small[64:] = jnp.zeros((16, D), F32)
    at = 64
    for k, count in VECTORS.items():
        if k == "lift":
            v = acc.exp[D:D + 1, :]
        elif k == "recenter":
            v = acc.mix[D:D + 1, :]
        elif k == "offsets":
            v = jnp.concatenate([acc.proj[D:D + 1, :D], acc.proj[D:D + 1, 2 * D:]], axis=1)
        else:
            v = jnp.sum(getattr(acc, k)[...], axis=0, keepdims=True)
        for i in range(count):
            m.small[at:at + 1, :] = v[:, i * D:(i + 1) * D]
            at += 1
    mine = pl.ds(pl.multiple_of(core * HALF, 8), HALF)
    other = pl.ds(pl.multiple_of((1 - core) * HALF, 8), HALF)
    small_sib = remote(m.small.at[other], m.small_sib, one_send.at[1], one_recv.at[1], sibling)
    small_sib.start()

    def peers(axis):
        for d in (2, 1, 3):
            there = (place[axis] + d) % 4
            yield d - 1, there, me + (there - place[axis]) * units[axis]

    def small_hop(axis, value):
        m.hop_send[axis] = value
        m.hop[axis, place[axis]] = value
        copies = []
        for i, there, to in peers(axis):
            n = 2 + 3 * axis + i
            copies.append(remote(m.hop_send.at[axis], m.hop.at[axis, place[axis]], one_send.at[n], one_recv.at[n], to))
        return copies

    def small_sum(axis):
        return (m.hop[axis, 0] + m.hop[axis, 1]) + (m.hop[axis, 2] + m.hop[axis, 3])

    def hop(step, parts, arrive):
        copies = []
        axis_of = lambda j: j
        for i in range(3):
            for j in range(3):
                d, there, to = list(peers(axis_of(j)))[i]
                n = step * 9 + j * 3 + d
                copies.append(remote(parts(j, there), arrive(j, place[axis_of(j)]), hop_sent.at[n], hop_came.at[n], to))
        return copies

    def start(copies):
        for c in copies:
            c.start()
        return copies

    def finish(copies):
        for c in copies:
            c.wait()

    big_sib.wait()
    for r, x, v in chunks(core):
        for j in range(3):
            at = (j, *at_chip(j, r, x))
            m.part0[at] = (v[:, j * L:(j + 1) * L] + m.sib_recv[at].astype(F32)).astype(BF)
    copies = start(hop(0, lambda j, there: m.part0.at[j, there], lambda j, here: m.came0.at[j, here]))
    small_sib.wait()
    small_copies = start(small_hop(0, m.small[mine, :] + m.small_sib[...]))

    def total(part, came, j, here):
        own = part[j, here].astype(F32)
        v = [jnp.where(here == i, own, came[j, i].astype(F32)) for i in range(4)]
        return ((v[0] + v[1]) + (v[2] + v[3])).astype(BF)

    def plane(part, arrive, sent, came):
        copies = []
        for d2, d3 in sorted(((a, b) for a in range(4) for b in range(4) if a or b), key=lambda d: -(d[0] == 2) - (d[1] == 2)):
            for j in range(3):
                second, third = (j + 1) % 3, (j + 2) % 3
                p2, p3 = (place[second] + d2) % 4, (place[third] + d3) % 4
                to = me + (p2 - place[second]) * units[second] + (p3 - place[third]) * units[third]
                copies.append(remote(part(j, p2 * 4 + p3), arrive.at[j, in_plane(j)], sent, came, to))
        return start(copies)

    in_plane = lambda j: place[(j + 1) % 3] * 4 + place[(j + 2) % 3]
    finish(copies)
    for j in range(3):
        m.part1[j] = total(m.part0, m.came0, j, place[j])
        m.came1[j, in_plane(j)] = m.part1[j, in_plane(j)]
    plane(lambda j, there: m.part1.at[j, there], m.came1, plane_sem.at[0], plane_sem.at[1])
    finish(small_copies)
    small_copies = start(small_hop(1, small_sum(0)))
    landed_all(m.came1.at[:, pl.ds(0, 15)], plane_sem.at[1])
    for j in range(3):
        m.sum0[j] = jnp.sum(m.came1[j].astype(F32), axis=0).astype(BF)
        m.sum2[j, in_plane(j)] = m.sum0[j]
    plane(lambda j, there: m.sum0.at[j], m.sum2, plane_sem.at[2], plane_sem.at[3])
    finish(small_copies)
    small_copies = start(small_hop(2, small_sum(1)))

    landed_all(m.land, out_recv.at[0])
    for g in range(4):
        a = m.land[g * 32:(g + 1) * 32].reshape(1024, D).astype(F32)
        m.land32[0, g * 1024:(g + 1) * 1024] = a[:, :L]
        m.land32[1, g * 1024:(g + 1) * 1024] = a[:, L:]

    def gather(i, _):
        js = [slot[i * 32 + u] for u in range(32)]
        vs = [[m.land32[k, pl.ds(j, 1), :] for k in range(2)] for j in js]
        for u in range(32):
            for k in range(2):
                m.out32[k, pl.ds(i * 32 + u, 1), :] = vs[u][k]
        return 0

    def gather_some(part):
        steps = TRAJ // 32 // 3
        lax.fori_loop(part * steps, (part + 1) * steps if part < 2 else TRAJ // 32, gather, 0)

    gather_some(0)
    finish(small_copies)
    small_out[mine, :] = small_sum(2)
    small_last = remote(small_out.at[mine], small_out.at[mine], one_send.at[11], one_recv.at[11], sibling)
    small_last.start()
    landed_all(m.sum2.at[:, pl.ds(0, 15)], plane_sem.at[3])
    for j in range(3):
        ag[core, j, place[j]] = m.sum2[j]
    copies = start(hop(1, lambda j, there: m.sum2.at[j], lambda j, here: ag.at[core, j, here]))
    gather_some(1)
    finish(copies)
    big_last = remote(ag.at[core], ag.at[core], one_send.at[12], one_recv.at[12], sibling)
    big_last.start()
    gather_some(2)
    m.genc_v[...] = jnp.concatenate([m.out32[0], m.out32[1]], axis=1).astype(BF)
    genc_copy = pltpu.make_async_copy(m.genc_v, genc, local.at[6])
    genc_copy.start()
    small_last.wait()
    landed_all(m.dec_v, local.at[5])
    for g in range(PHASES):
        landed_all(m.recv.at[g, pl.ds(0, N - 1)], in_send.at[g])
        landed_all(m.ret.at[g, pl.ds(0, N - 1)], out_send.at[g])
    for i in (0, 2):
        landed_all(m.came1.at[:, pl.ds(0, 15)], plane_sem.at[i])
    big_last.wait()
    genc_copy.wait()


def main(outgoing, perm, obs, slot, up, raw):
    vm, sm, an = (pl.BlockSpec(memory_space=m) for m in (pltpu.VMEM, pltpu.SMEM, pl.ANY))
    scratch = [pltpu.VMEM(shape, kind) for shape, kind in MAIN_SCRATCH.values()]
    scratch += [pltpu.VMEM(shape, kind) for shape, kind in SCRATCH.values()] * 2
    scratch += [pltpu.VMEM(shape, kind) for shape, kind in WEIGHTS.values()]
    scratch += [pltpu.VMEM(shape, F32) for shape in ACC.values()]
    scratch += [pltpu.SemaphoreType.DMA((n,)) for n in (PHASES, PHASES, PHASES, 1, 13, 13, 18, 18, 4, 8)]
    return pl.pallas_call(
        main_kernel,
        out_shape=[
            jax.ShapeDtypeStruct((32, L, D), BF),
            jax.ShapeDtypeStruct((TRAJ, D), BF),
            jax.ShapeDtypeStruct((2, 3, 4, 16, 16, L), BF),
            jax.ShapeDtypeStruct((SMALL, D), F32),
        ],
        in_specs=[an, an, vm, vm, sm, an] + [an if k in MATRICES else vm for k in RAW],
        out_specs=[an, an, vm, vm],
        scratch_shapes=scratch,
        compiler_params=pltpu.CompilerParams(vmem_limit_bytes=62 << 20, has_side_effects=True, collective_id=0),
    )(outgoing, perm, obs.reshape(32, L), slot.reshape(32, L), slot, up, *raw)


LAST = dict(time=64, **VECTORS)


def last_kernel(dec, genc, ag, small, dec_out, genc_out, proj, mix, exp, red, *rest):
    outs, (ga, dec_v, genc_v, sem_in, sem_out) = rest[:len(LAST)], rest[len(LAST):]
    moves = [(dec.at[pl.ds(i * 8, 8)], dec_v.at[pl.ds(i * 8, 8)], dec_out.at[pl.ds(i * 8, 8)]) for i in range(4)]
    moves += [(genc.at[pl.ds(i * 1024, 1024)], genc_v.at[pl.ds(i * 1024, 1024)], genc_out.at[pl.ds(i * 1024, 1024)]) for i in range(4)]
    copies_in = [pltpu.make_async_copy(a, b, sem_in.at[i]) for i, (a, b, _) in enumerate(moves)]
    copies_out = [pltpu.make_async_copy(b, c, sem_out.at[i]) for i, (_, b, c) in enumerate(moves)]
    for copy in copies_in:
        copy.start()
    for a, b in zip(copies_in, copies_out):
        a.wait()
        b.start()
    for r in range(16):
        for c in range(8):
            coordinate = (c // 2, r % 4, r // 4)
            for j in range(3):
                at = c * CW + j * L
                p1, p2, p3 = (coordinate[(j + i) % 3] for i in range(3))
                ga[r * 16:(r + 1) * 16, at:at + L] = ag[c % 2, j, p1, p2 * 4 + p3].astype(F32)
    proj[...] = ga[:, :3 * D]
    mix[...] = ga[:, 3 * D:4 * D]
    exp[...] = ga[:, 4 * D:8 * D]
    red[...] = ga[:, 8 * D:].T
    at = 0
    for out, rows in zip(outs, LAST.values()):
        if len(out.shape) == 1:
            for i in range(rows):
                out[pl.ds(i * D, D)] = small[at + i:at + i + 1, :].reshape(D)
        else:
            out[...] = small[at:at + rows, :]
        at += rows
    for copy in copies_out:
        copy.wait()


def last(dec, genc, ag, small):
    vm, an = (pl.BlockSpec(memory_space=m) for m in (pltpu.VMEM, pl.ANY))
    shapes = [((32, L, D), BF), ((TRAJ, D), BF), ((D, 3 * D), F32), ((D, D), F32), ((D, 4 * D), F32), ((4 * D, D), F32)]
    shapes += [((rows, D) if k in ("time", "offsets") else (rows * D,), F32) for k, rows in LAST.items()]
    return pl.pallas_call(
        last_kernel,
        out_shape=[jax.ShapeDtypeStruct(*s) for s in shapes],
        in_specs=[an, an, vm, vm],
        out_specs=[an, an] + [vm] * (len(shapes) - 2),
        scratch_shapes=[
            pltpu.VMEM((D, WIDE), F32), pltpu.VMEM((32, L, D), BF), pltpu.VMEM((TRAJ, D), BF),
            pltpu.SemaphoreType.DMA((8,)), pltpu.SemaphoreType.DMA((8,)),
        ],
        compiler_params=pltpu.CompilerParams(vmem_limit_bytes=62 << 20),
    )(dec, genc, ag, small)


def on_device(encoder_states, position_permutation, observed_tokens, decoder_slot, *rest):
    raw, sensitivity = rest[:-1], rest[-1]
    outgoing = prep(decoder_slot, encoder_states.reshape(TRAJ, D))
    dec, genc, ag, small = main(outgoing, position_permutation, observed_tokens, decoder_slot, sensitivity, raw)
    dec, genc, proj, mix, exp, red, *vectors = last(dec, genc, ag, small)
    v = dict(zip(LAST, vectors))
    return (
        dec, genc.reshape(TRAJ, 1, D), v["hidden"], v["time"], v["scale"], v["shift"], proj, v["offsets"], mix,
        v["recenter"], v["midnorm"], v["midshift"], exp, v["lift"], red, v["trail"],
    )


def solution(mesh):
    in_specs = (P(None, "dp", None),) + (P(),) * 17 + (P("dp", None, None),)
    out_specs = (P("dp", None, None), P(None, "dp", None)) + (P(),) * 14
    return jax.shard_map(on_device, mesh=mesh, in_specs=in_specs, out_specs=out_specs, check_vma=False)
```
